128 devices in a mesh: dp: 8 (over x, y_hi), shard: 16 (over y_lo, z, core).
Axes of the slice: x: 4, y: 4 (y_hi: 2, y_lo: 2; y = y_hi * 2 + y_lo), z: 4, core: 2. Of those that a mesh axis runs over, the one named last changes fastest.
Arguments:
- frames: bfloat16 [256, 256, 2048], P(('dp', 'shard')), may hold values from -6 to 6
- crop_starts: int32 [256], P(('dp', 'shard')), may hold values from 0 to 128
- pairing: int32 [256], replicated, may hold values from 0 to 255, each once
- bias_table: float32 [8, 255], replicated, may hold values from -6 to 320, as said below
- input_master: float32 [2048, 3072], P('shard'), may hold values from -0.125 to 0.125
- input_moment: float32 [2048, 3072], P('shard'), may hold values from -3 to 3
- input_square: float32 [2048, 3072], P('shard'), may hold values from 0.01 to 1
- output_master: float32 [1024, 2048], P('shard'), may hold values from -0.1875 to 0.1875
- output_moment: float32 [1024, 2048], P('shard'), may hold values from -3 to 3
- output_square: float32 [1024, 2048], P('shard'), may hold values from 0.01 to 1
- gain_master: float32 [2048], P('shard'), may hold values from 0.5 to 1.5
- gain_moment: float32 [2048], P('shard'), may hold values from -3 to 3
- gain_square: float32 [2048], P('shard'), may hold values from 0.01 to 1
Outputs:
- pair_losses: float32 [256], P(('dp', 'shard'))
- input_updated: float32 [2048, 3072], P('shard')
- input_moments: float32 [2048, 3072], P('shard')
- input_squares: float32 [2048, 3072], P('shard')
- output_updated: float32 [1024, 2048], P('shard')
- output_moments: float32 [1024, 2048], P('shard')
- output_squares: float32 [1024, 2048], P('shard')
- gain_updated: float32 [2048], P('shard')
- gain_moments: float32 [2048], P('shard')
- gain_squares: float32 [2048], P('shard')
The draws below stay inside these ranges and needn't reach their ends.
Inputs may be any that keep to these rules, and one draw needn't show every extreme that they name: `bias_table`: entry k of a head belongs to the offset k - (127) between the query's frame and the key's frame.
All inputs are finite; a program needn't handle non-finite values.
Results may differ from the reference program's by a relative error of at most 0.017.
Values may be sent and summed in bfloat16 or wider, within the bound.
A program may use at most 128 MiB of HBM per device.

```python
import math
import jax
import jax.numpy as jnp
from jax import lax

D = 2048
HEADS = 8
HEAD_DIM = 128
INNER = 1024
CROP = 128
SEG = 256
BDEV = 2
ITEMS = 256
N_DP = 8
N_SHARD = 16


def draw_bias_table(key, part):
    length = 2 * CROP - 1
    table = jnp.clip(jax.random.normal(key, (HEADS, length), jnp.float32), -6.0, 6.0)
    return table


def set_ends(values, own_key, low, top_value):
    spot = [jax.random.randint(jax.random.fold_in(own_key, axis), (), 0, length) for axis, length in enumerate(values.shape)]
    main_axis = values.shape.index(max(values.shape))
    beside = spot[:main_axis] + [(spot[main_axis] + 1) % values.shape[main_axis]] + spot[main_axis + 1:]
    return values.at[tuple(spot)].set(low).at[tuple(beside)].set(top_value)


def level_of(rng, dims, cuts, least, high):
    def one(axis_at, blocks):
        draws = jax.random.uniform(jax.random.fold_in(jax.random.fold_in(rng, 6), axis_at), (blocks,), jnp.float32, least / len(cuts), high / len(cuts))
        return jnp.repeat(jnp.exp(draws), dims[axis_at] // blocks).reshape((-1,) + (1,) * (len(dims) - axis_at - 1))

    factor_of = one(*cuts[0])
    for cut in cuts[1:]:
        factor_of = factor_of * one(*cut)
    return factor_of


def scatter_about(own_key, dims, width, most, cuts=(), kind=jnp.bfloat16):
    drawn = width * jax.random.normal(own_key, dims, jnp.float32)
    if cuts:
        drawn = drawn * level_of(own_key, dims, cuts, -0.22, 0.18)
    return jnp.clip(drawn, -most, most).astype(kind)


def setup_inputs(seed: int = 0) -> dict:
    key_list = jax.random.split(jax.random.key(seed), 14)
    return {
        "frames": scatter_about(key_list[0], (ITEMS, SEG, D), 1.0, 6.0, ((0, 128),)),
        "crop_starts": set_ends(jax.random.randint(key_list[1], (ITEMS,), 0, SEG - CROP + 1), jax.random.fold_in(key_list[1], 1), 0, SEG - CROP).astype(jnp.int32),
        "pairing": jax.random.permutation(key_list[2], ITEMS).astype(jnp.int32),
        "bias_table": draw_bias_table(jax.random.fold_in(key_list[13], 71), 0),
        "input_master": scatter_about(key_list[4], (D, 3 * INNER), D ** -0.5, 0.125, ((0, 16),), jnp.float32),
        "input_moment": scatter_about(key_list[5], (D, 3 * INNER), 0.2, 3.0, ((0, 16),), jnp.float32),
        "input_square": jnp.clip(jnp.exp(math.log(1.0) - 4.6051702 * jax.random.uniform(key_list[6], (D, 3 * INNER), jnp.float32) ** level_of(key_list[6], (D, 3 * INNER), ((0, 16),), -0.2, 0.2)), 0.01, 1.0),
        "output_master": scatter_about(key_list[7], (INNER, D), INNER ** -0.5, 0.1875, ((0, 16),), jnp.float32),
        "output_moment": scatter_about(key_list[8], (INNER, D), 0.2, 3.0, ((0, 16),), jnp.float32),
        "output_square": jnp.clip(jnp.exp(math.log(1.0) - 4.6051702 * jax.random.uniform(key_list[9], (INNER, D), jnp.float32) ** level_of(key_list[9], (INNER, D), ((0, 16),), -0.2, 0.2)), 0.01, 1.0),
        "gain_master": jnp.clip(1.0 + 0.1 * jax.random.normal(key_list[10], (D,), jnp.float32), 0.5, 1.5),
        "gain_moment": scatter_about(key_list[11], (D,), 0.2, 3.0, ((0, 16),), jnp.float32),
        "gain_square": jnp.clip(jnp.exp(math.log(1.0) - 4.6051702 * jax.random.uniform(key_list[12], (D,), jnp.float32) ** level_of(key_list[12], (D,), ((0, 16),), -0.2, 0.2)), 0.01, 1.0),
    }


inv_tau = 20.0
norm_eps = 1e-05
embed_eps = 1e-06
beta_one = 0.9
beta_two = 0.999
adam_eps = 1e-08
learn_rate = 0.002
weight_decay = 0.1
adam_step = 1000

def rounded(values):
    return lax.optimization_barrier(values.astype(jnp.bfloat16))

def band_bias(bias_table):
    span = (bias_table.shape[1] + 1) // 2
    flipped = bias_table[:, ::-1]
    tiled = jnp.tile(flipped, (1, span + 1))
    strip = tiled[:, span - 1:span - 1 + span * (2 * span - 2)]
    return strip.reshape(bias_table.shape[0], span, 2 * span - 2)[:, :, :span]

def crop_block(segments, starts):

    def one_crop(segment, begin):
        return lax.dynamic_slice_in_dim(segment, begin.astype(jnp.int32), CROP, 0)
    return jax.vmap(one_crop)(segments, starts)

def forward_block(crops, gain_w, input_w, output_w, band):
    count = crops.shape[0]
    frames_f = crops.astype(jnp.float32)
    centred = frames_f - lax.optimization_barrier(jnp.mean(frames_f, axis=-1, keepdims=True))
    normed = centred * lax.rsqrt(lax.optimization_barrier(jnp.mean(centred * centred, axis=-1, keepdims=True)) + norm_eps)
    hidden = rounded(normed * gain_w.astype(jnp.float32))
    packed = rounded(jnp.dot(hidden.reshape(count * CROP, D), input_w, preferred_element_type=jnp.float32))
    packed = packed.reshape(count, CROP, 3, HEADS, HEAD_DIM)
    queries = packed[:, :, 0].astype(jnp.float32)
    key_heads = packed[:, :, 1].astype(jnp.float32)
    value_heads = packed[:, :, 2].astype(jnp.float32)
    scores = jnp.einsum('bihd,bjhd->bhij', queries, key_heads) * HEAD_DIM ** (-0.5) + band[None]
    probabilities = jax.nn.softmax(scores, axis=-1)
    mixed_heads = rounded(jnp.einsum('bhij,bjhd->bihd', rounded(probabilities).astype(jnp.float32), value_heads))
    attention = jnp.dot(mixed_heads.reshape(count * CROP, INNER), output_w, preferred_element_type=jnp.float32)
    pooled = lax.optimization_barrier(jnp.mean(frames_f, axis=1)) + lax.optimization_barrier(jnp.mean(attention.reshape(count, CROP, D), axis=1))
    return (pooled, normed, hidden, queries, key_heads, value_heads, probabilities, mixed_heads)

def backward_block(saved, grad_frame, input_w, output_w):
    pooled, normed, hidden, queries, key_heads, value_heads, probabilities, mixed_heads = saved
    count = grad_frame.shape[0]
    mixed_sum = lax.optimization_barrier(jnp.sum(mixed_heads.astype(jnp.float32), axis=1)).reshape(count, INNER)
    grad_output = jnp.dot(mixed_sum.T, grad_frame.astype(jnp.float32), precision=lax.Precision.HIGHEST)
    grad_mixed = rounded(jnp.dot(grad_frame, output_w.T, preferred_element_type=jnp.float32))
    grad_mixed = grad_mixed.astype(jnp.float32).reshape(count, HEADS, HEAD_DIM)
    dprob = jnp.einsum('bjhd,bhd->bhj', value_heads, grad_mixed)
    centred = dprob[:, :, None, :] - lax.optimization_barrier(jnp.sum(probabilities * dprob[:, :, None, :], axis=-1, keepdims=True))
    dscores = rounded(probabilities * centred * HEAD_DIM ** (-0.5)).astype(jnp.float32)
    grad_queries = rounded(jnp.einsum('bhij,bjhd->bihd', dscores, key_heads))
    grad_keys = rounded(jnp.einsum('bhij,bihd->bjhd', dscores, queries))
    column_mass = lax.optimization_barrier(jnp.sum(probabilities, axis=2))
    grad_values = rounded(jnp.transpose(column_mass, (0, 2, 1))[:, :, :, None] * grad_mixed[:, None, :, :])
    grad_packed = jnp.stack([grad_queries, grad_keys, grad_values], axis=2).reshape(count * CROP, 3 * INNER)
    grad_input = jnp.dot(hidden.reshape(count * CROP, D).T, grad_packed, preferred_element_type=jnp.float32)
    grad_hidden = jnp.dot(grad_packed, input_w.T, preferred_element_type=jnp.float32)
    grad_gain = lax.optimization_barrier(jnp.sum(normed.reshape(count * CROP, D) * grad_hidden, axis=0))
    return (grad_input, grad_output, grad_gain)

def adam_update(master, moment, square, gradient, decay):
    moment_new = beta_one * moment + (1.0 - beta_one) * gradient
    square_new = beta_two * square + (1.0 - beta_two) * gradient * gradient
    mean_hat = moment_new / (1.0 - beta_one ** adam_step)
    square_hat = square_new / (1.0 - beta_two ** adam_step)
    master_new = master - learn_rate * (mean_hat / (jnp.sqrt(square_hat) + adam_eps) + decay * master)
    return (master_new, moment_new, square_new)

def reference(frames, crop_starts, pairing, bias_table, input_master, input_moment, input_square, output_master, output_moment, output_square, gain_master, gain_moment, gain_square):
    blocks = N_DP * N_SHARD
    band = band_bias(bias_table)
    gain_w = gain_master.astype(jnp.bfloat16)
    input_w = input_master.astype(jnp.bfloat16)
    output_w = output_master.astype(jnp.bfloat16)
    segments = frames.reshape(blocks, BDEV, SEG, D)
    starts = crop_starts.reshape(blocks, BDEV)

    def pool_block(packet):
        crops = crop_block(packet[0], packet[1])
        return forward_block(crops, gain_w, input_w, output_w, band)[0]
    pooled = lax.map(pool_block, (segments, starts)).reshape(ITEMS, D)
    norm_inv = lax.rsqrt(lax.optimization_barrier(jnp.sum(pooled * pooled, axis=1, keepdims=True)) + embed_eps)
    embedding = pooled * norm_inv
    item_order = jnp.arange(ITEMS, dtype=jnp.int32)
    position = jnp.zeros((ITEMS,), jnp.int32).at[pairing].set(item_order)
    partner = pairing[jnp.bitwise_xor(position, 1)]
    target = (partner[:, None] == item_order[None, :]).astype(jnp.float32)
    sims = jnp.dot(embedding, embedding.T, precision=lax.Precision.HIGHEST) * inv_tau
    exponents = jnp.where(item_order[:, None] == item_order[None, :], jnp.float32(0.0), jnp.exp(sims - inv_tau))
    totals = lax.optimization_barrier(jnp.sum(exponents, axis=1))
    pair_losses = jnp.log(totals) + inv_tau - lax.optimization_barrier(jnp.sum(sims * target, axis=1))
    weights = exponents / totals[:, None] + exponents / totals[None, :] - 2.0 * target
    grad_embedding = jnp.dot(weights, embedding, precision=lax.Precision.HIGHEST) * inv_tau
    grad_pooled = (grad_embedding - embedding * lax.optimization_barrier(jnp.sum(embedding * grad_embedding, axis=1, keepdims=True))) * norm_inv
    grad_frame = (grad_pooled / CROP).astype(jnp.bfloat16).reshape(blocks, BDEV, D)

    def back_step(carry, packet):
        crops = crop_block(packet[0], packet[1])
        saved = forward_block(crops, gain_w, input_w, output_w, band)
        sums = backward_block(saved, packet[2], input_w, output_w)
        return (tuple((total + rounded(term).astype(jnp.float32) for total, term in zip(carry, sums))), None)
    initial = (jnp.zeros((D, 3 * INNER), jnp.float32), jnp.zeros((INNER, D), jnp.float32), jnp.zeros((D,), jnp.float32))
    grads, unused = lax.scan(back_step, initial, (segments, starts, grad_frame))
    input_new = adam_update(input_master, input_moment, input_square, grads[0], weight_decay)
    output_new = adam_update(output_master, output_moment, output_square, grads[1], weight_decay)
    gain_new = adam_update(gain_master, gain_moment, gain_square, grads[2], 0.0)
    return (pair_losses, input_new[0], input_new[1], input_new[2], output_new[0], output_new[1], output_new[2], gain_new[0], gain_new[1], gain_new[2])
```

```python
import functools

import jax
import jax.numpy as jnp
from jax import lax
from jax.experimental import pallas as pl
from jax.experimental.pallas import tpu as pltpu
from jax.sharding import PartitionSpec as P

D = 2048
HEADS = 8
HEAD_DIM = 128
INNER = 1024
CROP = 128
QKV = 3 * HEAD_DIM
SLICE = D // 8

inv_tau = 20.0
norm_eps = 1e-05
embed_eps = 1e-06
beta_one = 0.9
beta_two = 0.999
adam_eps = 1e-08
learn_rate = 0.002
weight_decay = 0.1
adam_step = 1000
score_scale = HEAD_DIM ** (-0.5)

f32 = jnp.float32
bf16 = jnp.bfloat16
HIGHEST = lax.Precision.HIGHEST
NT = (((1,), (1,)), ((), ()))
TN = (((0,), (0,)), ((), ()))


def dot(a, b, dims=(((1,), (0,)), ((), ())), precision=None):
    return lax.dot_general(a, b, dims, precision=precision, preferred_element_type=f32)


def adam_update(master, moment, square, gradient, decay):
    moment_new = beta_one * moment + (1.0 - beta_one) * gradient
    square_new = beta_two * square + (1.0 - beta_two) * gradient * gradient
    mean_hat = moment_new / (1.0 - beta_one**adam_step)
    square_hat = square_new / (1.0 - beta_two**adam_step)
    master_new = master - learn_rate * (
        mean_hat / (jnp.sqrt(square_hat) + adam_eps) + decay * master
    )
    return (master_new, moment_new, square_new)


W, WO, MC, MM, M2, PO, GR, TO, GF, GM, RS = range(11)


def kernel(
    xn, mc, wp, wo2, bias, pair_a, pair_b,
    loss_out, s_out, o_out,
    xbuf, wbuf, wobuf, mcbuf, qkvbuf, probs, mmbuf, m2buf, pobuf, grbuf, tobuf, gfbuf,
    gmsend, gmbuf, gp, rsend, rbuf, s_fin, o_tmp, o_fin, band,
    ssem, rsem, xssem, xrsem, f_send, f_recv, f2_send, f2_recv,
):
    dp = lax.axis_index("dp")
    sh = lax.axis_index("shard")
    x, yh = dp // 2, dp % 2
    yl, z, c = sh // 8, (sh // 2) % 4, sh % 2
    base = yl * 8 + z * 2
    t = 2 * x + c
    p = yh * 8 + yl * 4 + z

    def tp_dev(m):
        return ((m // 2) * 2 + yh, base + m % 2)

    def plane_dev(q):
        return (x * 2 + q // 8, ((q // 4) % 2) * 8 + (q % 4) * 2 + c)

    def push(src, dst, send, recv, dev):
        pltpu.make_async_remote_copy(
            src_ref=src, dst_ref=dst, send_sem=send, recv_sem=recv,
            device_id=dev, device_id_type=pl.DeviceIdType.MESH,
        ).start()

    def await_bytes(ref, sem):
        pltpu.make_async_copy(ref, ref, sem).wait()

    barrier = pltpu.get_barrier_semaphore()

    def greet(k, _):
        for dev in (
            (dp, (sh + k) % 16),
            plane_dev((p + k) % 16),
        ):
            pl.semaphore_signal(barrier, inc=1, device_id=dev, device_id_type=pl.DeviceIdType.MESH)
        j = (dp * 2 + c + k) % 16
        pl.semaphore_signal(
            barrier, inc=1, device_id=(j // 2, base + j % 2), device_id_type=pl.DeviceIdType.MESH
        )
        return 0

    lax.fori_loop(1, 16, greet, 0)
    pl.semaphore_wait(barrier, 45)

    right = ((x + 1) % 4) * 2 + c
    left = ((x + 3) % 4) * 2 + c
    far = ((x + 2) % 4) * 2 + c
    sib = x * 2 + 1 - c
    other = 1 - 2 * c

    def send_item(src, slot, member):
        push(src, xbuf.at[slot], xssem, xrsem.at[slot], tp_dev(member))

    send_item(xn.at[0], 2 * t, right)
    send_item(xn.at[1], 2 * t + 1, left)
    send_item(xn.at[0], 2 * t, sib)
    send_item(xn.at[1], 2 * t + 1, sib)

    def send_w(k, _):
        s = (sh + k) % 16
        push(wp.at[s % 2], wbuf.at[sh], ssem.at[W], rsem.at[W], (dp, s))
        return 0

    lax.fori_loop(1, 16, send_w, 0)
    send_item(xn.at[1], 2 * t + 1, right)
    send_item(xn.at[0], 2 * t, left)

    def send_wo(k, _):
        s = (sh + k) % 16
        push(wo2.at[s % 2], wobuf.at[sh], ssem.at[WO], rsem.at[WO], (dp, s))
        return 0

    lax.fori_loop(1, 16, send_wo, 0)

    def send_mc(k, _):
        m = (t + k) % 8
        push(mc.at[m], mcbuf.at[t], ssem.at[MC], rsem.at[MC], tp_dev(m))
        return 0

    lax.fori_loop(1, 8, send_mc, 0)

    wbuf[sh] = wp[c]
    wobuf[sh] = wo2[c]
    mcbuf[t] = mc[t]
    xbuf[2 * t] = xn[0]
    xbuf[2 * t + 1] = xn[1]

    row = jnp.broadcast_to(bias[t], (CROP, 2 * CROP))
    shifted = pltpu.roll(row, CROP + 1, 1, stride=1, stride_axis=0)
    band[...] = shifted[:, :CROP].T

    def wait_item(slot):
        await_bytes(xbuf.at[slot], xrsem.at[slot])

    wait_item(2 * left)
    send_item(xbuf.at[2 * left], 2 * left, right)
    send_item(xbuf.at[2 * left], 2 * left, sib)
    wait_item(2 * right + 1)
    send_item(xbuf.at[2 * right + 1], 2 * right + 1, left)
    send_item(xbuf.at[2 * right + 1], 2 * right + 1, sib)
    wait_item(2 * sib)
    wait_item(2 * sib + 1)
    await_bytes(wbuf.at[pl.ds(0, 15)], rsem.at[W])

    def forward(m):
        rows = xbuf[pl.ds(2 * m, 2)].reshape(2 * CROP, D)
        packed = dot(rows, wbuf[...].reshape(D, QKV)).astype(bf16)
        qkvbuf[pl.ds(2 * m, 2)] = packed.reshape(2, CROP, QKV)
        for i in range(2):
            part = packed[i * CROP : (i + 1) * CROP]
            q, k, v = part[:, :128], part[:, 128:256], part[:, 256:]
            scores = dot(q, k, NT) * score_scale + band[...]
            raised = jnp.exp(scores - jnp.max(scores, axis=-1, keepdims=True))
            prob = raised / jnp.sum(raised, axis=-1, keepdims=True)
            probs[2 * m + i] = prob
            mixed = dot(prob.astype(bf16), v).astype(bf16).astype(f32)
            mmbuf[t, pl.ds(2 * m + i, 1), :] = jnp.sum(mixed, axis=0, keepdims=True)

    def fwd_own(k, _):
        forward(t + k * other)
        return 0

    lax.fori_loop(0, 2, fwd_own, 0)

    wait_item(2 * left + 1)
    send_item(xbuf.at[2 * left + 1], 2 * left + 1, sib)
    wait_item(2 * right)
    send_item(xbuf.at[2 * right], 2 * right, sib)

    def fwd_near(k, _):
        member = ((x + 3 + 2 * (k % 2)) % 4) * 2 + c + (k // 2) * other

        @pl.when(k >= 2)
        def _():
            wait_item(2 * member)
            wait_item(2 * member + 1)

        forward(member)
        return 0

    lax.fori_loop(0, 4, fwd_near, 0)

    wait_item(2 * far)
    send_item(xbuf.at[2 * far], 2 * far, sib)
    wait_item(2 * far + 1)
    send_item(xbuf.at[2 * far + 1], 2 * far + 1, sib)

    def fwd_far(k, _):
        member = far + k * other

        @pl.when(k >= 1)
        def _():
            wait_item(2 * member)
            wait_item(2 * member + 1)

        forward(member)
        return 0

    lax.fori_loop(0, 2, fwd_far, 0)

    def send_mm(k, _):
        push(mmbuf.at[t], mmbuf.at[t], ssem.at[MM], rsem.at[MM], tp_dev((t + k) % 8))
        return 0

    lax.fori_loop(1, 8, send_mm, 0)
    await_bytes(wobuf.at[pl.ds(0, 15)], rsem.at[WO])
    await_bytes(mcbuf.at[pl.ds(0, 7)], rsem.at[MC])
    await_bytes(mmbuf.at[pl.ds(0, 7)], rsem.at[MM])

    wo_slice = wobuf[...].reshape(INNER, SLICE)
    summed = jnp.concatenate([mmbuf[h] for h in range(8)], axis=1)
    high = summed.astype(bf16)
    low = (summed - high.astype(f32)).astype(bf16)
    product = dot(jnp.concatenate([high, low], axis=0), wo_slice)
    means = jnp.concatenate([mcbuf[m] for m in range(8)], axis=0)
    pooled = means + (product[:16] + product[16:]) * (1.0 / CROP)
    pobuf[p] = pooled

    def send_po(k, _):
        q = (p + k) % 16
        push(pobuf.at[p], pobuf.at[p], ssem.at[PO], rsem.at[PO], plane_dev(q))
        return 0

    lax.fori_loop(1, 16, send_po, 0)

    def send_m2(k, _):
        q = (p + k) % 16
        push(mmbuf.at[q % 8], m2buf.at[p], ssem.at[M2], rsem.at[M2], plane_dev(q))
        return 0

    lax.fori_loop(1, 16, send_m2, 0)
    m2buf[p] = mmbuf[p % 8]

    lane = lax.broadcasted_iota(jnp.int32, (256, 256), 1)
    r_t = (lane // 2) % 8
    r_p = lane // 16
    item = 2 * (
        ((r_t // 2) * 2 + r_p // 8) * 16 + ((r_p // 4) % 2) * 8 + (r_p % 4) * 2 + r_t % 2
    ) + lane % 2
    hot_a = (pair_a[...] == item).astype(bf16)
    hot_b = (pair_b[...] == item).astype(bf16)
    lane16 = lax.broadcasted_iota(jnp.int32, (16, 256), 1)
    sub16 = lax.broadcasted_iota(jnp.int32, (16, 256), 0)
    own = (lane16 == sub16 + p * 16).astype(f32)
    first = dot(own.astype(bf16), hot_a, NT).astype(bf16)
    target = dot(first, hot_b)

    await_bytes(pobuf.at[pl.ds(0, 15)], rsem.at[PO])
    everyone = pobuf[...].reshape(256, SLICE)
    grbuf[t, pl.ds(0, 16), :] = dot(pooled, everyone, NT, HIGHEST)
    grbuf[t, pl.ds(16, 8), :] = dot(jnp.ones((8, SLICE), f32), everyone * everyone, NT, HIGHEST)

    def send_gr(k, _):
        push(grbuf.at[t], grbuf.at[t], ssem.at[GR], rsem.at[GR], tp_dev((t + k) % 8))
        return 0

    lax.fori_loop(1, 8, send_gr, 0)
    await_bytes(grbuf.at[pl.ds(0, 7)], rsem.at[GR])
    gram = grbuf[0]
    for m in range(1, 8):
        gram = gram + grbuf[m]
    inv_row = lax.rsqrt(gram[16:17] + embed_eps)
    inv_col = jnp.sum(own * inv_row, axis=1, keepdims=True)
    sims = gram[:16] * inv_col * inv_row * inv_tau
    exponents = jnp.where(own > 0.5, 0.0, jnp.exp(sims - inv_tau))
    totals = jnp.sum(exponents, axis=1, keepdims=True)
    tobuf[p] = jnp.broadcast_to(totals, (16, 128))

    def send_to(k, _):
        q = (p + k) % 16
        push(tobuf.at[p], tobuf.at[p], ssem.at[TO], rsem.at[TO], plane_dev(q))
        return 0

    lax.fori_loop(1, 16, send_to, 0)
    losses = jnp.log(totals) + inv_tau - jnp.sum(sims * target, axis=1, keepdims=True)
    loss_out[...] = jnp.broadcast_to(losses, (16, 128))
    await_bytes(tobuf.at[pl.ds(0, 15)], rsem.at[TO])
    columns = tobuf[...].reshape(256, 128)
    columns = jnp.concatenate([columns, columns], axis=1)
    eye = lax.broadcasted_iota(jnp.int32, (256, 256), 0) == lane
    column_totals = jnp.sum(jnp.where(eye, columns, 0.0), axis=0, keepdims=True)
    weights = exponents / totals + exponents / column_totals - 2.0 * target
    grad_embedding = dot(weights * inv_row, everyone, precision=HIGHEST) * inv_tau
    along = jnp.sum(weights * sims, axis=1, keepdims=True)
    grad_pooled = (grad_embedding - pooled * inv_col * along) * inv_col
    grad_frame = (grad_pooled * (1.0 / CROP)).astype(bf16)
    partial = dot(grad_frame, wo_slice, NT)
    for h in range(8):
        gmsend[h] = partial[:, h * 128 : (h + 1) * 128]
    gfbuf[p] = grad_frame

    def send_gm(k, _):
        m = (t + k) % 8
        push(gmsend.at[m], gmbuf.at[t], ssem.at[GM], rsem.at[GM], tp_dev(m))
        return 0

    lax.fori_loop(1, 8, send_gm, 0)
    gmbuf[t] = gmsend[t]

    def send_gf(k, _):
        q = (p + k) % 16
        push(gfbuf.at[p], gfbuf.at[p], ssem.at[GF], rsem.at[GF], plane_dev(q))
        return 0

    lax.fori_loop(1, 16, send_gf, 0)
    await_bytes(gmbuf.at[pl.ds(0, 7)], rsem.at[GM])
    gm = gmbuf[0]
    for m in range(1, 8):
        gm = gm + gmbuf[m]
    grad_mixed = gm.astype(bf16)
    gmsum = grad_mixed.astype(f32)
    sub_item = lax.broadcasted_iota(jnp.int32, (16, 128), 0)

    def backward(b, _):
        part = qkvbuf[b]
        q, k, v = part[:, :128], part[:, 128:256], part[:, 256:]
        prob = probs[b]
        mask = sub_item == b
        g_row = jnp.sum(jnp.where(mask, dot(grad_mixed, v, NT), 0.0), axis=0, keepdims=True)
        gm_row = jnp.sum(jnp.where(mask, gmsum, 0.0), axis=0, keepdims=True)
        centred = g_row - jnp.sum(prob * g_row, axis=-1, keepdims=True)
        dscores = (prob * centred * score_scale).astype(bf16)
        grad_q = dot(dscores, k)
        grad_k = dot(dscores, q, TN)
        grad_v = dot(prob.astype(bf16), jnp.broadcast_to(gm_row, (CROP, 128)).astype(bf16), TN)
        gp[b] = jnp.concatenate([grad_q, grad_k, grad_v], axis=1).astype(bf16)
        return 0

    lax.fori_loop(0, 16, backward, 0)

    def block(q):
        s = ((q // 4) % 2) * 8 + (q % 4) * 2 + q // 8
        cols = xbuf[:, :, pl.ds(pl.multiple_of(s * 128, 128), 128)].reshape(16 * CROP, 128)
        return dot(cols, gp[...].reshape(16 * CROP, QKV), TN).astype(bf16)

    def scatter(k, _):
        q = (p + k) % 16
        value = block(q)
        for i in range(3):
            rsend[q, i] = value[:, i * 128 : (i + 1) * 128]
        push(rsend.at[q], rbuf.at[p], ssem.at[RS], rsem.at[RS], plane_dev(q))
        return 0

    lax.fori_loop(1, 16, scatter, 0)
    value = block(p)
    for i in range(3):
        rbuf[p, i] = value[:, i * 128 : (i + 1) * 128]

    await_bytes(m2buf.at[pl.ds(0, 15)], rsem.at[M2])
    await_bytes(gfbuf.at[pl.ds(0, 15)], rsem.at[GF])
    o_tmp[...] = dot(
        m2buf[...].reshape(256, 128).astype(bf16), gfbuf[...].reshape(256, SLICE), TN
    )
    o_fin[...] = o_tmp[pl.ds(pl.multiple_of(yh * 64, 64), 64), :].astype(bf16)

    s_cols = pl.ds(pl.multiple_of(t * 128, 128), 128)
    o_cols = pl.ds(pl.multiple_of(t * SLICE, SLICE), SLICE)

    def each_target(fn):
        def step(j, _):
            @pl.when(jnp.logical_or(j != dp, c != yh))
            def _():
                fn(j)
            return 0
        lax.fori_loop(0, 8, step, 0)

    def send_o(j):
        push(o_fin, o_out.at[:, o_cols], f2_send.at[j], f2_recv.at[t], (j, base + yh))

    each_target(send_o)

    await_bytes(rbuf.at[pl.ds(0, 15)], rsem.at[RS])
    for i in range(3):
        total = rbuf[0, i].astype(f32)
        for q in range(1, 16):
            total = total + rbuf[q, i].astype(f32)
        s_fin[i] = total.astype(bf16)

    def send_s(j):
        push(s_fin, s_out.at[:, :, s_cols], f_send.at[j], f_recv.at[t], (j, base + yh))

    each_target(send_s)

    @pl.when(c == yh)
    def _():
        s_out[:, :, s_cols] = s_fin[...]
        o_out[:, o_cols] = o_fin[...]

    def collect(m, _):
        @pl.when(jnp.logical_or(m != t, c != yh))
        def _():
            await_bytes(s_fin, f_recv.at[m])
            await_bytes(o_fin, f2_recv.at[m])
        return 0

    lax.fori_loop(0, 8, collect, 0)

    def sent(j):
        await_bytes(s_fin, f_send.at[j])
        await_bytes(o_fin, f2_send.at[j])

    each_target(sent)
    await_bytes(xbuf.at[pl.ds(0, 14)], xssem)
    for sem, ref in (
        (W, wbuf), (WO, wobuf), (M2, m2buf), (PO, pobuf), (TO, tobuf), (GF, gfbuf), (RS, rbuf),
    ):
        await_bytes(ref.at[pl.ds(0, 15)], ssem.at[sem])
    for sem, ref in ((MC, mcbuf), (MM, mmbuf), (GR, grbuf), (GM, gmbuf)):
        await_bytes(ref.at[pl.ds(0, 7)], ssem.at[sem])


def run_kernel(*args):
    vmem = pl.BlockSpec(memory_space=pltpu.VMEM)
    return pl.pallas_call(
        kernel,
        out_shape=(
            jax.ShapeDtypeStruct((16, 128), f32),
            jax.ShapeDtypeStruct((3, 128, INNER), bf16),
            jax.ShapeDtypeStruct((64, D), bf16),
        ),
        in_specs=[vmem] * len(args),
        out_specs=(vmem, vmem, vmem),
        scratch_shapes=[
            pltpu.VMEM((16, CROP, D), bf16),
            pltpu.VMEM((16, 128, QKV), bf16),
            pltpu.VMEM((16, 64, SLICE), bf16),
            pltpu.VMEM((8, 2, SLICE), f32),
            pltpu.VMEM((16, CROP, QKV), bf16),
            pltpu.VMEM((16, CROP, CROP), f32),
            pltpu.VMEM((8, 16, 128), f32),
            pltpu.VMEM((16, 16, 128), f32),
            pltpu.VMEM((16, 16, SLICE), f32),
            pltpu.VMEM((8, 24, 256), f32),
            pltpu.VMEM((16, 16, 128), f32),
            pltpu.VMEM((16, 16, SLICE), bf16),
            pltpu.VMEM((8, 16, 128), f32),
            pltpu.VMEM((8, 16, 128), f32),
            pltpu.VMEM((16, CROP, QKV), bf16),
            pltpu.VMEM((16, 3, 128, 128), bf16),
            pltpu.VMEM((16, 3, 128, 128), bf16),
            pltpu.VMEM((3, 128, 128), bf16),
            pltpu.VMEM((128, SLICE), f32),
            pltpu.VMEM((64, SLICE), bf16),
            pltpu.VMEM((CROP, CROP), f32),
            pltpu.SemaphoreType.DMA((11,)),
            pltpu.SemaphoreType.DMA((11,)),
            pltpu.SemaphoreType.DMA,
            pltpu.SemaphoreType.DMA((16,)),
            pltpu.SemaphoreType.DMA((8,)),
            pltpu.SemaphoreType.DMA((8,)),
            pltpu.SemaphoreType.DMA((8,)),
            pltpu.SemaphoreType.DMA((8,)),
        ],
        compiler_params=pltpu.CompilerParams(
            collective_id=0, has_side_effects=True, vmem_limit_bytes=56 * 1024 * 1024
        ),
        name="encoder",
    )(*args)


def per_device(
    frames, crop_starts, pairing, bias_table,
    input_master, input_moment, input_square,
    output_master, output_moment, output_square,
    gain_master, gain_moment, gain_square,
):
    x = lax.axis_index("dp") // 2
    t = 2 * x + lax.axis_index("shard") % 2
    gain_w = gain_master.astype(bf16).astype(f32)
    input_w = input_master.astype(bf16).astype(f32)
    crops = jnp.stack(
        [lax.dynamic_slice_in_dim(frames[i], crop_starts[i], CROP, 0) for i in range(2)]
    )
    frames_f = crops.astype(f32)
    centred = frames_f - jnp.mean(frames_f, axis=-1, keepdims=True)
    normed = centred * lax.rsqrt(jnp.mean(centred * centred, axis=-1, keepdims=True) + norm_eps)
    xn = normed.astype(bf16)
    mc = jnp.mean(frames_f, axis=1).reshape(2, 8, SLICE).transpose(1, 0, 2)
    pieces = lax.dynamic_slice_in_dim(
        input_master.reshape(128, 3, HEADS, HEAD_DIM), 2 * x, 2, 2
    ).astype(bf16).astype(f32)
    wp = (pieces * gain_w[:, None, None, None]).astype(bf16)
    wp = wp.transpose(2, 0, 1, 3).reshape(2, 128, QKV)
    wo2 = lax.dynamic_slice_in_dim(output_master.reshape(64, 8, SLICE), 2 * x, 2, 1)
    wo2 = wo2.astype(bf16).transpose(1, 0, 2)
    bias = jnp.pad(bias_table, ((0, 0), (0, 1))).reshape(HEADS, 1, 2 * CROP)
    pair_b = pairing.reshape(128, 2)[:, ::-1].reshape(256, 1)
    losses, s_grad, o_grad = run_kernel(
        xn, mc, wp, wo2, bias, pairing.reshape(256, 1), pair_b
    )
    pair_losses = lax.dynamic_slice(losses, (2 * t, 0), (2, 1)).reshape(2)
    share = s_grad.astype(f32).transpose(1, 0, 2).reshape(128, 3 * INNER)
    gain_total = jnp.sum(share * input_w, axis=1)
    input_new = adam_update(
        input_master, input_moment, input_square, share * gain_w[:, None], weight_decay
    )
    output_new = adam_update(
        output_master, output_moment, output_square, o_grad.astype(f32), weight_decay
    )
    gain_new = adam_update(gain_master, gain_moment, gain_square, gain_total, 0.0)
    return (pair_losses, *input_new, *output_new, *gain_new)


def solution(mesh):
    one = P("shard")
    two = P("shard", None)
    items = P(("dp", "shard"))
    in_specs = (P(("dp", "shard"), None, None), items, P(), P()) + (two,) * 6 + (one,) * 3
    out_specs = (items,) + (two,) * 6 + (one,) * 3
    return jax.shard_map(
        per_device, mesh=mesh, in_specs=in_specs, out_specs=out_specs, check_vma=False
    )
```

```python
import functools

import jax
import jax.numpy as jnp
from jax import lax
from jax.experimental import pallas as pl
from jax.experimental.pallas import tpu as pltpu
from jax.sharding import PartitionSpec as P

D = 2048
HEADS = 8
HEAD_DIM = 128
INNER = 1024
CROP = 128
QKV = 3 * HEAD_DIM
SLICE = D // 8

inv_tau = 20.0
norm_eps = 1e-05
embed_eps = 1e-06
beta_one = 0.9
beta_two = 0.999
adam_eps = 1e-08
learn_rate = 0.002
weight_decay = 0.1
adam_step = 1000
score_scale = HEAD_DIM ** (-0.5)

f32 = jnp.float32
bf16 = jnp.bfloat16
HIGHEST = lax.Precision.HIGHEST
NT = (((1,), (1,)), ((), ()))
TN = (((0,), (0,)), ((), ()))


def dot(a, b, dims=(((1,), (0,)), ((), ())), precision=None):
    return lax.dot_general(a, b, dims, precision=precision, preferred_element_type=f32)


def adam_update(master, moment, square, gradient, decay):
    moment_new = beta_one * moment + (1.0 - beta_one) * gradient
    square_new = beta_two * square + (1.0 - beta_two) * gradient * gradient
    mean_hat = moment_new / (1.0 - beta_one**adam_step)
    square_hat = square_new / (1.0 - beta_two**adam_step)
    master_new = master - learn_rate * (
        mean_hat / (jnp.sqrt(square_hat) + adam_eps) + decay * master
    )
    return (master_new, moment_new, square_new)


W, WO, MC, MM, EA, PO, GR, TO, LA, GM, RS = range(11)


def item_of(row):
    t, p = (row // 2) % 8, row // 16
    return 2 * (
        ((t // 2) * 2 + p // 8) * 16 + ((p // 4) % 2) * 8 + (p % 4) * 2 + t % 2
    ) + row % 2


def kernel(
    xn, mc, pairing, bias, input_master, output_master, gain,
    loss_out, s_out, o_out,
    wraw, woraw, wp, wo2, mcsend, target,
    xbuf, xt, wbuf, wobuf, mcbuf, qkvbuf, probs, arows, mmbuf, eabuf, easend, pobuf, grbuf,
    tobuf, labuf, gmsend, gmbuf, gp, rsend, rbuf, s_fin, o_tmp, o_fin, band, table,
    lsem, ssem, rsem, xssem, xrsem, q_send, q_recv, v_send, v_recv, o_send, o_recv,
):
    dp = lax.axis_index("dp")
    sh = lax.axis_index("shard")
    x, yh = dp // 2, dp % 2
    yl, z, c = sh // 8, (sh // 2) % 4, sh % 2
    base = yl * 8 + z * 2
    t = 2 * x + c
    p = yh * 8 + yl * 4 + z

    def tp_dev(m):
        return ((m // 2) * 2 + yh, base + m % 2)

    def plane_dev(q):
        return (x * 2 + q // 8, ((q // 4) % 2) * 8 + (q % 4) * 2 + c)

    def push(src, dst, send, recv, dev):
        pltpu.make_async_remote_copy(
            src_ref=src, dst_ref=dst, send_sem=send, recv_sem=recv,
            device_id=dev, device_id_type=pl.DeviceIdType.MESH,
        ).start()

    def await_bytes(ref, sem):
        pltpu.make_async_copy(ref, ref, sem).wait()

    loads = []
    for i in range(3):
        cols = pl.ds(pl.multiple_of(i * INNER + x * 256, 256), 256)
        loads.append(
            pltpu.make_async_copy(input_master.at[:, cols], wraw.at[i], lsem.at[i])
        )
    loads.append(
        pltpu.make_async_copy(
            output_master.at[:, pl.ds(pl.multiple_of(x * 512, 512), 512)], woraw, lsem.at[3]
        )
    )
    for load in loads:
        load.start()

    barrier = pltpu.get_barrier_semaphore()

    def greet(k, _):
        for dev in (
            (dp, (sh + k) % 16),
            plane_dev((p + k) % 16),
        ):
            pl.semaphore_signal(barrier, inc=1, device_id=dev, device_id_type=pl.DeviceIdType.MESH)
        j = (dp * 2 + c + k) % 16
        pl.semaphore_signal(
            barrier, inc=1, device_id=(j // 2, base + j % 2), device_id_type=pl.DeviceIdType.MESH
        )
        return 0

    lax.fori_loop(1, 16, greet, 0)

    right = ((x + 1) % 4) * 2 + c
    left = ((x + 3) % 4) * 2 + c
    far = ((x + 2) % 4) * 2 + c
    sib = x * 2 + 1 - c
    other = 1 - 2 * c

    def send_item(src, slot, member):
        push(src, xbuf.at[slot], xssem, xrsem.at[slot], tp_dev(member))

    pl.semaphore_wait(barrier, 45)
    send_item(xn.at[0], 2 * t, right)
    send_item(xn.at[1], 2 * t + 1, left)
    send_item(xn.at[0], 2 * t, sib)
    send_item(xn.at[1], 2 * t + 1, sib)
    send_item(xn.at[1], 2 * t + 1, right)
    send_item(xn.at[0], 2 * t, left)

    for load in loads:
        load.wait()
    square = lax.broadcasted_iota(jnp.int32, (128, 128), 0) == lax.broadcasted_iota(
        jnp.int32, (128, 128), 1
    )
    gain_row = gain[...].astype(bf16).astype(f32)
    gain_col = jnp.sum(jnp.where(square, gain_row, 0.0), axis=1, keepdims=True)
    for core in range(2):
        for i in range(3):
            piece = wraw[i, :, core * 128 : (core + 1) * 128].astype(bf16).astype(f32)
            wp[core, :, i * 128 : (i + 1) * 128] = (piece * gain_col).astype(bf16)
        wo2[core] = woraw[:, core * SLICE : (core + 1) * SLICE].astype(bf16)

    def send_w(k, _):
        s = (sh + k) % 16
        push(wp.at[s % 2], wbuf.at[sh], ssem.at[W], rsem.at[W], (dp, s))
        return 0

    lax.fori_loop(1, 16, send_w, 0)

    def send_wo(k, _):
        s = (sh + k) % 16
        push(wo2.at[s % 2], wobuf.at[sh], ssem.at[WO], rsem.at[WO], (dp, s))
        return 0

    lax.fori_loop(1, 16, send_wo, 0)

    for m in range(8):
        for i in range(2):
            mcsend[m, i : i + 1, :] = mc[i, m : m + 1, :]

    def send_mc(k, _):
        m = (t + k) % 8
        push(mcsend.at[m], mcbuf.at[t], ssem.at[MC], rsem.at[MC], tp_dev(m))
        return 0

    lax.fori_loop(1, 8, send_mc, 0)

    wbuf[sh] = wp[c]
    wobuf[sh] = wo2[c]
    mcbuf[t] = mcsend[t]
    xbuf[2 * t] = xn[0]
    xbuf[2 * t + 1] = xn[1]

    table[...] = jnp.zeros_like(table)
    table[:, : 2 * CROP - 1] = bias[...]
    row = jnp.broadcast_to(table[pl.ds(t, 1), :], (CROP, 2 * CROP))
    shifted = pltpu.roll(row, CROP + 1, 1, stride=1, stride_axis=0)
    band[...] = shifted[:, :CROP].T

    lane16 = lax.broadcasted_iota(jnp.int32, (16, 256), 1)
    sub16 = lax.broadcasted_iota(jnp.int32, (16, 256), 0)
    pair = jnp.broadcast_to(pairing[...], (16, 256))
    swapped = jnp.where(lane16 % 2 == 0, pltpu.roll(pair, 255, 1), pltpu.roll(pair, 1, 1))
    hot_a = (pair == item_of(sub16 + p * 16)).astype(f32).astype(bf16)
    rows256 = lax.broadcasted_iota(jnp.int32, (256, 256), 0)
    hot_b = (jnp.broadcast_to(swapped[:1], (256, 256)) == item_of(rows256)).astype(f32).astype(bf16)
    target[...] = dot(hot_a, hot_b, NT)

    def wait_item(slot):
        await_bytes(xbuf.at[slot], xrsem.at[slot])

    wait_item(2 * left)
    send_item(xbuf.at[2 * left], 2 * left, right)
    send_item(xbuf.at[2 * left], 2 * left, sib)
    wait_item(2 * right + 1)
    send_item(xbuf.at[2 * right + 1], 2 * right + 1, left)
    send_item(xbuf.at[2 * right + 1], 2 * right + 1, sib)
    wait_item(2 * sib)
    wait_item(2 * sib + 1)
    await_bytes(wbuf.at[pl.ds(0, 15)], rsem.at[W])

    half_mask = (
        lax.broadcasted_iota(jnp.int32, (16, 256), 0)
        == lax.broadcasted_iota(jnp.int32, (16, 256), 1) // 128
    )

    def forward(m):
        rows = xbuf[pl.ds(2 * m, 2)].reshape(2 * CROP, D)
        packed = dot(rows, wbuf[...].reshape(D, QKV)).astype(bf16)
        xt[:, pl.ds(pl.multiple_of(m * 256, 256), 256)] = rows.T
        qkvbuf[pl.ds(2 * m, 2)] = packed.reshape(2, CROP, QKV)
        mass = []
        for i in range(2):
            part = packed[i * CROP : (i + 1) * CROP]
            q, k, v = part[:, :128], part[:, 128:256], part[:, 256:]
            scores = dot(q, k, NT) * score_scale + band[...]
            raised = jnp.exp(scores - jnp.max(scores, axis=-1, keepdims=True))
            prob = raised / jnp.sum(raised, axis=-1, keepdims=True)
            probs[2 * m + i] = prob
            mixed = dot(prob.astype(bf16), v).astype(bf16).astype(f32)
            mmbuf[t, pl.ds(2 * m + i, 1), :] = jnp.sum(mixed, axis=0, keepdims=True)
            mass.append(jnp.sum(prob, axis=0, keepdims=True))
        both = jnp.where(half_mask, jnp.concatenate(mass, axis=1), 0.0).astype(bf16)
        weighed = dot(both, rows)
        for i in range(2):
            arows[pl.ds(2 * m + i, 1), :] = weighed[i : i + 1]

    def fwd_own(k, _):
        forward(t + k * other)
        return 0

    lax.fori_loop(0, 2, fwd_own, 0)

    wait_item(2 * left + 1)
    send_item(xbuf.at[2 * left + 1], 2 * left + 1, sib)
    wait_item(2 * right)
    send_item(xbuf.at[2 * right], 2 * right, sib)

    def fwd_near(k, _):
        member = ((x + 3 + 2 * (k % 2)) % 4) * 2 + c + (k // 2) * other

        @pl.when(k >= 2)
        def _():
            wait_item(2 * member)
            wait_item(2 * member + 1)

        forward(member)
        return 0

    lax.fori_loop(0, 4, fwd_near, 0)

    wait_item(2 * far)
    send_item(xbuf.at[2 * far], 2 * far, sib)
    wait_item(2 * far + 1)
    send_item(xbuf.at[2 * far + 1], 2 * far + 1, sib)

    def fwd_far(k, _):
        member = far + k * other

        @pl.when(k >= 1)
        def _():
            wait_item(2 * member)
            wait_item(2 * member + 1)

        forward(member)
        return 0

    lax.fori_loop(0, 2, fwd_far, 0)

    def send_mm(k, _):
        push(mmbuf.at[t], mmbuf.at[t], ssem.at[MM], rsem.at[MM], tp_dev((t + k) % 8))
        return 0

    lax.fori_loop(1, 8, send_mm, 0, unroll=True)
    await_bytes(wobuf.at[pl.ds(0, 15)], rsem.at[WO])
    await_bytes(mcbuf.at[pl.ds(0, 7)], rsem.at[MC])
    await_bytes(mmbuf.at[pl.ds(0, 7)], rsem.at[MM])

    wo_slice = wobuf[...].reshape(INNER, SLICE)
    summed = jnp.concatenate([mmbuf[h] for h in range(8)], axis=1)
    high = summed.astype(bf16)
    low = (summed - high.astype(f32)).astype(bf16)
    product = dot(jnp.concatenate([high, low], axis=0), wo_slice)
    means = jnp.concatenate([mcbuf[m] for m in range(8)], axis=0)
    pooled = means + (product[:16] + product[16:]) * (1.0 / CROP)
    pobuf[p] = pooled

    def send_po(k, _):
        q = (p + k) % 16
        push(pobuf.at[p], pobuf.at[p], ssem.at[PO], rsem.at[PO], plane_dev(q))
        return 0

    lax.fori_loop(1, 16, send_po, 0, unroll=True)

    own = (lane16 == sub16 + p * 16).astype(f32)
    await_bytes(pobuf.at[pl.ds(0, 15)], rsem.at[PO])
    everyone = pobuf[...].reshape(256, SLICE)
    grbuf[t, pl.ds(0, 16), :] = dot(pooled, everyone, NT, HIGHEST)
    grbuf[t, pl.ds(16, 8), :] = dot(jnp.ones((8, SLICE), f32), everyone * everyone, NT, HIGHEST)

    def send_gr(k, _):
        push(grbuf.at[t], grbuf.at[t], ssem.at[GR], rsem.at[GR], tp_dev((t + k) % 8))
        return 0

    lax.fori_loop(1, 8, send_gr, 0, unroll=True)

    for s in range(16):
        q = (s % 2) * 8 + s // 2
        easend[q, :, :128] = arows[:, s * 128 : (s + 1) * 128].astype(bf16)
        easend[q, :, 128:] = mmbuf[s // 2].astype(bf16)
    eabuf[p] = easend[p]
    await_bytes(grbuf.at[pl.ds(0, 7)], rsem.at[GR])
    gram = grbuf[0]
    for m in range(1, 8):
        gram = gram + grbuf[m]
    inv_row = lax.rsqrt(gram[16:17] + embed_eps)
    inv_col = jnp.sum(own * inv_row, axis=1, keepdims=True)
    sims = gram[:16] * inv_col * inv_row * inv_tau
    exponents = jnp.where(own > 0.5, 0.0, jnp.exp(sims - inv_tau))
    totals = jnp.sum(exponents, axis=1, keepdims=True)
    tobuf[p] = jnp.broadcast_to(totals, (16, 128))

    def send_to(k, _):
        q = (p + k) % 16
        push(tobuf.at[p], tobuf.at[p], ssem.at[TO], rsem.at[TO], plane_dev(q))
        return 0

    lax.fori_loop(1, 16, send_to, 0, unroll=True)
    losses = jnp.log(totals) + inv_tau - jnp.sum(sims * target[...], axis=1, keepdims=True)
    loss_out[...] = jnp.broadcast_to(losses, (16, 128))
    await_bytes(tobuf.at[pl.ds(0, 15)], rsem.at[TO])
    columns = tobuf[...].reshape(256, 128)
    columns = jnp.concatenate([columns, columns], axis=1)
    eye = lax.broadcasted_iota(jnp.int32, (256, 256), 0) == (
        lax.broadcasted_iota(jnp.int32, (256, 256), 1)
    )
    column_totals = jnp.sum(jnp.where(eye, columns, 0.0), axis=0, keepdims=True)
    weights = exponents / totals + exponents / column_totals - 2.0 * target[...]
    grad_embedding = dot(weights * inv_row, everyone, precision=HIGHEST) * inv_tau
    along = jnp.sum(weights * sims, axis=1, keepdims=True)
    grad_pooled = (grad_embedding - pooled * inv_col * along) * inv_col
    grad_frame = (grad_pooled * (1.0 / CROP)).astype(bf16)
    partial = dot(grad_frame, wo_slice, NT)
    for h in range(8):
        gmsend[h] = partial[:, h * 128 : (h + 1) * 128]
    labuf[p, :, :SLICE] = grad_frame

    def send_gm(k, _):
        m = (t + k) % 8
        push(gmsend.at[m], gmbuf.at[t], ssem.at[GM], rsem.at[GM], tp_dev(m))
        return 0

    lax.fori_loop(1, 8, send_gm, 0, unroll=True)
    gmbuf[t] = gmsend[t]

    def send_ea(k, _):
        q = (p + k) % 16
        push(easend.at[q], eabuf.at[p], ssem.at[EA], rsem.at[EA], plane_dev(q))
        return 0

    lax.fori_loop(1, 16, send_ea, 0)
    await_bytes(gmbuf.at[pl.ds(0, 7)], rsem.at[GM])
    gm = gmbuf[0]
    for m in range(1, 8):
        gm = gm + gmbuf[m]
    grad_mixed = gm.astype(bf16)
    labuf[p, :, SLICE:] = grad_mixed

    def send_la(k, _):
        q = (p + k) % 16
        push(labuf.at[p], labuf.at[p], ssem.at[LA], rsem.at[LA], plane_dev(q))
        return 0

    lax.fori_loop(1, 16, send_la, 0)
    sub_item = lax.broadcasted_iota(jnp.int32, (16, 128), 0)

    def backward(step, _):
        for i in range(4):
            b = step * 4 + i
            part = qkvbuf[b]
            q, k, v = part[:, :128], part[:, 128:256], part[:, 256:]
            prob = probs[b]
            all_rows = dot(grad_mixed, v, NT)
            g_row = jnp.sum(jnp.where(sub_item == b, all_rows, 0.0), axis=0, keepdims=True)
            centred = g_row - jnp.sum(prob * g_row, axis=-1, keepdims=True)
            dscores = (prob * centred * score_scale).astype(bf16)
            grad_q = dot(dscores, k)
            grad_k = dot(dscores, q, TN)
            gp[b] = jnp.concatenate([grad_q, grad_k], axis=1).astype(bf16)
        return 0

    lax.fori_loop(0, 4, backward, 0)

    def scatter(k, _):
        pair_at = (p + k) % 8
        rows = pl.ds(pl.multiple_of(pair_at * 256, 256), 256)
        value = dot(xt[rows, :], gp[...].reshape(16 * CROP, 256)).astype(bf16)
        for half in range(2):
            q = half * 8 + pair_at
            block = value[half * 128 : (half + 1) * 128]

            @pl.when(q != p)
            def _():
                for i in range(2):
                    rsend[q, i] = block[:, i * 128 : (i + 1) * 128]
                push(rsend.at[q], rbuf.at[p], ssem.at[RS], rsem.at[RS], plane_dev(q))

            @pl.when(q == p)
            def _():
                for i in range(2):
                    rbuf[p, i] = block[:, i * 128 : (i + 1) * 128]
        return 0

    lax.fori_loop(1, 9, scatter, 0)

    await_bytes(eabuf.at[pl.ds(0, 15)], rsem.at[EA])
    await_bytes(labuf.at[pl.ds(0, 15)], rsem.at[LA])
    early = eabuf[...].reshape(256, 256)
    late = labuf[...].reshape(256, SLICE + 128)
    o_tmp[...] = dot(early[:, 128:], late[:, :SLICE], TN)
    s_fin[2] = dot(early[:, :128], late[:, SLICE:], TN).astype(bf16)
    o_fin[...] = o_tmp[pl.ds(pl.multiple_of(yh * 64, 64), 64), :].astype(bf16)

    s_cols = pl.ds(pl.multiple_of(t * 128, 128), 128)
    o_cols = pl.ds(pl.multiple_of(t * SLICE, SLICE), SLICE)

    def each_target(fn):
        def step(j, _):
            @pl.when(jnp.logical_or(j != dp, c != yh))
            def _():
                fn(j)
            return 0
        lax.fori_loop(0, 8, step, 0)

    def send_early(j):
        dev = (j, base + yh)
        push(s_fin.at[2], s_out.at[2, :, s_cols], v_send.at[j], v_recv.at[t], dev)
        push(o_fin, o_out.at[:, o_cols], o_send.at[j], o_recv.at[t], dev)

    each_target(send_early)

    await_bytes(rbuf.at[pl.ds(0, 15)], rsem.at[RS])
    for i in range(2):
        total = rbuf[0, i].astype(f32)
        for q in range(1, 16):
            total = total + rbuf[q, i].astype(f32)
        s_fin[i] = total.astype(bf16)

    def send_s(j):
        push(
            s_fin.at[pl.ds(0, 2)], s_out.at[pl.ds(0, 2), :, s_cols],
            q_send.at[j], q_recv.at[t], (j, base + yh),
        )

    each_target(send_s)

    @pl.when(c == yh)
    def _():
        s_out[:, :, s_cols] = s_fin[...]
        o_out[:, o_cols] = o_fin[...]

    def collect(m, _):
        @pl.when(jnp.logical_or(m != t, c != yh))
        def _():
            await_bytes(s_fin.at[2], v_recv.at[m])
            await_bytes(o_fin, o_recv.at[m])
            await_bytes(s_fin.at[pl.ds(0, 2)], q_recv.at[m])
        return 0

    lax.fori_loop(0, 8, collect, 0)

    def sent(j):
        await_bytes(s_fin.at[2], v_send.at[j])
        await_bytes(o_fin, o_send.at[j])
        await_bytes(s_fin.at[pl.ds(0, 2)], q_send.at[j])

    each_target(sent)
    await_bytes(xbuf.at[pl.ds(0, 14)], xssem)
    for sem, ref in (
        (W, wbuf), (WO, wobuf), (EA, eabuf), (PO, pobuf), (TO, tobuf), (LA, labuf), (RS, rbuf),
    ):
        await_bytes(ref.at[pl.ds(0, 15)], ssem.at[sem])
    for sem, ref in ((MC, mcbuf), (MM, mmbuf), (GR, grbuf), (GM, gmbuf)):
        await_bytes(ref.at[pl.ds(0, 7)], ssem.at[sem])


def norm_kernel(starts, frames, xn, mc, wide):
    def widen(r, _):
        rows = pl.ds(pl.multiple_of(r * 32, 32), 32)
        wide[rows, :] = frames[0, rows, :].astype(f32)
        return 0

    lax.fori_loop(0, 8, widen, 0)
    wide[pl.ds(2 * CROP, 8), :] = jnp.zeros((8, D), f32)
    begin = starts[pl.program_id(0)]
    base, odd = (begin // 8) * 8, begin % 8

    def chunk(r, total):
        near = wide[pl.ds(pl.multiple_of(base + r * 16, 8), 24), :]
        rows = pltpu.roll(near, 24 - odd, 0)[:16]
        centred = rows - jnp.mean(rows, axis=-1, keepdims=True)
        scale = lax.rsqrt(jnp.mean(centred * centred, axis=-1, keepdims=True) + norm_eps)
        xn[0, pl.ds(pl.multiple_of(r * 16, 16), 16), :] = (centred * scale).astype(bf16)
        return total + rows[:8] + rows[8:]

    total = lax.fori_loop(0, CROP // 16, chunk, jnp.zeros((8, D), f32))
    mean = jnp.sum(total, axis=0, keepdims=True) * (1.0 / CROP)
    for m in range(8):
        mc[0, m : m + 1, :] = mean[:, m * SLICE : (m + 1) * SLICE]


def run_norm(frames, starts):
    return pl.pallas_call(
        norm_kernel,
        grid=(2,),
        out_shape=(
            jax.ShapeDtypeStruct((2, CROP, D), bf16),
            jax.ShapeDtypeStruct((2, 8, SLICE), f32),
        ),
        in_specs=[
            pl.BlockSpec(memory_space=pltpu.SMEM),
            pl.BlockSpec((1, 2 * CROP, D), lambda i: (i, 0, 0)),
        ],
        out_specs=(
            pl.BlockSpec((1, CROP, D), lambda i: (i, 0, 0)),
            pl.BlockSpec((1, 8, SLICE), lambda i: (i, 0, 0)),
        ),
        scratch_shapes=[pltpu.VMEM((2 * CROP + 8, D), f32)],
        compiler_params=pltpu.CompilerParams(vmem_limit_bytes=24 * 1024 * 1024),
        name="norm",
    )(starts, frames)


def run_kernel(*args):
    vmem = pl.BlockSpec(memory_space=pltpu.VMEM)
    hbm = pl.BlockSpec(memory_space=pl.ANY)
    return pl.pallas_call(
        kernel,
        out_shape=(
            jax.ShapeDtypeStruct((16, 128), f32),
            jax.ShapeDtypeStruct((3, 128, INNER), bf16),
            jax.ShapeDtypeStruct((64, D), bf16),
        ),
        in_specs=[vmem, vmem, vmem, vmem, hbm, hbm, vmem],
        out_specs=(vmem, vmem, vmem),
        scratch_shapes=[
            pltpu.VMEM((3, 128, 256), f32),
            pltpu.VMEM((64, 512), f32),
            pltpu.VMEM((2, 128, QKV), bf16),
            pltpu.VMEM((2, 64, SLICE), bf16),
            pltpu.VMEM((8, 2, SLICE), f32),
            pltpu.VMEM((16, 256), f32),
            pltpu.VMEM((16, CROP, D), bf16),
            pltpu.VMEM((D, 16 * CROP), bf16),
            pltpu.VMEM((16, 128, QKV), bf16),
            pltpu.VMEM((16, 64, SLICE), bf16),
            pltpu.VMEM((8, 2, SLICE), f32),
            pltpu.VMEM((16, CROP, QKV), bf16),
            pltpu.VMEM((16, CROP, CROP), f32),
            pltpu.VMEM((16, D), f32),
            pltpu.VMEM((8, 16, 128), f32),
            pltpu.VMEM((16, 16, 256), bf16),
            pltpu.VMEM((16, 16, 256), bf16),
            pltpu.VMEM((16, 16, SLICE), f32),
            pltpu.VMEM((8, 24, 256), f32),
            pltpu.VMEM((16, 16, 128), f32),
            pltpu.VMEM((16, 16, SLICE + 128), bf16),
            pltpu.VMEM((8, 16, 128), f32),
            pltpu.VMEM((8, 16, 128), f32),
            pltpu.VMEM((16, CROP, 256), bf16),
            pltpu.VMEM((16, 2, 128, 128), bf16),
            pltpu.VMEM((16, 2, 128, 128), bf16),
            pltpu.VMEM((3, 128, 128), bf16),
            pltpu.VMEM((128, SLICE), f32),
            pltpu.VMEM((64, SLICE), bf16),
            pltpu.VMEM((CROP, CROP), f32),
            pltpu.VMEM((HEADS, 2 * CROP), f32),
            pltpu.SemaphoreType.DMA((4,)),
            pltpu.SemaphoreType.DMA((11,)),
            pltpu.SemaphoreType.DMA((11,)),
            pltpu.SemaphoreType.DMA,
            pltpu.SemaphoreType.DMA((16,)),
        ]
        + [pltpu.SemaphoreType.DMA((8,))] * 6,
        compiler_params=pltpu.CompilerParams(
            collective_id=0, has_side_effects=True, vmem_limit_bytes=52 * 1024 * 1024
        ),
        name="encoder",
    )(*args)


STEPS = 4


def adam_kernel(
    share, o_grad, gain, gain_m, gain_s, in_w, in_m, in_s, out_w, out_m, out_s,
    new_in_w, new_in_m, new_in_s, new_out_w, new_out_m, new_out_s, new_gw, new_gm, new_gs,
    column,
):
    step = pl.program_id(0)
    rows = 128 // STEPS
    gain_row = gain[...].astype(bf16).astype(f32)
    lane = lax.broadcasted_iota(jnp.int32, (rows, 128), 1)
    sub = lax.broadcasted_iota(jnp.int32, (rows, 128), 0)
    gain_col = jnp.sum(jnp.where(lane == sub + step * rows, gain_row, 0.0), axis=1, keepdims=True)

    def part(j, total):
        i, cols = j // 4, pl.ds(pl.multiple_of(j * 256, 256), 256)
        inner = pl.ds(pl.multiple_of((j % 4) * 256, 256), 256)
        master = in_w[:, cols]
        piece = share[i, :, inner].astype(f32)
        new = adam_update(master, in_m[:, cols], in_s[:, cols], piece * gain_col, weight_decay)
        new_in_w[:, cols], new_in_m[:, cols], new_in_s[:, cols] = new
        terms = piece * master.astype(bf16).astype(f32)
        return total + terms[:, :128] + terms[:, 128:]

    total = lax.fori_loop(0, 12, part, jnp.zeros((rows, 128), f32))

    def out_part(j, _):
        cols = pl.ds(pl.multiple_of(j * 512, 512), 512)
        new = adam_update(
            out_w[:, cols], out_m[:, cols], out_s[:, cols], o_grad[:, cols].astype(f32), weight_decay
        )
        new_out_w[:, cols], new_out_m[:, cols], new_out_s[:, cols] = new
        return 0

    lax.fori_loop(0, 4, out_part, 0)
    column[pl.ds(pl.multiple_of(step * rows, rows), rows), :] = jnp.broadcast_to(
        jnp.sum(total, axis=1, keepdims=True), (rows, 128)
    )

    @pl.when(step == STEPS - 1)
    def _():
        square = lax.broadcasted_iota(jnp.int32, (128, 128), 0) == lax.broadcasted_iota(
            jnp.int32, (128, 128), 1
        )
        grad = jnp.sum(jnp.where(square, column[...], 0.0), axis=0, keepdims=True)
        new_gw[...], new_gm[...], new_gs[...] = adam_update(
            gain[...], gain_m[...], gain_s[...], grad, 0.0
        )


def run_adam(share, o_grad, gains, inputs, outputs):
    one = pl.BlockSpec((1, 128), lambda i: (0, 0))
    big = pl.BlockSpec((128 // STEPS, 3 * INNER), lambda i: (i, 0))
    mid = pl.BlockSpec((64 // STEPS, D), lambda i: (i, 0))
    shares = pl.BlockSpec((3, 128 // STEPS, INNER), lambda i: (0, i, 0))
    return pl.pallas_call(
        adam_kernel,
        grid=(STEPS,),
        out_shape=[jax.ShapeDtypeStruct((128, 3 * INNER), f32)] * 3
        + [jax.ShapeDtypeStruct((64, D), f32)] * 3
        + [jax.ShapeDtypeStruct((1, 128), f32)] * 3,
        in_specs=[shares, mid] + [one] * 3 + [big] * 3 + [mid] * 3,
        out_specs=[big] * 3 + [mid] * 3 + [one] * 3,
        scratch_shapes=[pltpu.VMEM((128, 128), f32)],
        compiler_params=pltpu.CompilerParams(vmem_limit_bytes=24 * 1024 * 1024),
        name="adam",
    )(share, o_grad, *gains, *inputs, *outputs)


def per_device(
    frames, crop_starts, pairing, bias_table,
    input_master, input_moment, input_square,
    output_master, output_moment, output_square,
    gain_master, gain_moment, gain_square,
):
    t = 2 * (lax.axis_index("dp") // 2) + lax.axis_index("shard") % 2
    gains = [g.reshape(1, 128) for g in (gain_master, gain_moment, gain_square)]
    losses, s_grad, o_grad = run_kernel(
        *run_norm(frames, crop_starts), pairing.reshape(1, 256), bias_table,
        input_master, output_master, gains[0],
    )
    pair_losses = lax.dynamic_slice(losses, (2 * t, 0), (2, 1)).reshape(2)
    new = run_adam(
        s_grad, o_grad, gains,
        (input_master, input_moment, input_square),
        (output_master, output_moment, output_square),
    )
    return (pair_losses, *new[:6], *(g.reshape(128) for g in new[6:]))


def solution(mesh):
    one = P("shard")
    two = P("shard", None)
    items = P(("dp", "shard"))
    in_specs = (P(("dp", "shard"), None, None), items, P(), P()) + (two,) * 6 + (one,) * 3
    out_specs = (items,) + (two,) * 6 + (one,) * 3
    return jax.shard_map(
        per_device, mesh=mesh, in_specs=in_specs, out_specs=out_specs, check_vma=False
    )
```

```python
import functools

import jax
import jax.numpy as jnp
from jax import lax
from jax.experimental import pallas as pl
from jax.experimental.pallas import tpu as pltpu
from jax.sharding import PartitionSpec as P

D = 2048
HEADS = 8
HEAD_DIM = 128
INNER = 1024
CROP = 128
QKV = 3 * HEAD_DIM
SLICE = D // 8

inv_tau = 20.0
norm_eps = 1e-05
embed_eps = 1e-06
beta_one = 0.9
beta_two = 0.999
adam_eps = 1e-08
learn_rate = 0.002
weight_decay = 0.1
adam_step = 1000
score_scale = HEAD_DIM ** (-0.5)

f32 = jnp.float32
bf16 = jnp.bfloat16
NT = (((1,), (1,)), ((), ()))
TN = (((0,), (0,)), ((), ()))


def dot(a, b, dims=(((1,), (0,)), ((), ()))):
    return lax.dot_general(a, b, dims, preferred_element_type=f32)


def split(a):
    high = a.astype(bf16)
    return high, (a - high.astype(f32)).astype(bf16)


def dot3(a, b, dims=(((1,), (0,)), ((), ()))):
    rows = a.shape[0]
    high, low = split(a)
    both = dot(jnp.concatenate([high, low], axis=0), b[0], dims)
    return both[:rows] + both[rows:] + dot(high, b[1], dims)


def adam_update(master, moment, square, gradient, decay):
    moment_new = beta_one * moment + (1.0 - beta_one) * gradient
    square_new = beta_two * square + (1.0 - beta_two) * gradient * gradient
    mean_hat = moment_new / (1.0 - beta_one**adam_step)
    square_hat = square_new / (1.0 - beta_two**adam_step)
    master_new = master - learn_rate * (
        mean_hat / (jnp.sqrt(square_hat) + adam_eps) + decay * master
    )
    return (master_new, moment_new, square_new)


W, WO, MC, MM, EA, PO, GR, TO, LA, GM, RZ, RY, BQ, BK = range(14)


def item_of(row):
    t, p = (row // 2) % 8, row // 16
    return 2 * (
        ((t // 2) * 2 + p // 8) * 16 + ((p // 4) % 2) * 8 + (p % 4) * 2 + t % 2
    ) + row % 2


def kernel(
    xn, mc, pairing, bias, input_master, output_master, gain,
    loss_out, s_out, o_out,
    wraw, woraw, wp, wo2, mcsend, target,
    xbuf, xt, wbuf, wobuf, mcbuf, qkvbuf, probs, arows, mmbuf, eabuf, easend, pobuf, grbuf,
    tobuf, labuf, gmsend, gmbuf, gp, zsend, ysend, zrecv, yrecv, mid, qrecv, krecv, s_fin, o_tmp, o_fin, band, table,
    lsem, ssem, rsem, xssem, xrsem, q_send, q_recv, k_send, k_recv, v_send, v_recv, o_send, o_recv,
):
    dp = lax.axis_index("dp")
    sh = lax.axis_index("shard")
    x, yh = dp // 2, dp % 2
    yl, z, c = sh // 8, (sh // 2) % 4, sh % 2
    base = yl * 8 + z * 2
    t = 2 * x + c
    p = yh * 8 + yl * 4 + z
    y = yh * 2 + yl

    def tp_dev(m):
        return ((m // 2) * 2 + yh, base + m % 2)

    def plane_dev(q):
        return (x * 2 + q // 8, ((q // 4) % 2) * 8 + (q % 4) * 2 + c)

    def at(y, z2):
        return (x * 2 + y // 2, (y % 2) * 8 + z2 * 2 + c)

    def push(src, dst, send, recv, dev):
        pltpu.make_async_remote_copy(
            src_ref=src, dst_ref=dst, send_sem=send, recv_sem=recv,
            device_id=dev, device_id_type=pl.DeviceIdType.MESH,
        ).start()

    def await_bytes(ref, sem):
        pltpu.make_async_copy(ref, ref, sem).wait()

    loads = []
    for i in range(3):
        cols = pl.ds(pl.multiple_of(i * INNER + x * 256, 256), 256)
        loads.append(
            pltpu.make_async_copy(input_master.at[:, cols], wraw.at[i], lsem.at[i])
        )
    loads.append(
        pltpu.make_async_copy(
            output_master.at[:, pl.ds(pl.multiple_of(x * 512, 512), 512)], woraw, lsem.at[3]
        )
    )
    for load in loads:
        load.start()

    barrier = pltpu.get_barrier_semaphore()

    def greet(k, _):
        for dev in (
            (dp, (sh + k) % 16),
            plane_dev((p + k) % 16),
        ):
            pl.semaphore_signal(barrier, inc=1, device_id=dev, device_id_type=pl.DeviceIdType.MESH)
        j = (dp * 2 + c + k) % 16
        pl.semaphore_signal(
            barrier, inc=1, device_id=(j // 2, base + j % 2), device_id_type=pl.DeviceIdType.MESH
        )
        return 0

    lax.fori_loop(1, 16, greet, 0)

    right = ((x + 1) % 4) * 2 + c
    left = ((x + 3) % 4) * 2 + c
    far = ((x + 2) % 4) * 2 + c
    sib = x * 2 + 1 - c
    other = 1 - 2 * c

    def send_item(src, slot, member):
        push(src, xbuf.at[slot], xssem, xrsem.at[slot], tp_dev(member))

    pl.semaphore_wait(barrier, 45)
    send_item(xn.at[0], 2 * t, right)
    send_item(xn.at[1], 2 * t + 1, left)
    send_item(xn.at[0], 2 * t, sib)
    send_item(xn.at[1], 2 * t + 1, sib)
    send_item(xn.at[1], 2 * t + 1, right)
    send_item(xn.at[0], 2 * t, left)

    for load in loads:
        load.wait()
    square = lax.broadcasted_iota(jnp.int32, (128, 128), 0) == lax.broadcasted_iota(
        jnp.int32, (128, 128), 1
    )
    gain_row = gain[...].astype(bf16).astype(f32)
    gain_col = jnp.sum(jnp.where(square, gain_row, 0.0), axis=1, keepdims=True)
    for core in range(2):
        for i in range(3):
            piece = wraw[i, :, core * 128 : (core + 1) * 128].astype(bf16).astype(f32)
            wp[core, :, i * 128 : (i + 1) * 128] = (piece * gain_col).astype(bf16)
        wo2[core] = woraw[:, core * SLICE : (core + 1) * SLICE].astype(bf16)

    def send_w(k, _):
        s = (sh + k) % 16
        push(wp.at[s % 2], wbuf.at[sh], ssem.at[W], rsem.at[W], (dp, s))
        return 0

    lax.fori_loop(1, 16, send_w, 0)

    def send_wo(k, _):
        s = (sh + k) % 16
        push(wo2.at[s % 2], wobuf.at[sh], ssem.at[WO], rsem.at[WO], (dp, s))
        return 0

    lax.fori_loop(1, 16, send_wo, 0)

    for m in range(8):
        for i in range(2):
            mcsend[m, i : i + 1, :] = mc[i, m : m + 1, :]

    def send_mc(k, _):
        m = (t + k) % 8
        push(mcsend.at[m], mcbuf.at[t], ssem.at[MC], rsem.at[MC], tp_dev(m))
        return 0

    lax.fori_loop(1, 8, send_mc, 0)

    wbuf[sh] = wp[c]
    wobuf[sh] = wo2[c]
    mcbuf[t] = mcsend[t]
    xbuf[2 * t] = xn[0]
    xbuf[2 * t + 1] = xn[1]

    table[...] = jnp.zeros_like(table)
    table[:, : 2 * CROP - 1] = bias[...]
    row = jnp.broadcast_to(table[pl.ds(t, 1), :], (CROP, 2 * CROP))
    shifted = pltpu.roll(row, CROP + 1, 1, stride=1, stride_axis=0)
    band[...] = shifted[:, :CROP].T

    lane16 = lax.broadcasted_iota(jnp.int32, (16, 256), 1)
    sub16 = lax.broadcasted_iota(jnp.int32, (16, 256), 0)
    pair = jnp.broadcast_to(pairing[...], (16, 256))
    swapped = jnp.where(lane16 % 2 == 0, pltpu.roll(pair, 255, 1), pltpu.roll(pair, 1, 1))
    hot_a = (pair == item_of(sub16 + p * 16)).astype(f32).astype(bf16)
    rows256 = lax.broadcasted_iota(jnp.int32, (256, 256), 0)
    hot_b = (jnp.broadcast_to(swapped[:1], (256, 256)) == item_of(rows256)).astype(f32).astype(bf16)
    target[...] = dot(hot_a, hot_b, NT)

    def wait_item(slot):
        await_bytes(xbuf.at[slot], xrsem.at[slot])

    wait_item(2 * left)
    send_item(xbuf.at[2 * left], 2 * left, right)
    send_item(xbuf.at[2 * left], 2 * left, sib)
    wait_item(2 * right + 1)
    send_item(xbuf.at[2 * right + 1], 2 * right + 1, left)
    send_item(xbuf.at[2 * right + 1], 2 * right + 1, sib)
    wait_item(2 * sib)
    wait_item(2 * sib + 1)
    await_bytes(wbuf.at[pl.ds(0, 15)], rsem.at[W])

    half_mask = (
        lax.broadcasted_iota(jnp.int32, (16, 256), 0)
        == lax.broadcasted_iota(jnp.int32, (16, 256), 1) // 128
    )

    def forward(m):
        rows = xbuf[pl.ds(2 * m, 2)].reshape(2 * CROP, D)
        packed = dot(rows, wbuf[...].reshape(D, QKV)).astype(bf16)
        xt[:, pl.ds(pl.multiple_of(m * 256, 256), 256)] = rows.T
        qkvbuf[pl.ds(2 * m, 2)] = packed.reshape(2, CROP, QKV)
        mass = []
        for i in range(2):
            part = packed[i * CROP : (i + 1) * CROP]
            q, k, v = part[:, :128], part[:, 128:256], part[:, 256:]
            scores = dot(q, k, NT) * score_scale + band[...]
            raised = jnp.exp(scores - jnp.max(scores, axis=-1, keepdims=True))
            prob = raised / jnp.sum(raised, axis=-1, keepdims=True)
            probs[2 * m + i] = prob
            mixed = dot(prob.astype(bf16), v).astype(bf16).astype(f32)
            mmbuf[t, pl.ds(2 * m + i, 1), :] = jnp.sum(mixed, axis=0, keepdims=True)
            mass.append(jnp.sum(prob, axis=0, keepdims=True))
        both = jnp.where(half_mask, jnp.concatenate(mass, axis=1), 0.0).astype(bf16)
        weighed = dot(both, rows)
        for i in range(2):
            arows[pl.ds(2 * m + i, 1), :] = weighed[i : i + 1]

    def fwd_own(k, _):
        forward(t + k * other)
        return 0

    lax.fori_loop(0, 2, fwd_own, 0)

    wait_item(2 * left + 1)
    send_item(xbuf.at[2 * left + 1], 2 * left + 1, sib)
    wait_item(2 * right)
    send_item(xbuf.at[2 * right], 2 * right, sib)

    def fwd_near(k, _):
        member = ((x + 3 + 2 * (k % 2)) % 4) * 2 + c + (k // 2) * other

        @pl.when(k >= 2)
        def _():
            wait_item(2 * member)
            wait_item(2 * member + 1)

        forward(member)
        return 0

    lax.fori_loop(0, 4, fwd_near, 0)

    wait_item(2 * far)
    send_item(xbuf.at[2 * far], 2 * far, sib)
    wait_item(2 * far + 1)
    send_item(xbuf.at[2 * far + 1], 2 * far + 1, sib)

    def fwd_far(k, _):
        member = far + k * other

        @pl.when(k >= 1)
        def _():
            wait_item(2 * member)
            wait_item(2 * member + 1)

        forward(member)
        return 0

    lax.fori_loop(0, 2, fwd_far, 0)

    def send_mm(k, _):
        push(mmbuf.at[t], mmbuf.at[t], ssem.at[MM], rsem.at[MM], tp_dev((t + k) % 8))
        return 0

    lax.fori_loop(1, 8, send_mm, 0, unroll=True)
    await_bytes(wobuf.at[pl.ds(0, 15)], rsem.at[WO])
    await_bytes(mcbuf.at[pl.ds(0, 7)], rsem.at[MC])
    await_bytes(mmbuf.at[pl.ds(0, 7)], rsem.at[MM])

    wo_slice = wobuf[...].reshape(INNER, SLICE)
    summed = jnp.concatenate([mmbuf[h] for h in range(8)], axis=1)
    product = dot(jnp.concatenate(split(summed), axis=0), wo_slice)
    means = jnp.concatenate([mcbuf[m] for m in range(8)], axis=0)
    pooled = means + (product[:16] + product[16:]) * (1.0 / CROP)
    pobuf[p] = pooled

    def send_po(k, _):
        q = (p + k) % 16
        push(pobuf.at[p], pobuf.at[p], ssem.at[PO], rsem.at[PO], plane_dev(q))
        return 0

    lax.fori_loop(1, 16, send_po, 0, unroll=True)

    own = (lane16 == sub16 + p * 16).astype(f32)
    for s in range(16):
        q = (s % 2) * 8 + s // 2
        easend[q, :, :128] = arows[:, s * 128 : (s + 1) * 128].astype(bf16)
        easend[q, :, 128:] = mmbuf[s // 2].astype(bf16)
    eabuf[p] = easend[p]

    def send_ea(k, _):
        q = (p + k) % 16
        push(easend.at[q], eabuf.at[p], ssem.at[EA], rsem.at[EA], plane_dev(q))
        return 0

    lax.fori_loop(1, 16, send_ea, 0)
    await_bytes(pobuf.at[pl.ds(0, 15)], rsem.at[PO])
    everyone = pobuf[...].reshape(256, SLICE)
    parts = split(everyone)
    grbuf[t, pl.ds(0, 16), :] = dot3(pooled, parts, NT)
    squares = jnp.concatenate(split(everyone * everyone), axis=1)
    grbuf[t, pl.ds(16, 8), :] = dot(jnp.ones((8, 2 * SLICE), bf16), squares, NT)

    def send_gr(k, _):
        push(grbuf.at[t], grbuf.at[t], ssem.at[GR], rsem.at[GR], tp_dev((t + k) % 8))
        return 0

    lax.fori_loop(1, 8, send_gr, 0, unroll=True)
    await_bytes(grbuf.at[pl.ds(0, 7)], rsem.at[GR])
    gram = grbuf[0]
    for m in range(1, 8):
        gram = gram + grbuf[m]
    inv_row = lax.rsqrt(gram[16:17] + embed_eps)
    inv_col = jnp.sum(own * inv_row, axis=1, keepdims=True)
    sims = gram[:16] * inv_col * inv_row * inv_tau
    exponents = jnp.where(own > 0.5, 0.0, jnp.exp(sims - inv_tau))
    totals = jnp.sum(exponents, axis=1, keepdims=True)
    tobuf[p] = jnp.sum(own * totals, axis=0, keepdims=True)

    def send_to(k, _):
        q = (p + k) % 16
        push(tobuf.at[p], tobuf.at[p], ssem.at[TO], rsem.at[TO], plane_dev(q))
        return 0

    lax.fori_loop(1, 16, send_to, 0, unroll=True)
    losses = jnp.log(totals) + inv_tau - jnp.sum(sims * target[...], axis=1, keepdims=True)
    loss_out[...] = jnp.broadcast_to(losses, (16, 128))
    await_bytes(tobuf.at[pl.ds(0, 15)], rsem.at[TO])
    column_totals = jnp.sum(tobuf[...], axis=0)
    weights = exponents / totals + exponents / column_totals - 2.0 * target[...]
    grad_embedding = dot3(weights * inv_row, parts) * inv_tau
    along = jnp.sum(weights * sims, axis=1, keepdims=True)
    grad_pooled = (grad_embedding - pooled * inv_col * along) * inv_col
    grad_frame = (grad_pooled * (1.0 / CROP)).astype(bf16)
    partial = dot(grad_frame, wo_slice, NT)
    for h in range(8):
        gmsend[h] = partial[:, h * 128 : (h + 1) * 128]
    labuf[p, :, :SLICE] = grad_frame

    def send_gm(k, _):
        m = (t + k) % 8
        push(gmsend.at[m], gmbuf.at[t], ssem.at[GM], rsem.at[GM], tp_dev(m))
        return 0

    lax.fori_loop(1, 8, send_gm, 0, unroll=True)
    gmbuf[t] = gmsend[t]

    await_bytes(gmbuf.at[pl.ds(0, 7)], rsem.at[GM])
    gm = gmbuf[0]
    for m in range(1, 8):
        gm = gm + gmbuf[m]
    grad_mixed = gm.astype(bf16)
    labuf[p, :, SLICE:] = grad_mixed
    sub_item = lax.broadcasted_iota(jnp.int32, (16, 128), 0)

    def backward(step, _):
        for i in range(4):
            b = step * 4 + i
            part = qkvbuf[b]
            q, k, v = part[:, :128], part[:, 128:256], part[:, 256:]
            prob = probs[b]
            all_rows = dot(grad_mixed, v, NT)
            g_row = jnp.sum(jnp.where(sub_item == b, all_rows, 0.0), axis=0, keepdims=True)
            centred = g_row - jnp.sum(prob * g_row, axis=-1, keepdims=True)
            dscores = (prob * centred * score_scale).astype(bf16)
            grad_q = dot(dscores, k)
            grad_k = dot(dscores, q, TN)
            gp[b] = jnp.concatenate([grad_q, grad_k], axis=1).astype(bf16)
        return 0

    lax.fori_loop(0, 4, backward, 0)

    def scatter(k, _):
        z2 = (z + k) % 4
        for yl2 in range(2):
            rows = pl.ds(pl.multiple_of((yl2 * 4 + z2) * 256, 256), 256)
            value = dot(xt[rows, :], gp[...].reshape(16 * CROP, 256)).astype(bf16)
            for half in range(2):
                y2 = half * 2 + yl2
                block = value[half * 128 : (half + 1) * 128]
                zsend[z2, y2] = block[:, :128]
                ysend[y2, z2] = block[:, 128:]

                @pl.when(y2 != y)
                def _():
                    push(ysend.at[y2, z2], yrecv.at[y, z2], ssem.at[RY], rsem.at[RY], at(y2, z))

        @pl.when(z2 != z)
        def _():
            push(zsend.at[z2], zrecv.at[z], ssem.at[RZ], rsem.at[RZ], at(y, z2))

        def send_la(j, _):
            q = (p + j) % 16

            @pl.when(q != p)
            def _():
                push(labuf.at[p], labuf.at[p], ssem.at[LA], rsem.at[LA], plane_dev(q))
            return 0

        lax.fori_loop(4 * k - 3, 4 * k + 1, send_la, 0)
        return 0

    lax.fori_loop(1, 5, scatter, 0)
    zrecv[z] = zsend[z]
    yrecv[y] = ysend[y]

    def add_up(ref, *index):
        total = ref[(0, *index)].astype(f32)
        for q in range(1, 4):
            total = total + ref[(q, *index)].astype(f32)
        return total.astype(bf16)

    await_bytes(zrecv.at[pl.ds(0, 3)], rsem.at[RZ])
    for i in range(4):
        mid[0, i] = add_up(zrecv, i)
    for j in range(1, 4):
        y2 = (y + j) % 4
        push(mid.at[0, y2], qrecv.at[y], ssem.at[BQ], rsem.at[BQ], at(y2, z))
    qrecv[y] = mid[0, y]
    await_bytes(yrecv.at[pl.ds(0, 3)], rsem.at[RY])
    for i in range(4):
        mid[1, i] = add_up(yrecv, i)
    for j in range(1, 4):
        z2 = (z + j) % 4
        push(mid.at[1, z2], krecv.at[z], ssem.at[BK], rsem.at[BK], at(y, z2))
    krecv[z] = mid[1, z]

    await_bytes(eabuf.at[pl.ds(0, 15)], rsem.at[EA])
    await_bytes(labuf.at[pl.ds(0, 15)], rsem.at[LA])
    early = eabuf[...].reshape(256, 256)
    late = labuf[...].reshape(256, SLICE + 128)
    o_tmp[...] = dot(early[:, 128:], late[:, :SLICE], TN)
    s_fin[2] = dot(early[:, :128], late[:, SLICE:], TN).astype(bf16)
    o_fin[...] = o_tmp[pl.ds(pl.multiple_of(yh * 64, 64), 64), :].astype(bf16)

    s_cols = pl.ds(pl.multiple_of(t * 128, 128), 128)
    o_cols = pl.ds(pl.multiple_of(t * SLICE, SLICE), SLICE)

    def each_target(fn):
        def step(j, _):
            @pl.when(jnp.logical_or(j != dp, c != yh))
            def _():
                fn(j)
            return 0
        lax.fori_loop(0, 8, step, 0)

    def send_early(j):
        dev = (j, base + yh)
        push(s_fin.at[2], s_out.at[2, :, s_cols], v_send.at[j], v_recv.at[t], dev)
        push(o_fin, o_out.at[:, o_cols], o_send.at[j], o_recv.at[t], dev)

    each_target(send_early)

    def send_part(i, sends, recvs):
        def send(j):
            push(
                s_fin.at[i], s_out.at[i, :, s_cols], sends.at[j], recvs.at[t], (j, base + yh)
            )

        each_target(send)

    await_bytes(qrecv.at[pl.ds(0, 3)], rsem.at[BQ])
    s_fin[0] = add_up(qrecv)
    send_part(0, q_send, q_recv)
    await_bytes(krecv.at[pl.ds(0, 3)], rsem.at[BK])
    s_fin[1] = add_up(krecv)
    send_part(1, k_send, k_recv)

    @pl.when(c == yh)
    def _():
        s_out[:, :, s_cols] = s_fin[...]
        o_out[:, o_cols] = o_fin[...]

    def collect(m, _):
        @pl.when(jnp.logical_or(m != t, c != yh))
        def _():
            await_bytes(s_fin.at[2], v_recv.at[m])
            await_bytes(o_fin, o_recv.at[m])
            await_bytes(s_fin.at[0], q_recv.at[m])
            await_bytes(s_fin.at[1], k_recv.at[m])
        return 0

    lax.fori_loop(0, 8, collect, 0)

    def sent(j):
        await_bytes(s_fin.at[2], v_send.at[j])
        await_bytes(o_fin, o_send.at[j])
        await_bytes(s_fin.at[0], q_send.at[j])
        await_bytes(s_fin.at[1], k_send.at[j])

    each_target(sent)
    await_bytes(xbuf.at[pl.ds(0, 14)], xssem)
    for sem, ref in (
        (W, wbuf), (WO, wobuf), (EA, eabuf), (PO, pobuf), (TO, tobuf), (LA, labuf),
    ):
        await_bytes(ref.at[pl.ds(0, 15)], ssem.at[sem])
    for sem, ref in ((RZ, zrecv), (RY, yrecv), (BQ, qrecv), (BK, krecv)):
        await_bytes(ref.at[pl.ds(0, 3)], ssem.at[sem])
    for sem, ref in ((MC, mcbuf), (MM, mmbuf), (GR, grbuf), (GM, gmbuf)):
        await_bytes(ref.at[pl.ds(0, 7)], ssem.at[sem])


def norm_kernel(starts, frames, xn, mc, wide):
    def widen(r, _):
        rows = pl.ds(pl.multiple_of(r * 32, 32), 32)
        wide[rows, :] = frames[0, rows, :].astype(f32)
        return 0

    lax.fori_loop(0, 8, widen, 0)
    wide[pl.ds(2 * CROP, 8), :] = jnp.zeros((8, D), f32)
    begin = starts[pl.program_id(0)]
    base, odd = (begin // 8) * 8, begin % 8

    def chunk(r, total):
        near = wide[pl.ds(pl.multiple_of(base + r * 16, 8), 24), :]
        rows = pltpu.roll(near, 24 - odd, 0)[:16]
        centred = rows - jnp.mean(rows, axis=-1, keepdims=True)
        scale = lax.rsqrt(jnp.mean(centred * centred, axis=-1, keepdims=True) + norm_eps)
        xn[0, pl.ds(pl.multiple_of(r * 16, 16), 16), :] = (centred * scale).astype(bf16)
        return total + rows[:8] + rows[8:]

    total = lax.fori_loop(0, CROP // 16, chunk, jnp.zeros((8, D), f32))
    mean = jnp.sum(total, axis=0, keepdims=True) * (1.0 / CROP)
    for m in range(8):
        mc[0, m : m + 1, :] = mean[:, m * SLICE : (m + 1) * SLICE]


def run_norm(frames, starts):
    return pl.pallas_call(
        norm_kernel,
        grid=(2,),
        out_shape=(
            jax.ShapeDtypeStruct((2, CROP, D), bf16),
            jax.ShapeDtypeStruct((2, 8, SLICE), f32),
        ),
        in_specs=[
            pl.BlockSpec(memory_space=pltpu.SMEM),
            pl.BlockSpec((1, 2 * CROP, D), lambda i: (i, 0, 0)),
        ],
        out_specs=(
            pl.BlockSpec((1, CROP, D), lambda i: (i, 0, 0)),
            pl.BlockSpec((1, 8, SLICE), lambda i: (i, 0, 0)),
        ),
        scratch_shapes=[pltpu.VMEM((2 * CROP + 8, D), f32)],
        compiler_params=pltpu.CompilerParams(vmem_limit_bytes=24 * 1024 * 1024),
        name="norm",
    )(starts, frames)


def run_kernel(*args):
    vmem = pl.BlockSpec(memory_space=pltpu.VMEM)
    hbm = pl.BlockSpec(memory_space=pl.ANY)
    return pl.pallas_call(
        kernel,
        out_shape=(
            jax.ShapeDtypeStruct((16, 128), f32),
            jax.ShapeDtypeStruct((3, 128, INNER), bf16),
            jax.ShapeDtypeStruct((64, D), bf16),
        ),
        in_specs=[vmem, vmem, vmem, vmem, hbm, hbm, vmem],
        out_specs=(vmem, vmem, vmem),
        scratch_shapes=[
            pltpu.VMEM((3, 128, 256), f32),
            pltpu.VMEM((64, 512), f32),
            pltpu.VMEM((2, 128, QKV), bf16),
            pltpu.VMEM((2, 64, SLICE), bf16),
            pltpu.VMEM((8, 2, SLICE), f32),
            pltpu.VMEM((16, 256), f32),
            pltpu.VMEM((16, CROP, D), bf16),
            pltpu.VMEM((D, 16 * CROP), bf16),
            pltpu.VMEM((16, 128, QKV), bf16),
            pltpu.VMEM((16, 64, SLICE), bf16),
            pltpu.VMEM((8, 2, SLICE), f32),
            pltpu.VMEM((16, CROP, QKV), bf16),
            pltpu.VMEM((16, CROP, CROP), f32),
            pltpu.VMEM((16, D), f32),
            pltpu.VMEM((8, 16, 128), f32),
            pltpu.VMEM((16, 16, 256), bf16),
            pltpu.VMEM((16, 16, 256), bf16),
            pltpu.VMEM((16, 16, SLICE), f32),
            pltpu.VMEM((8, 24, 256), f32),
            pltpu.VMEM((16, 1, 256), f32),
            pltpu.VMEM((16, 16, SLICE + 128), bf16),
            pltpu.VMEM((8, 16, 128), f32),
            pltpu.VMEM((8, 16, 128), f32),
            pltpu.VMEM((16, CROP, 256), bf16),
            pltpu.VMEM((4, 4, 128, 128), bf16),
            pltpu.VMEM((4, 4, 128, 128), bf16),
            pltpu.VMEM((4, 4, 128, 128), bf16),
            pltpu.VMEM((4, 4, 128, 128), bf16),
            pltpu.VMEM((2, 4, 128, 128), bf16),
            pltpu.VMEM((4, 128, 128), bf16),
            pltpu.VMEM((4, 128, 128), bf16),
            pltpu.VMEM((3, 128, 128), bf16),
            pltpu.VMEM((128, SLICE), f32),
            pltpu.VMEM((64, SLICE), bf16),
            pltpu.VMEM((CROP, CROP), f32),
            pltpu.VMEM((HEADS, 2 * CROP), f32),
            pltpu.SemaphoreType.DMA((4,)),
            pltpu.SemaphoreType.DMA((14,)),
            pltpu.SemaphoreType.DMA((14,)),
            pltpu.SemaphoreType.DMA,
            pltpu.SemaphoreType.DMA((16,)),
        ]
        + [pltpu.SemaphoreType.DMA((8,))] * 8,
        compiler_params=pltpu.CompilerParams(
            collective_id=0, has_side_effects=True, vmem_limit_bytes=40 * 1024 * 1024
        ),
        name="encoder",
    )(*args)


STEPS = 4


def adam_kernel(
    share, o_grad, gain, gain_m, gain_s, in_w, in_m, in_s, out_w, out_m, out_s,
    new_in_w, new_in_m, new_in_s, new_out_w, new_out_m, new_out_s, new_gw, new_gm, new_gs,
    column,
):
    step = pl.program_id(0)
    rows = 128 // STEPS
    gain_row = gain[...].astype(bf16).astype(f32)
    lane = lax.broadcasted_iota(jnp.int32, (rows, 128), 1)
    sub = lax.broadcasted_iota(jnp.int32, (rows, 128), 0)
    gain_col = jnp.sum(jnp.where(lane == sub + step * rows, gain_row, 0.0), axis=1, keepdims=True)

    def part(j, total):
        i, cols = j // 4, pl.ds(pl.multiple_of(j * 256, 256), 256)
        inner = pl.ds(pl.multiple_of((j % 4) * 256, 256), 256)
        master = in_w[:, cols]
        piece = share[i, :, inner].astype(f32)
        new = adam_update(master, in_m[:, cols], in_s[:, cols], piece * gain_col, weight_decay)
        new_in_w[:, cols], new_in_m[:, cols], new_in_s[:, cols] = new
        terms = piece * master.astype(bf16).astype(f32)
        return total + terms[:, :128] + terms[:, 128:]

    total = lax.fori_loop(0, 12, part, jnp.zeros((rows, 128), f32))

    def out_part(j, _):
        cols = pl.ds(pl.multiple_of(j * 512, 512), 512)
        new = adam_update(
            out_w[:, cols], out_m[:, cols], out_s[:, cols], o_grad[:, cols].astype(f32), weight_decay
        )
        new_out_w[:, cols], new_out_m[:, cols], new_out_s[:, cols] = new
        return 0

    lax.fori_loop(0, 4, out_part, 0)
    column[pl.ds(pl.multiple_of(step * rows, rows), rows), :] = jnp.broadcast_to(
        jnp.sum(total, axis=1, keepdims=True), (rows, 128)
    )

    @pl.when(step == STEPS - 1)
    def _():
        square = lax.broadcasted_iota(jnp.int32, (128, 128), 0) == lax.broadcasted_iota(
            jnp.int32, (128, 128), 1
        )
        grad = jnp.sum(jnp.where(square, column[...], 0.0), axis=0, keepdims=True)
        new_gw[...], new_gm[...], new_gs[...] = adam_update(
            gain[...], gain_m[...], gain_s[...], grad, 0.0
        )


def run_adam(share, o_grad, gains, inputs, outputs):
    one = pl.BlockSpec((1, 128), lambda i: (0, 0))
    big = pl.BlockSpec((128 // STEPS, 3 * INNER), lambda i: (i, 0))
    mid = pl.BlockSpec((64 // STEPS, D), lambda i: (i, 0))
    shares = pl.BlockSpec((3, 128 // STEPS, INNER), lambda i: (0, i, 0))
    return pl.pallas_call(
        adam_kernel,
        grid=(STEPS,),
        out_shape=[jax.ShapeDtypeStruct((128, 3 * INNER), f32)] * 3
        + [jax.ShapeDtypeStruct((64, D), f32)] * 3
        + [jax.ShapeDtypeStruct((1, 128), f32)] * 3,
        in_specs=[shares, mid] + [one] * 3 + [big] * 3 + [mid] * 3,
        out_specs=[big] * 3 + [mid] * 3 + [one] * 3,
        scratch_shapes=[pltpu.VMEM((128, 128), f32)],
        compiler_params=pltpu.CompilerParams(vmem_limit_bytes=24 * 1024 * 1024),
        name="adam",
    )(share, o_grad, *gains, *inputs, *outputs)


def per_device(
    frames, crop_starts, pairing, bias_table,
    input_master, input_moment, input_square,
    output_master, output_moment, output_square,
    gain_master, gain_moment, gain_square,
):
    t = 2 * (lax.axis_index("dp") // 2) + lax.axis_index("shard") % 2
    gains = [g.reshape(1, 128) for g in (gain_master, gain_moment, gain_square)]
    losses, s_grad, o_grad = run_kernel(
        *run_norm(frames, crop_starts), pairing.reshape(1, 256), bias_table,
        input_master, output_master, gains[0],
    )
    pair_losses = lax.dynamic_slice(losses, (2 * t, 0), (2, 1)).reshape(2)
    new = run_adam(
        s_grad, o_grad, gains,
        (input_master, input_moment, input_square),
        (output_master, output_moment, output_square),
    )
    return (pair_losses, *new[:6], *(g.reshape(128) for g in new[6:]))


def solution(mesh):
    one = P("shard")
    two = P("shard", None)
    items = P(("dp", "shard"))
    in_specs = (P(("dp", "shard"), None, None), items, P(), P()) + (two,) * 6 + (one,) * 3
    out_specs = (items,) + (two,) * 6 + (one,) * 3
    return jax.shard_map(
        per_device, mesh=mesh, in_specs=in_specs, out_specs=out_specs, check_vma=False
    )
```

```python
import functools

import jax
import jax.numpy as jnp
from jax import lax
from jax.experimental import pallas as pl
from jax.experimental.pallas import tpu as pltpu
from jax.sharding import PartitionSpec as P

D = 2048
HEADS = 8
HEAD_DIM = 128
INNER = 1024
CROP = 128
QKV = 3 * HEAD_DIM
SLICE = D // 8

inv_tau = 20.0
norm_eps = 1e-05
embed_eps = 1e-06
beta_one = 0.9
beta_two = 0.999
adam_eps = 1e-08
learn_rate = 0.002
weight_decay = 0.1
adam_step = 1000
score_scale = HEAD_DIM ** (-0.5)

f32 = jnp.float32
bf16 = jnp.bfloat16
NT = (((1,), (1,)), ((), ()))
TN = (((0,), (0,)), ((), ()))


def dot(a, b, dims=(((1,), (0,)), ((), ()))):
    return lax.dot_general(a, b, dims, preferred_element_type=f32)


def split(a):
    high = a.astype(bf16)
    return high, (a - high.astype(f32)).astype(bf16)


def dot3(a, b, dims=(((1,), (0,)), ((), ()))):
    rows = a.shape[0]
    high, low = split(a)
    both = dot(jnp.concatenate([high, low], axis=0), b[0], dims)
    return both[:rows] + both[rows:] + dot(high, b[1], dims)


def adam_update(master, moment, square, gradient, decay):
    moment_new = beta_one * moment + (1.0 - beta_one) * gradient
    square_new = beta_two * square + (1.0 - beta_two) * gradient * gradient
    mean_scale = learn_rate / (1.0 - beta_one**adam_step)
    square_scale = 1.0 / (1.0 - beta_two**adam_step)
    step = moment_new * mean_scale / (jnp.sqrt(square_new * square_scale) + adam_eps)
    return (master * (1.0 - learn_rate * decay) - step, moment_new, square_new)


W, WO, MC, MM, EA, PO, GR, TO, LA, GM, RZ, RY, BQ, BK = range(14)


def div(a, b):
    return lax.div(a, jnp.int32(b))


def rem(a, b):
    return lax.rem(a, jnp.int32(b))


def item_of(row):
    t, p = (row // 2) % 8, row // 16
    return 2 * (
        ((t // 2) * 2 + p // 8) * 16 + ((p // 4) % 2) * 8 + (p % 4) * 2 + t % 2
    ) + row % 2


def kernel(
    xn, mc, pairing, bias, input_master, output_master, gain,
    loss_out, s_out, o_out,
    wraw, woraw, wp, wo2, mcsend, target,
    xbuf, xt, wbuf, wobuf, mcbuf, qkvbuf, probs, arows, mmbuf, eabuf, easend, pobuf, grbuf,
    tobuf, labuf, gmsend, gmbuf, gp, zsend, ysend, zrecv, yrecv, zmid, ymid, qrecv, krecv, s_fin, o_tmp, o_fin, band, table,
    lsem, ssem, rsem, xssem, xrsem, f_send, f_recv,
):
    dp = lax.axis_index("dp")
    sh = lax.axis_index("shard")
    x, yh = div(dp, 2), rem(dp, 2)
    yl, z, c = div(sh, 8), rem(div(sh, 2), 4), rem(sh, 2)
    base = yl * 8 + z * 2
    t = 2 * x + c
    p = yh * 8 + yl * 4 + z
    y = yh * 2 + yl

    def tp_dev(m):
        return (div(m, 2) * 2 + yh, base + rem(m, 2))

    def plane_dev(q):
        return (x * 2 + div(q, 8), rem(div(q, 4), 2) * 8 + rem(q, 4) * 2 + c)

    def at(y2, z2):
        y2 = jnp.int32(y2)
        return (x * 2 + div(y2, 2), rem(y2, 2) * 8 + z2 * 2 + c)

    def push(src, dst, send, recv, dev):
        pltpu.make_async_remote_copy(
            src_ref=src, dst_ref=dst, send_sem=send, recv_sem=recv,
            device_id=dev, device_id_type=pl.DeviceIdType.MESH,
        ).start()

    def await_bytes(ref, sem):
        pltpu.make_async_copy(ref, ref, sem).wait()

    loads = []
    for i in range(3):
        cols = pl.ds(pl.multiple_of(i * INNER + x * 256, 256), 256)
        loads.append(
            pltpu.make_async_copy(input_master.at[:, cols], wraw.at[i], lsem.at[i])
        )
    loads.append(
        pltpu.make_async_copy(
            output_master.at[:, pl.ds(pl.multiple_of(x * 512, 512), 512)], woraw, lsem.at[3]
        )
    )
    for load in loads:
        load.start()

    barrier = pltpu.get_barrier_semaphore()

    def greet(dev):
        pl.semaphore_signal(barrier, inc=1, device_id=dev, device_id_type=pl.DeviceIdType.MESH)

    for k in range(1, 16):
        greet((dp, rem(sh + k, 16)))
    for k in range(8):
        greet((x * 2 + 1 - yh, div(jnp.int32(k), 4) * 8 + (k % 4) * 2 + c))
    for k in range(1, 8):
        j = rem(dp + k, 8)
        greet((j, base + 1 - c))
        if k % 2 == 0:
            greet((j, base + c))
        else:
            @pl.when(div(j, 2) != x)
            def _():
                greet((j, base + c))

    right = rem(x + 1, 4) * 2 + c
    left = rem(x + 3, 4) * 2 + c
    far = rem(x + 2, 4) * 2 + c
    sib = x * 2 + 1 - c
    other = 1 - 2 * c

    def send_item(src, slot, member):
        push(src, xbuf.at[slot], xssem, xrsem.at[slot], tp_dev(member))

    pl.semaphore_wait(barrier, 36)
    send_item(xn.at[0], 2 * t, right)
    send_item(xn.at[1], 2 * t + 1, left)
    send_item(xn.at[0], 2 * t, sib)
    send_item(xn.at[1], 2 * t + 1, sib)
    send_item(xn.at[1], 2 * t + 1, right)
    send_item(xn.at[0], 2 * t, left)

    for load in loads:
        load.wait()
    square = lax.broadcasted_iota(jnp.int32, (128, 128), 0) == lax.broadcasted_iota(
        jnp.int32, (128, 128), 1
    )
    gain_row = gain[...].astype(bf16).astype(f32)
    gain_col = jnp.sum(jnp.where(square, gain_row, 0.0), axis=1, keepdims=True)
    for core in range(2):
        for i in range(3):
            piece = wraw[i, :, core * 128 : (core + 1) * 128].astype(bf16).astype(f32)
            wp[core, :, i * 128 : (i + 1) * 128] = (piece * gain_col).astype(bf16)
        wo2[core] = woraw[:, core * SLICE : (core + 1) * SLICE].astype(bf16)

    def send_w(k, _):
        s = rem(sh + k, 16)
        push(wp.at[rem(s, 2)], wbuf.at[sh], ssem.at[W], rsem.at[W], (dp, s))
        return 0

    lax.fori_loop(1, 16, send_w, 0, unroll=True)

    def send_wo(k, _):
        s = rem(sh + k, 16)
        push(wo2.at[rem(s, 2)], wobuf.at[sh], ssem.at[WO], rsem.at[WO], (dp, s))
        return 0

    lax.fori_loop(1, 16, send_wo, 0, unroll=True)

    for m in range(8):
        for i in range(2):
            mcsend[m, i : i + 1, :] = mc[i, m : m + 1, :]

    def send_mc(k, _):
        m = rem(t + k, 8)
        push(mcsend.at[m], mcbuf.at[t], ssem.at[MC], rsem.at[MC], tp_dev(m))
        return 0

    lax.fori_loop(1, 8, send_mc, 0, unroll=True)

    wbuf[sh] = wp[c]
    wobuf[sh] = wo2[c]
    mcbuf[t] = mcsend[t]
    xbuf[2 * t] = xn[0]
    xbuf[2 * t + 1] = xn[1]

    table[...] = jnp.zeros_like(table)
    table[:, : 2 * CROP - 1] = bias[...]
    row = jnp.broadcast_to(table[pl.ds(t, 1), :], (CROP, 2 * CROP))
    shifted = pltpu.roll(row, CROP + 1, 1, stride=1, stride_axis=0)
    band[...] = shifted[:, :CROP].T

    lane16 = lax.broadcasted_iota(jnp.int32, (16, 256), 1)
    sub16 = lax.broadcasted_iota(jnp.int32, (16, 256), 0)
    pair = jnp.broadcast_to(pairing[...], (16, 256))
    swapped = jnp.where(lane16 % 2 == 0, pltpu.roll(pair, 255, 1), pltpu.roll(pair, 1, 1))
    hot_a = (pair == item_of(sub16 + p * 16)).astype(f32).astype(bf16)
    rows256 = lax.broadcasted_iota(jnp.int32, (256, 256), 0)
    hot_b = (jnp.broadcast_to(swapped[:1], (256, 256)) == item_of(rows256)).astype(f32).astype(bf16)
    target[...] = dot(hot_a, hot_b, NT)

    def wait_item(slot):
        await_bytes(xbuf.at[slot], xrsem.at[slot])

    wait_item(2 * left)
    send_item(xbuf.at[2 * left], 2 * left, right)
    send_item(xbuf.at[2 * left], 2 * left, sib)
    wait_item(2 * right + 1)
    send_item(xbuf.at[2 * right + 1], 2 * right + 1, left)
    send_item(xbuf.at[2 * right + 1], 2 * right + 1, sib)
    wait_item(2 * sib)
    wait_item(2 * sib + 1)
    await_bytes(wbuf.at[pl.ds(0, 15)], rsem.at[W])

    half_mask = (
        lax.broadcasted_iota(jnp.int32, (16, 256), 0)
        == lax.broadcasted_iota(jnp.int32, (16, 256), 1) // 128
    )

    def forward(m):
        rows = xbuf[pl.ds(2 * m, 2)].reshape(2 * CROP, D)
        packed = dot(rows, wbuf[...].reshape(D, QKV)).astype(bf16)
        xt[:, pl.ds(pl.multiple_of(m * 256, 256), 256)] = rows.T
        qkvbuf[pl.ds(2 * m, 2)] = packed.reshape(2, CROP, QKV)
        mass = []
        for i in range(2):
            part = packed[i * CROP : (i + 1) * CROP]
            q, k, v = part[:, :128], part[:, 128:256], part[:, 256:]
            scores = dot(q, k, NT) * score_scale + band[...]
            raised = jnp.exp(scores - jnp.max(scores, axis=-1, keepdims=True))
            prob = raised / jnp.sum(raised, axis=-1, keepdims=True)
            probs[2 * m + i] = prob
            mixed = dot(prob.astype(bf16), v).astype(bf16).astype(f32)
            mmbuf[t, pl.ds(2 * m + i, 1), :] = jnp.sum(mixed, axis=0, keepdims=True)
            mass.append(jnp.sum(prob, axis=0, keepdims=True))
        both = jnp.where(half_mask, jnp.concatenate(mass, axis=1), 0.0).astype(bf16)
        weighed = dot(both, rows)
        for i in range(2):
            arows[pl.ds(2 * m + i, 1), :] = weighed[i : i + 1]

    def fwd_own(k, _):
        forward(t + k * other)
        return 0

    lax.fori_loop(0, 2, fwd_own, 0)

    wait_item(2 * left + 1)
    send_item(xbuf.at[2 * left + 1], 2 * left + 1, sib)
    wait_item(2 * right)
    send_item(xbuf.at[2 * right], 2 * right, sib)

    def fwd_near(k, _):
        member = rem(x + 3 + 2 * rem(k, 2), 4) * 2 + c + div(k, 2) * other

        @pl.when(k >= 2)
        def _():
            wait_item(2 * member)
            wait_item(2 * member + 1)

        forward(member)
        return 0

    lax.fori_loop(0, 4, fwd_near, 0)

    wait_item(2 * far)
    send_item(xbuf.at[2 * far], 2 * far, sib)
    wait_item(2 * far + 1)
    send_item(xbuf.at[2 * far + 1], 2 * far + 1, sib)

    def fwd_far(k, _):
        member = far + k * other

        @pl.when(k >= 1)
        def _():
            wait_item(2 * member)
            wait_item(2 * member + 1)

        forward(member)
        return 0

    lax.fori_loop(0, 2, fwd_far, 0)

    def send_mm(k, _):
        push(mmbuf.at[t], mmbuf.at[t], ssem.at[MM], rsem.at[MM], tp_dev(rem(t + k, 8)))
        return 0

    lax.fori_loop(1, 8, send_mm, 0, unroll=True)
    await_bytes(wobuf.at[pl.ds(0, 15)], rsem.at[WO])
    await_bytes(mcbuf.at[pl.ds(0, 7)], rsem.at[MC])
    await_bytes(mmbuf.at[pl.ds(0, 7)], rsem.at[MM])

    wo_slice = wobuf[...].reshape(INNER, SLICE)
    summed = jnp.concatenate([mmbuf[h] for h in range(8)], axis=1)
    product = dot(jnp.concatenate(split(summed), axis=0), wo_slice)
    means = jnp.concatenate([mcbuf[m] for m in range(8)], axis=0)
    pooled = means + (product[:16] + product[16:]) * (1.0 / CROP)
    pobuf[p] = pooled

    def send_po(k, _):
        q = rem(p + k, 16)
        push(pobuf.at[p], pobuf.at[p], ssem.at[PO], rsem.at[PO], plane_dev(q))
        return 0

    lax.fori_loop(1, 16, send_po, 0, unroll=True)

    own = (lane16 == sub16 + p * 16).astype(f32)
    for s in range(16):
        q = (s % 2) * 8 + s // 2
        easend[q, :, :128] = arows[:, s * 128 : (s + 1) * 128].astype(bf16)
        easend[q, :, 128:] = mmbuf[s // 2].astype(bf16)
    eabuf[p] = easend[p]

    def send_ea(k, _):
        q = rem(p + k, 16)
        push(easend.at[q], eabuf.at[p], ssem.at[EA], rsem.at[EA], plane_dev(q))
        return 0

    lax.fori_loop(1, 16, send_ea, 0, unroll=True)
    await_bytes(pobuf.at[pl.ds(0, 15)], rsem.at[PO])
    everyone = pobuf[...].reshape(256, SLICE)
    parts = split(everyone)
    grbuf[t, pl.ds(0, 16), :] = dot3(pooled, parts, NT)
    squares = jnp.concatenate(split(everyone * everyone), axis=1)
    grbuf[t, pl.ds(16, 8), :] = dot(jnp.ones((8, 2 * SLICE), bf16), squares, NT)

    def send_gr(k, _):
        push(grbuf.at[t], grbuf.at[t], ssem.at[GR], rsem.at[GR], tp_dev(rem(t + k, 8)))
        return 0

    lax.fori_loop(1, 8, send_gr, 0, unroll=True)
    await_bytes(grbuf.at[pl.ds(0, 7)], rsem.at[GR])
    gram = grbuf[0]
    for m in range(1, 8):
        gram = gram + grbuf[m]
    inv_row = lax.rsqrt(gram[16:17] + embed_eps)
    inv_col = jnp.sum(own * inv_row, axis=1, keepdims=True)
    sims = gram[:16] * inv_col * inv_row * inv_tau
    exponents = jnp.where(own > 0.5, 0.0, jnp.exp(sims - inv_tau))
    totals = jnp.sum(exponents, axis=1, keepdims=True)
    tobuf[p] = jnp.sum(own * totals, axis=0, keepdims=True)

    def send_to(k, _):
        q = rem(p + k, 16)
        push(tobuf.at[p], tobuf.at[p], ssem.at[TO], rsem.at[TO], plane_dev(q))
        return 0

    lax.fori_loop(1, 16, send_to, 0, unroll=True)
    losses = jnp.log(totals) + inv_tau - jnp.sum(sims * target[...], axis=1, keepdims=True)
    loss_out[...] = jnp.broadcast_to(losses, (16, 128))
    await_bytes(tobuf.at[pl.ds(0, 15)], rsem.at[TO])
    column_totals = jnp.sum(tobuf[...], axis=0)
    weights = exponents / totals + exponents / column_totals - 2.0 * target[...]
    grad_embedding = dot3(weights * inv_row, parts) * inv_tau
    along = jnp.sum(weights * sims, axis=1, keepdims=True)
    grad_pooled = (grad_embedding - pooled * inv_col * along) * inv_col
    grad_frame = (grad_pooled * (1.0 / CROP)).astype(bf16)
    partial = dot(grad_frame, wo_slice, NT)
    for h in range(8):
        gmsend[h] = partial[:, h * 128 : (h + 1) * 128]
    labuf[p, :, :SLICE] = grad_frame

    def send_gm(k, _):
        m = rem(t + k, 8)
        push(gmsend.at[m], gmbuf.at[t], ssem.at[GM], rsem.at[GM], tp_dev(m))
        return 0

    lax.fori_loop(1, 8, send_gm, 0, unroll=True)
    gmbuf[t] = gmsend[t]

    await_bytes(gmbuf.at[pl.ds(0, 7)], rsem.at[GM])
    gm = gmbuf[0]
    for m in range(1, 8):
        gm = gm + gmbuf[m]
    grad_mixed = gm.astype(bf16)
    labuf[p, :, SLICE:] = grad_mixed
    sub_item = lax.broadcasted_iota(jnp.int32, (16, 128), 0)

    def backward(step, _):
        for i in range(8):
            b = step * 8 + i
            part = qkvbuf[b]
            q, k, v = part[:, :128], part[:, 128:256], part[:, 256:]
            prob = probs[b]
            all_rows = dot(grad_mixed, v, NT)
            g_row = jnp.sum(jnp.where(sub_item == b, all_rows, 0.0), axis=0, keepdims=True)
            centred = g_row - jnp.sum(prob * g_row, axis=-1, keepdims=True)
            dscores = (prob * centred * score_scale).astype(bf16)
            grad_q = dot(dscores, k)
            grad_k = dot(dscores, q, TN)
            gp[b] = jnp.concatenate([grad_q, grad_k], axis=1).astype(bf16)

        def send_la(j, _):
            q = rem(p + j, 16)
            push(labuf.at[p], labuf.at[p], ssem.at[LA], rsem.at[LA], plane_dev(q))
            return 0

        lax.fori_loop(1 + 8 * step, 9 + 7 * step, send_la, 0)
        return 0

    lax.fori_loop(0, 2, backward, 0)

    def scatter(k, _):
        z2 = rem(z + k, 4)
        for yl2 in range(2):
            rows = pl.ds(pl.multiple_of((yl2 * 4 + z2) * 256, 256), 256)
            value = dot(xt[rows, :], gp[...].reshape(16 * CROP, 256)).astype(bf16)
            for half in range(2):
                y2 = half * 2 + yl2
                block = value[half * 128 : (half + 1) * 128]
                zsend[z2, y2, :128] = block[:, :128]
                zsend[z2, y2, 128:] = block[:64, 128:]
                ysend[y2, z2] = block[64:, 128:]

                @pl.when(y2 != y)
                def _():
                    push(ysend.at[y2, z2], yrecv.at[y, z2], ssem.at[RY], rsem.at[RY], at(y2, z))

        @pl.when(z2 != z)
        def _():
            push(zsend.at[z2], zrecv.at[z], ssem.at[RZ], rsem.at[RZ], at(y, z2))

        return 0

    lax.fori_loop(1, 5, scatter, 0)
    zrecv[z] = zsend[z]
    yrecv[y] = ysend[y]

    def add_up(ref, *index):
        total = ref[(0, *index)].astype(f32)
        for q in range(1, 4):
            total = total + ref[(q, *index)].astype(f32)
        return total.astype(bf16)

    await_bytes(yrecv.at[pl.ds(0, 3)], rsem.at[RY])
    for i in range(4):
        ymid[i] = add_up(yrecv, i)
    for j in range(1, 4):
        z2 = rem(z + j, 4)
        push(ymid.at[z2], krecv.at[z], ssem.at[BK], rsem.at[BK], at(y, z2))
    krecv[z] = ymid[z]

    await_bytes(eabuf.at[pl.ds(0, 15)], rsem.at[EA])
    await_bytes(labuf.at[pl.ds(0, 15)], rsem.at[LA])
    early = eabuf[...].reshape(256, 256)
    late = labuf[...].reshape(256, SLICE + 128)
    o_tmp[...] = dot(early[:, 128:], late[:, :SLICE], TN)
    s_fin[2] = dot(early[:, :128], late[:, SLICE:], TN).astype(bf16)
    o_fin[...] = o_tmp[pl.ds(pl.multiple_of(yh * 64, 64), 64), :].astype(bf16)

    s_cols = pl.ds(pl.multiple_of(t * 128, 128), 128)
    o_cols = pl.ds(pl.multiple_of(t * SLICE, SLICE), SLICE)

    def each_target(fn):
        for k in range(1, 8):
            fn(rem(dp + k, 8))

        @pl.when(c != yh)
        def _():
            fn(dp)

    def send_early(j):
        dev = (j, base + yh)
        push(s_fin.at[2], s_out.at[2, :, s_cols], f_send.at[2], f_recv.at[2], dev)
        push(o_fin, o_out.at[:, o_cols], f_send.at[3], f_recv.at[3], dev)

    each_target(send_early)

    await_bytes(zrecv.at[pl.ds(0, 3)], rsem.at[RZ])
    for i in range(4):
        zmid[i] = add_up(zrecv, i)
    for j in range(1, 4):
        y2 = rem(y + j, 4)
        push(zmid.at[y2], qrecv.at[y], ssem.at[BQ], rsem.at[BQ], at(y2, z))
    qrecv[y] = zmid[y]

    def send_part(i, rows, sem):
        def send(j):
            push(
                s_fin.at[i, rows], s_out.at[i, rows, s_cols], f_send.at[sem], f_recv.at[sem],
                (j, base + yh),
            )

        each_target(send)

    all_rows, first_half, last_half = pl.ds(0, 128), pl.ds(0, 64), pl.ds(64, 64)
    await_bytes(krecv.at[pl.ds(0, 3)], rsem.at[BK])
    s_fin[1, 64:] = add_up(krecv)
    send_part(1, last_half, 4)
    await_bytes(qrecv.at[pl.ds(0, 3)], rsem.at[BQ])
    added = add_up(qrecv)
    s_fin[0] = added[:128]
    s_fin[1, :64] = added[128:]
    send_part(0, all_rows, 0)
    send_part(1, first_half, 1)

    @pl.when(c == yh)
    def _():
        s_out[:, :, s_cols] = s_fin[...]
        o_out[:, o_cols] = o_fin[...]

    def await_all(sems):
        def await_parts(members):
            cols = pl.ds(0, members * 128)
            await_bytes(s_out.at[0, :, cols], sems.at[0])
            await_bytes(s_out.at[1, first_half, cols], sems.at[1])
            await_bytes(s_out.at[2, :, cols], sems.at[2])
            await_bytes(o_out.at[:, pl.ds(0, members * SLICE)], sems.at[3])
            await_bytes(s_out.at[1, last_half, cols], sems.at[4])

        @pl.when(c == yh)
        def _():
            await_parts(7)

        @pl.when(c != yh)
        def _():
            await_parts(8)

    await_all(f_recv)
    await_all(f_send)
    await_bytes(xbuf.at[pl.ds(0, 14)], xssem)
    for sem, ref in (
        (W, wbuf), (WO, wobuf), (EA, eabuf), (PO, pobuf), (TO, tobuf), (LA, labuf),
    ):
        await_bytes(ref.at[pl.ds(0, 15)], ssem.at[sem])
    for sem, ref in ((RZ, zrecv), (RY, yrecv), (BQ, qrecv), (BK, krecv)):
        await_bytes(ref.at[pl.ds(0, 3)], ssem.at[sem])
    for sem, ref in ((MC, mcbuf), (MM, mmbuf), (GR, grbuf), (GM, gmbuf)):
        await_bytes(ref.at[pl.ds(0, 7)], ssem.at[sem])


def norm_kernel(starts, frames, xn, mc, raw, sems):
    begin = [starts[i] for i in range(2)]
    base = [(b // 16) * 16 for b in begin]
    base = [jnp.minimum(b, CROP - 16) for b in base]
    loads = [
        pltpu.make_async_copy(
            frames.at[i, pl.ds(pl.multiple_of(base[i], 16), CROP + 16)], raw.at[i], sems.at[i]
        )
        for i in range(2)
    ]
    for load in loads:
        load.start()
    for i in range(2):
        loads[i].wait()
        odd = begin[i] - base[i]

        def chunk(r, total):
            near = raw[i, pl.ds(pl.multiple_of(r * 16, 16), 32), :].astype(f32)
            rows = pltpu.roll(near, (32 - odd) % 32, 0)[:16]
            centred = rows - jnp.mean(rows, axis=-1, keepdims=True)
            scale = lax.rsqrt(jnp.mean(centred * centred, axis=-1, keepdims=True) + norm_eps)
            xn[i, pl.ds(pl.multiple_of(r * 16, 16), 16), :] = (centred * scale).astype(bf16)
            return total + rows[:8] + rows[8:]

        total = lax.fori_loop(0, CROP // 16, chunk, jnp.zeros((8, D), f32), unroll=4)
        mean = jnp.sum(total, axis=0, keepdims=True) * (1.0 / CROP)
        for m in range(8):
            mc[i, m : m + 1, :] = mean[:, m * SLICE : (m + 1) * SLICE]


def run_norm(frames, starts):
    vmem = pl.BlockSpec(memory_space=pltpu.VMEM)
    return pl.pallas_call(
        norm_kernel,
        out_shape=(
            jax.ShapeDtypeStruct((2, CROP, D), bf16),
            jax.ShapeDtypeStruct((2, 8, SLICE), f32),
        ),
        in_specs=[
            pl.BlockSpec(memory_space=pltpu.SMEM), pl.BlockSpec(memory_space=pltpu.HBM),
        ],
        out_specs=(vmem, vmem),
        scratch_shapes=[
            pltpu.VMEM((2, CROP + 16, D), bf16),
            pltpu.SemaphoreType.DMA((2,)),
        ],
        compiler_params=pltpu.CompilerParams(vmem_limit_bytes=24 * 1024 * 1024),
        name="norm",
    )(starts, frames)


def run_kernel(*args):
    vmem = pl.BlockSpec(memory_space=pltpu.VMEM)
    hbm = pl.BlockSpec(memory_space=pltpu.HBM)
    return pl.pallas_call(
        kernel,
        out_shape=(
            jax.ShapeDtypeStruct((16, 128), f32),
            jax.ShapeDtypeStruct((3, 128, INNER), bf16),
            jax.ShapeDtypeStruct((64, D), bf16),
        ),
        in_specs=[vmem, vmem, vmem, vmem, hbm, hbm, vmem],
        out_specs=(vmem, vmem, vmem),
        scratch_shapes=[
            pltpu.VMEM((3, 128, 256), f32),
            pltpu.VMEM((64, 512), f32),
            pltpu.VMEM((2, 128, QKV), bf16),
            pltpu.VMEM((2, 64, SLICE), bf16),
            pltpu.VMEM((8, 2, SLICE), f32),
            pltpu.VMEM((16, 256), f32),
            pltpu.VMEM((16, CROP, D), bf16),
            pltpu.VMEM((D, 16 * CROP), bf16),
            pltpu.VMEM((16, 128, QKV), bf16),
            pltpu.VMEM((16, 64, SLICE), bf16),
            pltpu.VMEM((8, 2, SLICE), f32),
            pltpu.VMEM((16, CROP, QKV), bf16),
            pltpu.VMEM((16, CROP, CROP), f32),
            pltpu.VMEM((16, D), f32),
            pltpu.VMEM((8, 16, 128), f32),
            pltpu.VMEM((16, 16, 256), bf16),
            pltpu.VMEM((16, 16, 256), bf16),
            pltpu.VMEM((16, 16, SLICE), f32),
            pltpu.VMEM((8, 24, 256), f32),
            pltpu.VMEM((16, 1, 256), f32),
            pltpu.VMEM((16, 16, SLICE + 128), bf16),
            pltpu.VMEM((8, 16, 128), f32),
            pltpu.VMEM((8, 16, 128), f32),
            pltpu.VMEM((16, CROP, 256), bf16),
            pltpu.VMEM((4, 4, 192, 128), bf16),
            pltpu.VMEM((4, 4, 64, 128), bf16),
            pltpu.VMEM((4, 4, 192, 128), bf16),
            pltpu.VMEM((4, 4, 64, 128), bf16),
            pltpu.VMEM((4, 192, 128), bf16),
            pltpu.VMEM((4, 64, 128), bf16),
            pltpu.VMEM((4, 192, 128), bf16),
            pltpu.VMEM((4, 64, 128), bf16),
            pltpu.VMEM((3, 128, 128), bf16),
            pltpu.VMEM((128, SLICE), f32),
            pltpu.VMEM((64, SLICE), bf16),
            pltpu.VMEM((CROP, CROP), f32),
            pltpu.VMEM((HEADS, 2 * CROP), f32),
            pltpu.SemaphoreType.DMA((4,)),
            pltpu.SemaphoreType.DMA((14,)),
            pltpu.SemaphoreType.DMA((14,)),
            pltpu.SemaphoreType.DMA,
            pltpu.SemaphoreType.DMA((16,)),
        ]
        + [pltpu.SemaphoreType.DMA((5,))] * 2,
        compiler_params=pltpu.CompilerParams(
            collective_id=0, has_side_effects=True, vmem_limit_bytes=40 * 1024 * 1024
        ),
        name="encoder",
    )(*args)


STEPS = 4


def adam_kernel(
    share, o_grad, losses, gain, gain_m, gain_s, in_w, in_m, in_s, out_w, out_m, out_s,
    pair_losses, new_in_w, new_in_m, new_in_s, new_out_w, new_out_m, new_out_s, new_gw, new_gm, new_gs,
    column, state, square_in, in_new, out_new, lsems, ssems, isems, osems,
):
    loads = [
        pltpu.make_async_copy(ref, state.at[i], lsems.at[i])
        for i, ref in enumerate((out_w, out_m, out_s))
    ]
    chunks = [
        pltpu.make_async_copy(
            in_s.at[pl.ds(i * 32, 32)], square_in.at[pl.ds(i * 32, 32)], ssems.at[i]
        )
        for i in range(STEPS)
    ]
    for load in chunks + loads:
        load.start()
    t = 2 * (lax.axis_index("dp") // 2) + lax.axis_index("shard") % 2
    item = lax.broadcasted_iota(jnp.int32, (16, 128), 0)
    lane = lax.broadcasted_iota(jnp.int32, (16, 128), 1)
    for i in range(2):
        mine = jnp.logical_and(item == 2 * t + i, lane == 0)
        pair_losses[i] = jnp.sum(jnp.where(mine, losses[...], 0.0))
    square = lax.broadcasted_iota(jnp.int32, (128, 128), 0) == lax.broadcasted_iota(
        jnp.int32, (128, 128), 1
    )
    gain_row = gain[...].astype(bf16).astype(f32)
    column[...] = jnp.broadcast_to(
        jnp.sum(jnp.where(square, gain_row, 0.0), axis=1, keepdims=True), (128, 128)
    )
    rows = 128 // STEPS
    stores = []
    for step in range(STEPS):
        at_rows = pl.ds(step * rows, rows)
        chunks[step].wait()
        gain_col = column[at_rows, :][:, :1]

        def part(j, total):
            i, cols = j // 2, pl.ds(pl.multiple_of(j * 512, 512), 512)
            inner = pl.ds(pl.multiple_of((j % 2) * 512, 512), 512)
            master = in_w[at_rows, cols]
            piece = share[i, at_rows, inner].astype(f32)
            new = adam_update(
                master, in_m[at_rows, cols], square_in[at_rows, cols], piece * gain_col, weight_decay
            )
            for n in range(3):
                in_new[n, at_rows, cols] = new[n]
            terms = piece * master.astype(bf16).astype(f32)
            return total + sum(terms[:, n * 128 : (n + 1) * 128] for n in range(4))

        total = lax.fori_loop(0, 6, part, jnp.zeros((rows, 128), f32), unroll=2)
        column[at_rows, :] = jnp.broadcast_to(jnp.sum(total, axis=1, keepdims=True), (rows, 128))
        for n, ref in enumerate((new_in_w, new_in_m, new_in_s)):
            stores.append(
                pltpu.make_async_copy(in_new.at[n, at_rows], ref.at[at_rows], isems.at[n, step])
            )
            stores[-1].start()
    for load in loads:
        load.wait()
    for step in range(2):
        at_rows = pl.ds(step * 32, 32)

        def out_part(j, _):
            cols = pl.ds(pl.multiple_of(j * 512, 512), 512)
            new = adam_update(
                state[0, at_rows, cols], state[1, at_rows, cols], state[2, at_rows, cols],
                o_grad[at_rows, cols].astype(f32), weight_decay,
            )
            for n in range(3):
                out_new[n, at_rows, cols] = new[n]
            return 0

        lax.fori_loop(0, 4, out_part, 0, unroll=2)
        for n, ref in enumerate((new_out_w, new_out_m, new_out_s)):
            stores.append(
                pltpu.make_async_copy(out_new.at[n, at_rows], ref.at[at_rows], osems.at[n, step])
            )
            stores[-1].start()
    grad = jnp.sum(jnp.where(square, column[...], 0.0), axis=0, keepdims=True)
    new_gw[...], new_gm[...], new_gs[...] = adam_update(
        gain[...], gain_m[...], gain_s[...], grad, 0.0
    )
    for store in stores:
        store.wait()


def run_adam(share, o_grad, losses, gains, inputs, outputs):
    vmem = pl.BlockSpec(memory_space=pltpu.VMEM)
    hbm = pl.BlockSpec(memory_space=pltpu.HBM)
    return pl.pallas_call(
        adam_kernel,
        out_shape=[jax.ShapeDtypeStruct((2,), f32)]
        + [jax.ShapeDtypeStruct((128, 3 * INNER), f32)] * 3
        + [jax.ShapeDtypeStruct((64, D), f32)] * 3
        + [jax.ShapeDtypeStruct((1, 128), f32)] * 3,
        in_specs=[vmem] * 8 + [hbm] * 4,
        out_specs=[pl.BlockSpec(memory_space=pltpu.SMEM)] + [hbm] * 6 + [vmem] * 3,
        scratch_shapes=[
            pltpu.VMEM((128, 128), f32),
            pltpu.VMEM((3, 64, D), f32),
            pltpu.VMEM((128, 3 * INNER), f32),
            pltpu.VMEM((3, 128, 3 * INNER), f32),
            pltpu.VMEM((3, 64, D), f32),
            pltpu.SemaphoreType.DMA((3,)),
            pltpu.SemaphoreType.DMA((STEPS,)),
            pltpu.SemaphoreType.DMA((3, STEPS)),
            pltpu.SemaphoreType.DMA((3, 2)),
        ],
        compiler_params=pltpu.CompilerParams(vmem_limit_bytes=48 * 1024 * 1024),
        name="adam",
    )(share, o_grad, losses, *gains, *inputs, *outputs)


def per_device(
    frames, crop_starts, pairing, bias_table,
    input_master, input_moment, input_square,
    output_master, output_moment, output_square,
    gain_master, gain_moment, gain_square,
):
    gains = [g.reshape(1, 128) for g in (gain_master, gain_moment, gain_square)]
    losses, s_grad, o_grad = run_kernel(
        *run_norm(frames, crop_starts), pairing.reshape(1, 256), bias_table,
        input_master, output_master, gains[0],
    )
    new = run_adam(
        s_grad, o_grad, losses, gains,
        (input_master, input_moment, input_square),
        (output_master, output_moment, output_square),
    )
    return (*new[:7], *(g.reshape(128) for g in new[7:]))


def solution(mesh):
    one = P("shard")
    two = P("shard", None)
    items = P(("dp", "shard"))
    in_specs = (P(("dp", "shard"), None, None), items, P(), P()) + (two,) * 6 + (one,) * 3
    out_specs = (items,) + (two,) * 6 + (one,) * 3
    return jax.shard_map(
        per_device, mesh=mesh, in_specs=in_specs, out_specs=out_specs, check_vma=False
    )
```

```python
import functools

import jax
import jax.numpy as jnp
from jax import lax
from jax.experimental import pallas as pl
from jax.experimental.pallas import tpu as pltpu
from jax.sharding import PartitionSpec as P

D = 2048
HEADS = 8
HEAD_DIM = 128
INNER = 1024
CROP = 128
QKV = 3 * HEAD_DIM
SLICE = D // 8

inv_tau = 20.0
norm_eps = 1e-05
embed_eps = 1e-06
beta_one = 0.9
beta_two = 0.999
adam_eps = 1e-08
learn_rate = 0.002
weight_decay = 0.1
adam_step = 1000
score_scale = HEAD_DIM ** (-0.5)

f32 = jnp.float32
bf16 = jnp.bfloat16
NT = (((1,), (1,)), ((), ()))
TN = (((0,), (0,)), ((), ()))


def dot(a, b, dims=(((1,), (0,)), ((), ()))):
    return lax.dot_general(a, b, dims, preferred_element_type=f32)


def split(a):
    high = a.astype(bf16)
    return high, (a - high.astype(f32)).astype(bf16)


def dot3(a, b, dims=(((1,), (0,)), ((), ()))):
    rows = a.shape[0]
    high, low = split(a)
    both = dot(jnp.concatenate([high, low], axis=0), b[0], dims)
    return both[:rows] + both[rows:] + dot(high, b[1], dims)


def adam_update(master, moment, square, gradient, decay):
    moment_new = beta_one * moment + (1.0 - beta_one) * gradient
    square_new = beta_two * square + (1.0 - beta_two) * gradient * gradient
    mean_scale = learn_rate / (1.0 - beta_one**adam_step)
    square_scale = 1.0 / (1.0 - beta_two**adam_step)
    step = moment_new * mean_scale / (jnp.sqrt(square_new * square_scale) + adam_eps)
    return (master * (1.0 - learn_rate * decay) - step, moment_new, square_new)


W, WO, MC, MM, EA, PO, GR, TO, LA, GM, RZ, RY, BQ, BK, SS = range(15)


def div(a, b):
    return lax.div(a, jnp.int32(b))


def rem(a, b):
    return lax.rem(a, jnp.int32(b))


def item_of(row):
    t, p = (row // 2) % 8, row // 16
    return 2 * (
        ((t // 2) * 2 + p // 8) * 16 + ((p // 4) % 2) * 8 + (p % 4) * 2 + t % 2
    ) + row % 2


def kernel(
    xn, mc, pairing, bias, input_master, output_master, gain,
    loss_out, s_out, o_out,
    wraw, woraw, wp, wo2, mcsend, target,
    xbuf, xt, wbuf, wobuf, mcbuf, qkvbuf, probs, arows, mmbuf, eabuf, easend, pobuf, grbuf, ssbuf,
    tobuf, labuf, gmsend, gmbuf, gp, zsend, ysend, zrecv, yrecv, zmid, ymid, qrecv, krecv, s_fin, o_tmp, o_fin, band, table,
    lsem, ssem, rsem, xssem, xrsem, f_send, f_recv,
):
    dp = lax.axis_index("dp")
    sh = lax.axis_index("shard")
    x, yh = div(dp, 2), rem(dp, 2)
    yl, z, c = div(sh, 8), rem(div(sh, 2), 4), rem(sh, 2)
    base = yl * 8 + z * 2
    t = 2 * x + c
    p = yh * 8 + yl * 4 + z
    y = yh * 2 + yl

    def tp_dev(m):
        return (div(m, 2) * 2 + yh, base + rem(m, 2))

    def plane_dev(q):
        return (x * 2 + div(q, 8), rem(div(q, 4), 2) * 8 + rem(q, 4) * 2 + c)

    def at(y2, z2):
        y2 = jnp.int32(y2)
        return (x * 2 + div(y2, 2), rem(y2, 2) * 8 + z2 * 2 + c)

    def push(src, dst, send, recv, dev):
        pltpu.make_async_remote_copy(
            src_ref=src, dst_ref=dst, send_sem=send, recv_sem=recv,
            device_id=dev, device_id_type=pl.DeviceIdType.MESH,
        ).start()

    def await_bytes(ref, sem):
        pltpu.make_async_copy(ref, ref, sem).wait()

    loads = []
    for i in range(3):
        cols = pl.ds(pl.multiple_of(i * INNER + x * 256, 256), 256)
        loads.append(
            pltpu.make_async_copy(input_master.at[:, cols], wraw.at[i], lsem.at[i])
        )
    loads.append(
        pltpu.make_async_copy(
            output_master.at[:, pl.ds(pl.multiple_of(x * 512, 512), 512)], woraw, lsem.at[3]
        )
    )
    for load in loads:
        load.start()

    barrier = pltpu.get_barrier_semaphore()

    def greet(dev):
        pl.semaphore_signal(barrier, inc=1, device_id=dev, device_id_type=pl.DeviceIdType.MESH)

    for k in range(1, 16):
        greet((dp, rem(sh + k, 16)))
    for k in range(8):
        greet((x * 2 + 1 - yh, div(jnp.int32(k), 4) * 8 + (k % 4) * 2 + c))
    for k in range(1, 8):
        j = rem(dp + k, 8)
        greet((j, base + 1 - c))
        if k % 2 == 0:
            greet((j, base + c))
        else:
            @pl.when(div(j, 2) != x)
            def _():
                greet((j, base + c))

    right = rem(x + 1, 4) * 2 + c
    left = rem(x + 3, 4) * 2 + c
    far = rem(x + 2, 4) * 2 + c
    sib = x * 2 + 1 - c
    other = 1 - 2 * c

    def send_item(src, slot, member):
        push(src, xbuf.at[slot], xssem, xrsem.at[slot], tp_dev(member))

    pl.semaphore_wait(barrier, 36)
    send_item(xn.at[0], 2 * t, right)
    send_item(xn.at[1], 2 * t + 1, left)
    send_item(xn.at[0], 2 * t, sib)
    send_item(xn.at[1], 2 * t + 1, sib)
    send_item(xn.at[1], 2 * t + 1, right)
    send_item(xn.at[0], 2 * t, left)

    for load in loads:
        load.wait()
    square = lax.broadcasted_iota(jnp.int32, (128, 128), 0) == lax.broadcasted_iota(
        jnp.int32, (128, 128), 1
    )
    gain_row = gain[...].astype(bf16).astype(f32)
    gain_col = jnp.sum(jnp.where(square, gain_row, 0.0), axis=1, keepdims=True)
    for core in range(2):
        for i in range(3):
            piece = wraw[i, :, core * 128 : (core + 1) * 128].astype(bf16).astype(f32)
            wp[core, :, i * 128 : (i + 1) * 128] = (piece * gain_col).astype(bf16)
        wo2[core] = woraw[:, core * SLICE : (core + 1) * SLICE].astype(bf16)

    def send_w(k, _):
        s = rem(sh + k, 16)
        push(wp.at[rem(s, 2)], wbuf.at[sh], ssem.at[W], rsem.at[W], (dp, s))
        return 0

    lax.fori_loop(1, 16, send_w, 0, unroll=True)

    def send_wo(k, _):
        s = rem(sh + k, 16)
        push(wo2.at[rem(s, 2)], wobuf.at[sh], ssem.at[WO], rsem.at[WO], (dp, s))
        return 0

    lax.fori_loop(1, 16, send_wo, 0, unroll=True)

    for m in range(8):
        for i in range(2):
            mcsend[m, i : i + 1, :] = mc[i, m : m + 1, :]

    def send_mc(k, _):
        m = rem(t + k, 8)
        push(mcsend.at[m], mcbuf.at[t], ssem.at[MC], rsem.at[MC], tp_dev(m))
        return 0

    lax.fori_loop(1, 8, send_mc, 0, unroll=True)

    wbuf[sh] = wp[c]
    wobuf[sh] = wo2[c]
    mcbuf[t] = mcsend[t]
    xbuf[2 * t] = xn[0]
    xbuf[2 * t + 1] = xn[1]

    table[...] = jnp.zeros_like(table)
    table[:, : 2 * CROP - 1] = bias[...]
    row = jnp.broadcast_to(table[pl.ds(t, 1), :], (CROP, 2 * CROP))
    shifted = pltpu.roll(row, CROP + 1, 1, stride=1, stride_axis=0)
    band[...] = shifted[:, :CROP].T

    lane16 = lax.broadcasted_iota(jnp.int32, (16, 256), 1)
    sub16 = lax.broadcasted_iota(jnp.int32, (16, 256), 0)
    pair = jnp.broadcast_to(pairing[...], (16, 256))
    swapped = jnp.where(lane16 % 2 == 0, pltpu.roll(pair, 255, 1), pltpu.roll(pair, 1, 1))
    hot_a = (pair == item_of(sub16 + p * 16)).astype(f32).astype(bf16)
    rows256 = lax.broadcasted_iota(jnp.int32, (256, 256), 0)
    hot_b = (jnp.broadcast_to(swapped[:1], (256, 256)) == item_of(rows256)).astype(f32).astype(bf16)
    target[...] = dot(hot_a, hot_b, NT)

    def wait_item(slot):
        await_bytes(xbuf.at[slot], xrsem.at[slot])

    wait_item(2 * left)
    send_item(xbuf.at[2 * left], 2 * left, right)
    send_item(xbuf.at[2 * left], 2 * left, sib)
    wait_item(2 * right + 1)
    send_item(xbuf.at[2 * right + 1], 2 * right + 1, left)
    send_item(xbuf.at[2 * right + 1], 2 * right + 1, sib)
    wait_item(2 * sib)
    wait_item(2 * sib + 1)
    await_bytes(wbuf.at[pl.ds(0, 15)], rsem.at[W])

    half_mask = (
        lax.broadcasted_iota(jnp.int32, (16, 256), 0)
        == lax.broadcasted_iota(jnp.int32, (16, 256), 1) // 128
    )

    def forward(m):
        rows = xbuf[pl.ds(2 * m, 2)].reshape(2 * CROP, D)
        packed = dot(rows, wbuf[...].reshape(D, QKV)).astype(bf16)
        xt[:, pl.ds(pl.multiple_of(m * 256, 256), 256)] = rows.T
        qkvbuf[pl.ds(2 * m, 2)] = packed.reshape(2, CROP, QKV)
        mass = []
        for i in range(2):
            part = packed[i * CROP : (i + 1) * CROP]
            q, k, v = part[:, :128], part[:, 128:256], part[:, 256:]
            scores = dot(q, k, NT) * score_scale + band[...]
            raised = jnp.exp(scores - jnp.max(scores, axis=-1, keepdims=True))
            prob = raised / jnp.sum(raised, axis=-1, keepdims=True)
            probs[2 * m + i] = prob
            mixed = dot(prob.astype(bf16), v).astype(bf16).astype(f32)
            mmbuf[t, pl.ds(2 * m + i, 1), :] = jnp.sum(mixed, axis=0, keepdims=True)
            mass.append(jnp.sum(prob, axis=0, keepdims=True))
        both = jnp.where(half_mask, jnp.concatenate(mass, axis=1), 0.0).astype(bf16)
        weighed = dot(both, rows)
        for i in range(2):
            arows[pl.ds(2 * m + i, 1), :] = weighed[i : i + 1]

    def fwd_own(k, _):
        forward(t + k * other)
        return 0

    lax.fori_loop(0, 2, fwd_own, 0)

    wait_item(2 * left + 1)
    send_item(xbuf.at[2 * left + 1], 2 * left + 1, sib)
    wait_item(2 * right)
    send_item(xbuf.at[2 * right], 2 * right, sib)

    def fwd_near(k, _):
        member = rem(x + 3 + 2 * rem(k, 2), 4) * 2 + c + div(k, 2) * other

        @pl.when(k >= 2)
        def _():
            wait_item(2 * member)
            wait_item(2 * member + 1)

        forward(member)
        return 0

    lax.fori_loop(0, 4, fwd_near, 0)

    wait_item(2 * far)
    send_item(xbuf.at[2 * far], 2 * far, sib)
    wait_item(2 * far + 1)
    send_item(xbuf.at[2 * far + 1], 2 * far + 1, sib)

    def fwd_far(k, _):
        member = far + k * other

        @pl.when(k >= 1)
        def _():
            wait_item(2 * member)
            wait_item(2 * member + 1)

        forward(member)
        return 0

    lax.fori_loop(0, 2, fwd_far, 0)

    def send_mm(k, _):
        push(mmbuf.at[t], mmbuf.at[t], ssem.at[MM], rsem.at[MM], tp_dev(rem(t + k, 8)))
        return 0

    lax.fori_loop(1, 8, send_mm, 0, unroll=True)
    await_bytes(wobuf.at[pl.ds(0, 15)], rsem.at[WO])
    await_bytes(mcbuf.at[pl.ds(0, 7)], rsem.at[MC])
    await_bytes(mmbuf.at[pl.ds(0, 7)], rsem.at[MM])

    wo_slice = wobuf[...].reshape(INNER, SLICE)
    summed = jnp.concatenate([mmbuf[h] for h in range(8)], axis=1)
    product = dot(jnp.concatenate(split(summed), axis=0), wo_slice)
    means = jnp.concatenate([mcbuf[m] for m in range(8)], axis=0)
    pooled = means + (product[:16] + product[16:]) * (1.0 / CROP)
    pobuf[p] = pooled

    def send_po(k, _):
        q = rem(p + k, 16)
        push(pobuf.at[p], pobuf.at[p], ssem.at[PO], rsem.at[PO], plane_dev(q))
        return 0

    lax.fori_loop(1, 16, send_po, 0, unroll=True)

    own = (lane16 == sub16 + p * 16).astype(f32)
    for s in range(16):
        q = (s % 2) * 8 + s // 2
        easend[q, :, :128] = arows[:, s * 128 : (s + 1) * 128].astype(bf16)
        easend[q, :, 128:] = mmbuf[s // 2].astype(bf16)
    eabuf[p] = easend[p]

    def send_ea(k, _):
        q = rem(p + k, 16)
        push(easend.at[q], eabuf.at[p], ssem.at[EA], rsem.at[EA], plane_dev(q))
        return 0

    lax.fori_loop(1, 16, send_ea, 0, unroll=True)
    await_bytes(pobuf.at[pl.ds(0, 15)], rsem.at[PO])
    everyone = pobuf[...].reshape(256, SLICE)
    parts = split(everyone)
    grbuf[t] = dot3(pooled, parts, NT)
    squares = jnp.concatenate(split(everyone * everyone), axis=1)
    ssbuf[t] = dot(jnp.ones((8, 2 * SLICE), bf16), squares, NT)[:1]

    def send_gr(k, _):
        dev = tp_dev(rem(t + k, 8))
        push(grbuf.at[t], grbuf.at[t], ssem.at[GR], rsem.at[GR], dev)
        push(ssbuf.at[t], ssbuf.at[t], ssem.at[SS], rsem.at[SS], dev)
        return 0

    lax.fori_loop(1, 8, send_gr, 0, unroll=True)
    await_bytes(grbuf.at[pl.ds(0, 7)], rsem.at[GR])
    await_bytes(ssbuf.at[pl.ds(0, 7)], rsem.at[SS])
    gram = grbuf[0]
    for m in range(1, 8):
        gram = gram + grbuf[m]
    inv_row = lax.rsqrt(jnp.sum(ssbuf[...], axis=0) + embed_eps)
    inv_col = jnp.sum(own * inv_row, axis=1, keepdims=True)
    sims = gram * inv_col * inv_row * inv_tau
    exponents = jnp.where(own > 0.5, 0.0, jnp.exp(sims - inv_tau))
    totals = jnp.sum(exponents, axis=1, keepdims=True)
    tobuf[p] = jnp.sum(own * totals, axis=0, keepdims=True)

    def send_to(k, _):
        q = rem(p + k, 16)
        push(tobuf.at[p], tobuf.at[p], ssem.at[TO], rsem.at[TO], plane_dev(q))
        return 0

    lax.fori_loop(1, 16, send_to, 0, unroll=True)
    losses = jnp.log(totals) + inv_tau - jnp.sum(sims * target[...], axis=1, keepdims=True)
    loss_out[...] = jnp.broadcast_to(losses, (16, 128))
    await_bytes(tobuf.at[pl.ds(0, 15)], rsem.at[TO])
    column_totals = jnp.sum(tobuf[...], axis=0)
    weights = exponents / totals + exponents / column_totals - 2.0 * target[...]
    grad_embedding = dot3(weights * inv_row, parts) * inv_tau
    along = jnp.sum(weights * sims, axis=1, keepdims=True)
    grad_pooled = (grad_embedding - pooled * inv_col * along) * inv_col
    grad_frame = (grad_pooled * (1.0 / CROP)).astype(bf16)
    partial = dot(grad_frame, wo_slice, NT)
    for h in range(8):
        gmsend[h] = partial[:, h * 128 : (h + 1) * 128]
    labuf[p, :, :SLICE] = grad_frame

    def send_gm(k, _):
        m = rem(t + k, 8)
        push(gmsend.at[m], gmbuf.at[t], ssem.at[GM], rsem.at[GM], tp_dev(m))
        return 0

    lax.fori_loop(1, 8, send_gm, 0, unroll=True)
    gmbuf[t] = gmsend[t]

    await_bytes(gmbuf.at[pl.ds(0, 7)], rsem.at[GM])
    gm = gmbuf[0]
    for m in range(1, 8):
        gm = gm + gmbuf[m]
    grad_mixed = gm.astype(bf16)
    labuf[p, :, SLICE:] = grad_mixed
    sub_item = lax.broadcasted_iota(jnp.int32, (16, 128), 0)

    def backward(step, _):
        for i in range(8):
            b = step * 8 + i
            part = qkvbuf[b]
            q, k, v = part[:, :128], part[:, 128:256], part[:, 256:]
            prob = probs[b]
            all_rows = dot(grad_mixed, v, NT)
            g_row = jnp.sum(jnp.where(sub_item == b, all_rows, 0.0), axis=0, keepdims=True)
            centred = g_row - jnp.sum(prob * g_row, axis=-1, keepdims=True)
            dscores = (prob * centred * score_scale).astype(bf16)
            grad_q = dot(dscores, k)
            grad_k = dot(dscores, q, TN)
            gp[b] = jnp.concatenate([grad_q, grad_k], axis=1).astype(bf16)

        def send_la(j, _):
            q = rem(p + j, 16)
            push(labuf.at[p], labuf.at[p], ssem.at[LA], rsem.at[LA], plane_dev(q))
            return 0

        lax.fori_loop(1 + 8 * step, 9 + 7 * step, send_la, 0)
        return 0

    lax.fori_loop(0, 2, backward, 0)

    def scatter(k, _):
        z2 = rem(z + k, 4)
        for yl2 in range(2):
            rows = pl.ds(pl.multiple_of((yl2 * 4 + z2) * 256, 256), 256)
            value = dot(xt[rows, :], gp[...].reshape(16 * CROP, 256)).astype(bf16)
            for half in range(2):
                y2 = half * 2 + yl2
                block = value[half * 128 : (half + 1) * 128]
                zsend[z2, y2, :128] = block[:, :128]
                zsend[z2, y2, 128:] = block[:16, 128:]
                ysend[y2, z2] = block[16:, 128:]

                @pl.when(y2 != y)
                def _():
                    push(ysend.at[y2, z2], yrecv.at[y, z2], ssem.at[RY], rsem.at[RY], at(y2, z))

        @pl.when(z2 != z)
        def _():
            push(zsend.at[z2], zrecv.at[z], ssem.at[RZ], rsem.at[RZ], at(y, z2))

        return 0

    lax.fori_loop(1, 5, scatter, 0)
    zrecv[z] = zsend[z]
    yrecv[y] = ysend[y]

    def add_up(ref, *index):
        total = ref[(0, *index)].astype(f32)
        for q in range(1, 4):
            total = total + ref[(q, *index)].astype(f32)
        return total.astype(bf16)

    await_bytes(yrecv.at[pl.ds(0, 3)], rsem.at[RY])
    for i in range(4):
        ymid[i] = add_up(yrecv, i)
    for j in range(1, 4):
        z2 = rem(z + j, 4)
        push(ymid.at[z2], krecv.at[z], ssem.at[BK], rsem.at[BK], at(y, z2))
    krecv[z] = ymid[z]

    await_bytes(eabuf.at[pl.ds(0, 15)], rsem.at[EA])
    await_bytes(labuf.at[pl.ds(0, 15)], rsem.at[LA])
    early = eabuf[...].reshape(256, 256)
    late = labuf[...].reshape(256, SLICE + 128)
    o_tmp[...] = dot(early[:, 128:], late[:, :SLICE], TN)
    s_fin[2] = dot(early[:, :128], late[:, SLICE:], TN).astype(bf16)
    o_fin[...] = o_tmp[pl.ds(pl.multiple_of(yh * 64, 64), 64), :].astype(bf16)

    s_cols = pl.ds(pl.multiple_of(t * 128, 128), 128)
    o_cols = pl.ds(pl.multiple_of(t * SLICE, SLICE), SLICE)

    def each_target(fn):
        for k in range(1, 8):
            fn(rem(dp + k, 8))

        @pl.when(c != yh)
        def _():
            fn(dp)

    def send_early(j):
        dev = (j, base + yh)
        push(s_fin.at[2], s_out.at[2, :, s_cols], f_send.at[2], f_recv.at[2], dev)
        push(o_fin, o_out.at[:, o_cols], f_send.at[3], f_recv.at[3], dev)

    each_target(send_early)

    await_bytes(zrecv.at[pl.ds(0, 3)], rsem.at[RZ])
    for i in range(4):
        zmid[i] = add_up(zrecv, i)
    for j in range(1, 4):
        y2 = rem(y + j, 4)
        push(zmid.at[y2], qrecv.at[y], ssem.at[BQ], rsem.at[BQ], at(y2, z))
    qrecv[y] = zmid[y]

    def send_part(i, rows, sem):
        def send(j):
            push(
                s_fin.at[i, rows], s_out.at[i, rows, s_cols], f_send.at[sem], f_recv.at[sem],
                (j, base + yh),
            )

        each_target(send)

    all_rows, first_half, last_half = pl.ds(0, 128), pl.ds(0, 16), pl.ds(16, 112)
    await_bytes(krecv.at[pl.ds(0, 3)], rsem.at[BK])
    s_fin[1, 16:] = add_up(krecv)
    send_part(1, last_half, 4)
    await_bytes(qrecv.at[pl.ds(0, 3)], rsem.at[BQ])
    added = add_up(qrecv)
    s_fin[0] = added[:128]
    s_fin[1, :16] = added[128:]
    send_part(0, all_rows, 0)
    send_part(1, first_half, 1)

    @pl.when(c == yh)
    def _():
        s_out[:, :, s_cols] = s_fin[...]
        o_out[:, o_cols] = o_fin[...]

    def await_all(sems):
        def await_parts(members):
            cols = pl.ds(0, members * 128)
            await_bytes(s_out.at[0, :, cols], sems.at[0])
            await_bytes(s_out.at[1, first_half, cols], sems.at[1])
            await_bytes(s_out.at[2, :, cols], sems.at[2])
            await_bytes(o_out.at[:, pl.ds(0, members * SLICE)], sems.at[3])
            await_bytes(s_out.at[1, last_half, cols], sems.at[4])

        @pl.when(c == yh)
        def _():
            await_parts(7)

        @pl.when(c != yh)
        def _():
            await_parts(8)

    await_all(f_recv)
    await_all(f_send)
    await_bytes(xbuf.at[pl.ds(0, 14)], xssem)
    for sem, ref in (
        (W, wbuf), (WO, wobuf), (EA, eabuf), (PO, pobuf), (TO, tobuf), (LA, labuf),
    ):
        await_bytes(ref.at[pl.ds(0, 15)], ssem.at[sem])
    for sem, ref in ((RZ, zrecv), (RY, yrecv), (BQ, qrecv), (BK, krecv)):
        await_bytes(ref.at[pl.ds(0, 3)], ssem.at[sem])
    for sem, ref in ((MC, mcbuf), (MM, mmbuf), (GR, grbuf), (SS, ssbuf), (GM, gmbuf)):
        await_bytes(ref.at[pl.ds(0, 7)], ssem.at[sem])


def norm_kernel(starts, frames, xn, mc, raw, sems):
    begin = [starts[i] for i in range(2)]
    base = [(b // 16) * 16 for b in begin]
    base = [jnp.minimum(b, CROP - 16) for b in base]
    loads = [
        pltpu.make_async_copy(
            frames.at[i, pl.ds(pl.multiple_of(base[i], 16), CROP + 16)], raw.at[i], sems.at[i]
        )
        for i in range(2)
    ]
    for load in loads:
        load.start()
    for i in range(2):
        loads[i].wait()
        odd = begin[i] - base[i]

        def chunk(r, total):
            near = raw[i, pl.ds(pl.multiple_of(r * 16, 16), 32), :].astype(f32)
            rows = pltpu.roll(near, (32 - odd) % 32, 0)[:16]
            centred = rows - jnp.mean(rows, axis=-1, keepdims=True)
            scale = lax.rsqrt(jnp.mean(centred * centred, axis=-1, keepdims=True) + norm_eps)
            xn[i, pl.ds(pl.multiple_of(r * 16, 16), 16), :] = (centred * scale).astype(bf16)
            return total + rows[:8] + rows[8:]

        total = lax.fori_loop(0, CROP // 16, chunk, jnp.zeros((8, D), f32), unroll=4)
        mean = jnp.sum(total, axis=0, keepdims=True) * (1.0 / CROP)
        for m in range(8):
            mc[i, m : m + 1, :] = mean[:, m * SLICE : (m + 1) * SLICE]


def run_norm(frames, starts):
    vmem = pl.BlockSpec(memory_space=pltpu.VMEM)
    return pl.pallas_call(
        norm_kernel,
        out_shape=(
            jax.ShapeDtypeStruct((2, CROP, D), bf16),
            jax.ShapeDtypeStruct((2, 8, SLICE), f32),
        ),
        in_specs=[
            pl.BlockSpec(memory_space=pltpu.SMEM), pl.BlockSpec(memory_space=pltpu.HBM),
        ],
        out_specs=(vmem, vmem),
        scratch_shapes=[
            pltpu.VMEM((2, CROP + 16, D), bf16),
            pltpu.SemaphoreType.DMA((2,)),
        ],
        compiler_params=pltpu.CompilerParams(vmem_limit_bytes=24 * 1024 * 1024),
        name="norm",
    )(starts, frames)


def run_kernel(*args):
    vmem = pl.BlockSpec(memory_space=pltpu.VMEM)
    hbm = pl.BlockSpec(memory_space=pltpu.HBM)
    return pl.pallas_call(
        kernel,
        out_shape=(
            jax.ShapeDtypeStruct((16, 128), f32),
            jax.ShapeDtypeStruct((3, 128, INNER), bf16),
            jax.ShapeDtypeStruct((64, D), bf16),
        ),
        in_specs=[vmem, vmem, vmem, vmem, hbm, hbm, vmem],
        out_specs=(vmem, vmem, vmem),
        scratch_shapes=[
            pltpu.VMEM((3, 128, 256), f32),
            pltpu.VMEM((64, 512), f32),
            pltpu.VMEM((2, 128, QKV), bf16),
            pltpu.VMEM((2, 64, SLICE), bf16),
            pltpu.VMEM((8, 2, SLICE), f32),
            pltpu.VMEM((16, 256), f32),
            pltpu.VMEM((16, CROP, D), bf16),
            pltpu.VMEM((D, 16 * CROP), bf16),
            pltpu.VMEM((16, 128, QKV), bf16),
            pltpu.VMEM((16, 64, SLICE), bf16),
            pltpu.VMEM((8, 2, SLICE), f32),
            pltpu.VMEM((16, CROP, QKV), bf16),
            pltpu.VMEM((16, CROP, CROP), f32),
            pltpu.VMEM((16, D), f32),
            pltpu.VMEM((8, 16, 128), f32),
            pltpu.VMEM((16, 16, 256), bf16),
            pltpu.VMEM((16, 16, 256), bf16),
            pltpu.VMEM((16, 16, SLICE), f32),
            pltpu.VMEM((8, 16, 256), f32),
            pltpu.VMEM((8, 1, 256), f32),
            pltpu.VMEM((16, 1, 256), f32),
            pltpu.VMEM((16, 16, SLICE + 128), bf16),
            pltpu.VMEM((8, 16, 128), f32),
            pltpu.VMEM((8, 16, 128), f32),
            pltpu.VMEM((16, CROP, 256), bf16),
            pltpu.VMEM((4, 4, 144, 128), bf16),
            pltpu.VMEM((4, 4, 112, 128), bf16),
            pltpu.VMEM((4, 4, 144, 128), bf16),
            pltpu.VMEM((4, 4, 112, 128), bf16),
            pltpu.VMEM((4, 144, 128), bf16),
            pltpu.VMEM((4, 112, 128), bf16),
            pltpu.VMEM((4, 144, 128), bf16),
            pltpu.VMEM((4, 112, 128), bf16),
            pltpu.VMEM((3, 128, 128), bf16),
            pltpu.VMEM((128, SLICE), f32),
            pltpu.VMEM((64, SLICE), bf16),
            pltpu.VMEM((CROP, CROP), f32),
            pltpu.VMEM((HEADS, 2 * CROP), f32),
            pltpu.SemaphoreType.DMA((4,)),
            pltpu.SemaphoreType.DMA((15,)),
            pltpu.SemaphoreType.DMA((15,)),
            pltpu.SemaphoreType.DMA,
            pltpu.SemaphoreType.DMA((16,)),
        ]
        + [pltpu.SemaphoreType.DMA((5,))] * 2,
        compiler_params=pltpu.CompilerParams(
            collective_id=0, has_side_effects=True, vmem_limit_bytes=40 * 1024 * 1024
        ),
        cost_estimate=pl.CostEstimate(
            flops=15_000_000_000, bytes_accessed=300_000_000, transcendentals=300_000
        ),
        name="encoder",
    )(*args)


STEPS = 4


def adam_kernel(
    share, o_grad, losses, gain, gain_m, gain_s, in_w, in_m, in_s, out_w, out_m, out_s,
    pair_losses, new_in_w, new_in_m, new_in_s, new_out_w, new_out_m, new_out_s, new_gw, new_gm, new_gs,
    column, in_new, out_new, isems, osems,
):
    t = 2 * (lax.axis_index("dp") // 2) + lax.axis_index("shard") % 2
    item = lax.broadcasted_iota(jnp.int32, (16, 128), 0)
    lane = lax.broadcasted_iota(jnp.int32, (16, 128), 1)
    for i in range(2):
        mine = jnp.logical_and(item == 2 * t + i, lane == 0)
        pair_losses[i] = jnp.sum(jnp.where(mine, losses[...], 0.0))
    square = lax.broadcasted_iota(jnp.int32, (128, 128), 0) == lax.broadcasted_iota(
        jnp.int32, (128, 128), 1
    )
    gain_row = gain[...].astype(bf16).astype(f32)
    column[...] = jnp.broadcast_to(
        jnp.sum(jnp.where(square, gain_row, 0.0), axis=1, keepdims=True), (128, 128)
    )
    rows = 128 // STEPS
    stores = []
    for step in range(STEPS):
        at_rows = pl.ds(step * rows, rows)
        gain_col = column[at_rows, :][:, :1]

        def part(j, total):
            i, cols = j // 2, pl.ds(pl.multiple_of(j * 512, 512), 512)
            inner = pl.ds(pl.multiple_of((j % 2) * 512, 512), 512)
            master = in_w[at_rows, cols]
            piece = share[i, at_rows, inner].astype(f32)
            new = adam_update(
                master, in_m[at_rows, cols], in_s[at_rows, cols], piece * gain_col, weight_decay
            )
            for n in range(3):
                in_new[n, at_rows, cols] = new[n]
            terms = piece * master.astype(bf16).astype(f32)
            return total + sum(terms[:, n * 128 : (n + 1) * 128] for n in range(4))

        total = lax.fori_loop(0, 6, part, jnp.zeros((rows, 128), f32), unroll=2)
        column[at_rows, :] = jnp.broadcast_to(jnp.sum(total, axis=1, keepdims=True), (rows, 128))
        for n, ref in enumerate((new_in_w, new_in_m, new_in_s)):
            stores.append(
                pltpu.make_async_copy(in_new.at[n, at_rows], ref.at[at_rows], isems.at[n, step])
            )
            stores[-1].start()
    for step in range(2):
        at_rows = pl.ds(step * 32, 32)

        def out_part(j, _):
            cols = pl.ds(pl.multiple_of(j * 512, 512), 512)
            new = adam_update(
                out_w[at_rows, cols], out_m[at_rows, cols], out_s[at_rows, cols],
                o_grad[at_rows, cols].astype(f32), weight_decay,
            )
            for n in range(3):
                out_new[n, at_rows, cols] = new[n]
            return 0

        lax.fori_loop(0, 4, out_part, 0, unroll=2)
        for n, ref in enumerate((new_out_w, new_out_m, new_out_s)):
            stores.append(
                pltpu.make_async_copy(out_new.at[n, at_rows], ref.at[at_rows], osems.at[n, step])
            )
            stores[-1].start()
    grad = jnp.sum(jnp.where(square, column[...], 0.0), axis=0, keepdims=True)
    new_gw[...], new_gm[...], new_gs[...] = adam_update(
        gain[...], gain_m[...], gain_s[...], grad, 0.0
    )
    for store in stores:
        store.wait()


def run_adam(share, o_grad, losses, gains, inputs, outputs):
    vmem = pl.BlockSpec(memory_space=pltpu.VMEM)
    hbm = pl.BlockSpec(memory_space=pltpu.HBM)
    return pl.pallas_call(
        adam_kernel,
        out_shape=[jax.ShapeDtypeStruct((2,), f32)]
        + [jax.ShapeDtypeStruct((128, 3 * INNER), f32)] * 3
        + [jax.ShapeDtypeStruct((64, D), f32)] * 3
        + [jax.ShapeDtypeStruct((1, 128), f32)] * 3,
        in_specs=[vmem] * 12,
        out_specs=[pl.BlockSpec(memory_space=pltpu.SMEM)] + [hbm] * 6 + [vmem] * 3,
        scratch_shapes=[
            pltpu.VMEM((128, 128), f32),
            pltpu.VMEM((3, 128, 3 * INNER), f32),
            pltpu.VMEM((3, 64, D), f32),
            pltpu.SemaphoreType.DMA((3, STEPS)),
            pltpu.SemaphoreType.DMA((3, 2)),
        ],
        compiler_params=pltpu.CompilerParams(vmem_limit_bytes=24 * 1024 * 1024),
        name="adam",
    )(share, o_grad, losses, *gains, *inputs, *outputs)


def per_device(
    frames, crop_starts, pairing, bias_table,
    input_master, input_moment, input_square,
    output_master, output_moment, output_square,
    gain_master, gain_moment, gain_square,
):
    gains = [g.reshape(1, 128) for g in (gain_master, gain_moment, gain_square)]
    losses, s_grad, o_grad = run_kernel(
        *run_norm(frames, crop_starts), pairing.reshape(1, 256), bias_table,
        input_master, output_master, gains[0],
    )
    new = run_adam(
        s_grad, o_grad, losses, gains,
        (input_master, input_moment, input_square),
        (output_master, output_moment, output_square),
    )
    return (*new[:7], *(g.reshape(128) for g in new[7:]))


def solution(mesh):
    one = P("shard")
    two = P("shard", None)
    items = P(("dp", "shard"))
    in_specs = (P(("dp", "shard"), None, None), items, P(), P()) + (two,) * 6 + (one,) * 3
    out_specs = (items,) + (two,) * 6 + (one,) * 3
    return jax.shard_map(
        per_device, mesh=mesh, in_specs=in_specs, out_specs=out_specs, check_vma=False
    )
```

```python
import functools

import jax
import jax.numpy as jnp
from jax import lax
from jax.experimental import pallas as pl
from jax.experimental.pallas import tpu as pltpu
from jax.sharding import PartitionSpec as P

D = 2048
HEADS = 8
HEAD_DIM = 128
INNER = 1024
CROP = 128
QKV = 3 * HEAD_DIM
SLICE = D // 8

inv_tau = 20.0
norm_eps = 1e-05
embed_eps = 1e-06
beta_one = 0.9
beta_two = 0.999
adam_eps = 1e-08
learn_rate = 0.002
weight_decay = 0.1
adam_step = 1000
score_scale = HEAD_DIM ** (-0.5)

f32 = jnp.float32
bf16 = jnp.bfloat16
NT = (((1,), (1,)), ((), ()))
TN = (((0,), (0,)), ((), ()))


def dot(a, b, dims=(((1,), (0,)), ((), ()))):
    return lax.dot_general(a, b, dims, preferred_element_type=f32)


def split(a):
    high = a.astype(bf16)
    return high, (a - high.astype(f32)).astype(bf16)


def dot3(a, b, dims=(((1,), (0,)), ((), ()))):
    rows = a.shape[0]
    high, low = split(a)
    both = dot(jnp.concatenate([high, low], axis=0), b[0], dims)
    return both[:rows] + both[rows:] + dot(high, b[1], dims)


def adam_update(master, moment, square, gradient, decay):
    moment_new = beta_one * moment + (1.0 - beta_one) * gradient
    square_new = beta_two * square + (1.0 - beta_two) * gradient * gradient
    mean_scale = learn_rate / (1.0 - beta_one**adam_step)
    square_scale = 1.0 / (1.0 - beta_two**adam_step)
    step = moment_new * mean_scale / (jnp.sqrt(square_new * square_scale) + adam_eps)
    return (master * (1.0 - learn_rate * decay) - step, moment_new, square_new)


W, WO, MC, MM, EA, PO, GR, TO, LA, GM, RZ, RY, BQ, BK, SS = range(15)


def div(a, b):
    return lax.div(a, jnp.int32(b))


def rem(a, b):
    return lax.rem(a, jnp.int32(b))


def item_of(row):
    t, p = (row // 2) % 8, row // 16
    return 2 * (
        ((t // 2) * 2 + p // 8) * 16 + ((p // 4) % 2) * 8 + (p % 4) * 2 + t % 2
    ) + row % 2


def kernel(
    xn, mc, pairing, bias, input_master, output_master, gain,
    loss_out, s_out, o_out,
    wraw, woraw, wp, wo2, mcsend, target,
    xbuf, xt, wbuf, wobuf, mcbuf, qkvbuf, probs, arows, mmbuf, eabuf, easend, pobuf, grbuf, ssbuf,
    tobuf, labuf, gmsend, gmbuf, gp, zsend, ysend, zrecv, yrecv, zmid, ymid, qrecv, krecv, s_fin, o_tmp, o_fin, band, table,
    lsem, ssem, rsem, xssem, xrsem, f_send, f_recv,
):
    dp = lax.axis_index("dp")
    sh = lax.axis_index("shard")
    x, yh = div(dp, 2), rem(dp, 2)
    yl, z, c = div(sh, 8), rem(div(sh, 2), 4), rem(sh, 2)
    base = yl * 8 + z * 2
    t = 2 * x + c
    p = yh * 8 + yl * 4 + z
    y = yh * 2 + yl

    def tp_dev(m):
        return (div(m, 2) * 2 + yh, base + rem(m, 2))

    def plane_dev(q):
        return (x * 2 + div(q, 8), rem(div(q, 4), 2) * 8 + rem(q, 4) * 2 + c)

    def at(y2, z2):
        y2 = jnp.int32(y2)
        return (x * 2 + div(y2, 2), rem(y2, 2) * 8 + z2 * 2 + c)

    def push(src, dst, send, recv, dev):
        pltpu.make_async_remote_copy(
            src_ref=src, dst_ref=dst, send_sem=send, recv_sem=recv,
            device_id=dev, device_id_type=pl.DeviceIdType.MESH,
        ).start()

    def await_bytes(ref, sem):
        pltpu.make_async_copy(ref, ref, sem).wait()

    loads = []
    for i in range(3):
        cols = pl.ds(pl.multiple_of(i * INNER + x * 256, 256), 256)
        loads.append(
            pltpu.make_async_copy(input_master.at[:, cols], wraw.at[i], lsem.at[i])
        )
    loads.append(
        pltpu.make_async_copy(
            output_master.at[:, pl.ds(pl.multiple_of(x * 512, 512), 512)], woraw, lsem.at[3]
        )
    )
    for load in loads:
        load.start()

    barrier = pltpu.get_barrier_semaphore()

    def greet(dev):
        pl.semaphore_signal(barrier, inc=1, device_id=dev, device_id_type=pl.DeviceIdType.MESH)

    for k in range(1, 16):
        greet((dp, rem(sh + k, 16)))
    for k in range(8):
        greet((x * 2 + 1 - yh, div(jnp.int32(k), 4) * 8 + (k % 4) * 2 + c))
    for k in range(1, 8):
        j = rem(dp + k, 8)
        greet((j, base + 1 - c))
        if k % 2 == 0:
            greet((j, base + c))
        else:
            @pl.when(div(j, 2) != x)
            def _():
                greet((j, base + c))

    right = rem(x + 1, 4) * 2 + c
    left = rem(x + 3, 4) * 2 + c
    far = rem(x + 2, 4) * 2 + c
    sib = x * 2 + 1 - c
    other = 1 - 2 * c

    def send_item(src, slot, member):
        push(src, xbuf.at[slot], xssem, xrsem.at[slot], tp_dev(member))

    pl.semaphore_wait(barrier, 36)
    send_item(xn.at[0], 2 * t, right)
    send_item(xn.at[1], 2 * t + 1, left)
    send_item(xn.at[0], 2 * t, sib)
    send_item(xn.at[1], 2 * t + 1, sib)
    send_item(xn.at[1], 2 * t + 1, right)
    send_item(xn.at[0], 2 * t, left)

    for load in loads:
        load.wait()
    square = lax.broadcasted_iota(jnp.int32, (128, 128), 0) == lax.broadcasted_iota(
        jnp.int32, (128, 128), 1
    )
    gain_row = gain[...].astype(bf16).astype(f32)
    gain_col = jnp.sum(jnp.where(square, gain_row, 0.0), axis=1, keepdims=True)
    for core in range(2):
        for i in range(3):
            piece = wraw[i, :, core * 128 : (core + 1) * 128].astype(bf16).astype(f32)
            wp[core, :, i * 128 : (i + 1) * 128] = (piece * gain_col).astype(bf16)
        wo2[core] = woraw[:, core * SLICE : (core + 1) * SLICE].astype(bf16)

    def send_w(k, _):
        s = rem(sh + k, 16)
        push(wp.at[rem(s, 2)], wbuf.at[sh], ssem.at[W], rsem.at[W], (dp, s))
        return 0

    lax.fori_loop(1, 16, send_w, 0, unroll=True)

    def send_wo(k, _):
        s = rem(sh + k, 16)
        push(wo2.at[rem(s, 2)], wobuf.at[sh], ssem.at[WO], rsem.at[WO], (dp, s))
        return 0

    lax.fori_loop(1, 16, send_wo, 0, unroll=True)

    for m in range(8):
        for i in range(2):
            mcsend[m, i : i + 1, :] = mc[i, m : m + 1, :]

    def send_mc(k, _):
        m = rem(t + k, 8)
        push(mcsend.at[m], mcbuf.at[t], ssem.at[MC], rsem.at[MC], tp_dev(m))
        return 0

    lax.fori_loop(1, 8, send_mc, 0, unroll=True)

    wbuf[sh] = wp[c]
    wobuf[sh] = wo2[c]
    mcbuf[t] = mcsend[t]
    xbuf[2 * t] = xn[0]
    xbuf[2 * t + 1] = xn[1]

    table[...] = jnp.zeros_like(table)
    table[:, : 2 * CROP - 1] = bias[...]
    row = jnp.broadcast_to(table[pl.ds(t, 1), :], (CROP, 2 * CROP))
    shifted = pltpu.roll(row, CROP + 1, 1, stride=1, stride_axis=0)
    band[...] = shifted[:, :CROP].T

    lane16 = lax.broadcasted_iota(jnp.int32, (16, 256), 1)
    sub16 = lax.broadcasted_iota(jnp.int32, (16, 256), 0)
    pair = jnp.broadcast_to(pairing[...], (16, 256))
    swapped = jnp.where(lane16 % 2 == 0, pltpu.roll(pair, 255, 1), pltpu.roll(pair, 1, 1))
    hot_a = (pair == item_of(sub16 + p * 16)).astype(f32).astype(bf16)
    rows256 = lax.broadcasted_iota(jnp.int32, (256, 256), 0)
    hot_b = (jnp.broadcast_to(swapped[:1], (256, 256)) == item_of(rows256)).astype(f32).astype(bf16)
    target[...] = dot(hot_a, hot_b, NT)

    def wait_item(slot):
        await_bytes(xbuf.at[slot], xrsem.at[slot])

    wait_item(2 * left)
    send_item(xbuf.at[2 * left], 2 * left, right)
    send_item(xbuf.at[2 * left], 2 * left, sib)
    wait_item(2 * right + 1)
    send_item(xbuf.at[2 * right + 1], 2 * right + 1, left)
    send_item(xbuf.at[2 * right + 1], 2 * right + 1, sib)
    wait_item(2 * sib)
    wait_item(2 * sib + 1)
    await_bytes(wbuf.at[pl.ds(0, 15)], rsem.at[W])

    half_mask = (
        lax.broadcasted_iota(jnp.int32, (16, 256), 0)
        == lax.broadcasted_iota(jnp.int32, (16, 256), 1) // 128
    )

    def forward(m):
        rows = xbuf[pl.ds(2 * m, 2)].reshape(2 * CROP, D)
        packed = dot(rows, wbuf[...].reshape(D, QKV)).astype(bf16)
        xt[:, pl.ds(pl.multiple_of(m * 256, 256), 256)] = rows.T
        qkvbuf[pl.ds(2 * m, 2)] = packed.reshape(2, CROP, QKV)
        mass = []
        for i in range(2):
            part = packed[i * CROP : (i + 1) * CROP]
            q, k, v = part[:, :128], part[:, 128:256], part[:, 256:]
            scores = dot(q, k, NT) * score_scale + band[...]
            raised = jnp.exp(scores - jnp.max(scores, axis=-1, keepdims=True))
            prob = raised / jnp.sum(raised, axis=-1, keepdims=True)
            probs[2 * m + i] = prob
            mixed = dot(prob.astype(bf16), v).astype(bf16).astype(f32)
            mmbuf[t, pl.ds(2 * m + i, 1), :] = jnp.sum(mixed, axis=0, keepdims=True)
            mass.append(jnp.sum(prob, axis=0, keepdims=True))
        both = jnp.where(half_mask, jnp.concatenate(mass, axis=1), 0.0).astype(bf16)
        weighed = dot(both, rows)
        for i in range(2):
            arows[pl.ds(2 * m + i, 1), :] = weighed[i : i + 1]

    def fwd_own(k, _):
        forward(t + k * other)
        return 0

    lax.fori_loop(0, 2, fwd_own, 0)

    wait_item(2 * left + 1)
    send_item(xbuf.at[2 * left + 1], 2 * left + 1, sib)
    wait_item(2 * right)
    send_item(xbuf.at[2 * right], 2 * right, sib)

    def fwd_near(k, _):
        member = rem(x + 3 + 2 * rem(k, 2), 4) * 2 + c + div(k, 2) * other

        @pl.when(k >= 2)
        def _():
            wait_item(2 * member)
            wait_item(2 * member + 1)

        forward(member)
        return 0

    lax.fori_loop(0, 4, fwd_near, 0)

    wait_item(2 * far)
    send_item(xbuf.at[2 * far], 2 * far, sib)
    wait_item(2 * far + 1)
    send_item(xbuf.at[2 * far + 1], 2 * far + 1, sib)

    def fwd_far(k, _):
        member = far + k * other

        @pl.when(k >= 1)
        def _():
            wait_item(2 * member)
            wait_item(2 * member + 1)

        forward(member)
        return 0

    lax.fori_loop(0, 2, fwd_far, 0)

    def send_mm(k, _):
        push(mmbuf.at[t], mmbuf.at[t], ssem.at[MM], rsem.at[MM], tp_dev(rem(t + k, 8)))
        return 0

    lax.fori_loop(1, 8, send_mm, 0, unroll=True)
    await_bytes(wobuf.at[pl.ds(0, 15)], rsem.at[WO])
    await_bytes(mcbuf.at[pl.ds(0, 7)], rsem.at[MC])
    await_bytes(mmbuf.at[pl.ds(0, 7)], rsem.at[MM])

    wo_slice = wobuf[...].reshape(INNER, SLICE)
    summed = jnp.concatenate([mmbuf[h] for h in range(8)], axis=1)
    product = dot(jnp.concatenate(split(summed), axis=0), wo_slice)
    means = jnp.concatenate([mcbuf[m] for m in range(8)], axis=0)
    pooled = means + (product[:16] + product[16:]) * (1.0 / CROP)
    pobuf[p] = pooled

    def send_po(k, _):
        q = rem(p + k, 16)
        push(pobuf.at[p], pobuf.at[p], ssem.at[PO], rsem.at[PO], plane_dev(q))
        return 0

    lax.fori_loop(1, 16, send_po, 0, unroll=True)

    own = (lane16 == sub16 + p * 16).astype(f32)
    for s in range(16):
        q = (s % 2) * 8 + s // 2
        easend[q, :, :128] = arows[:, s * 128 : (s + 1) * 128].astype(bf16)
        easend[q, :, 128:] = mmbuf[s // 2].astype(bf16)
    eabuf[p] = easend[p]

    def send_ea(k, _):
        q = rem(p + k, 16)
        push(easend.at[q], eabuf.at[p], ssem.at[EA], rsem.at[EA], plane_dev(q))
        return 0

    lax.fori_loop(1, 16, send_ea, 0, unroll=True)
    await_bytes(pobuf.at[pl.ds(0, 15)], rsem.at[PO])
    everyone = pobuf[...].reshape(256, SLICE)
    parts = split(everyone)
    grbuf[t] = dot3(pooled, parts, NT)
    squares = jnp.concatenate(split(everyone * everyone), axis=1)
    ssbuf[t] = dot(jnp.ones((8, 2 * SLICE), bf16), squares, NT)[:1]

    def send_gr(k, _):
        dev = tp_dev(rem(t + k, 8))
        push(grbuf.at[t], grbuf.at[t], ssem.at[GR], rsem.at[GR], dev)
        push(ssbuf.at[t], ssbuf.at[t], ssem.at[SS], rsem.at[SS], dev)
        return 0

    lax.fori_loop(1, 8, send_gr, 0, unroll=True)
    await_bytes(grbuf.at[pl.ds(0, 7)], rsem.at[GR])
    await_bytes(ssbuf.at[pl.ds(0, 7)], rsem.at[SS])
    gram = grbuf[0]
    for m in range(1, 8):
        gram = gram + grbuf[m]
    inv_row = lax.rsqrt(jnp.sum(ssbuf[...], axis=0) + embed_eps)
    inv_col = jnp.sum(own * inv_row, axis=1, keepdims=True)
    sims = gram * inv_col * inv_row * inv_tau
    exponents = jnp.where(own > 0.5, 0.0, jnp.exp(sims - inv_tau))
    totals = jnp.sum(exponents, axis=1, keepdims=True)
    tobuf[p] = jnp.sum(own * totals, axis=0, keepdims=True)

    def send_to(k, _):
        q = rem(p + k, 16)
        push(tobuf.at[p], tobuf.at[p], ssem.at[TO], rsem.at[TO], plane_dev(q))
        return 0

    lax.fori_loop(1, 16, send_to, 0, unroll=True)
    losses = jnp.log(totals) + inv_tau - jnp.sum(sims * target[...], axis=1, keepdims=True)
    loss_out[...] = jnp.broadcast_to(losses, (16, 128))
    await_bytes(tobuf.at[pl.ds(0, 15)], rsem.at[TO])
    column_totals = jnp.sum(tobuf[...], axis=0)
    weights = exponents / totals + exponents / column_totals - 2.0 * target[...]
    grad_embedding = dot3(weights * inv_row, parts) * inv_tau
    along = jnp.sum(weights * sims, axis=1, keepdims=True)
    grad_pooled = (grad_embedding - pooled * inv_col * along) * inv_col
    grad_frame = (grad_pooled * (1.0 / CROP)).astype(bf16)
    partial = dot(grad_frame, wo_slice, NT)
    for h in range(8):
        gmsend[h] = partial[:, h * 128 : (h + 1) * 128]
    labuf[p, :, :SLICE] = grad_frame

    def send_gm(k, _):
        m = rem(t + k, 8)
        push(gmsend.at[m], gmbuf.at[t], ssem.at[GM], rsem.at[GM], tp_dev(m))
        return 0

    lax.fori_loop(1, 8, send_gm, 0, unroll=True)
    gmbuf[t] = gmsend[t]

    await_bytes(gmbuf.at[pl.ds(0, 7)], rsem.at[GM])
    gm = gmbuf[0]
    for m in range(1, 8):
        gm = gm + gmbuf[m]
    grad_mixed = gm.astype(bf16)
    labuf[p, :, SLICE:] = grad_mixed
    sub_item = lax.broadcasted_iota(jnp.int32, (16, 128), 0)

    def backward(step, _):
        for i in range(16):
            b = step * 16 + i
            part = qkvbuf[b]
            q, k, v = part[:, :128], part[:, 128:256], part[:, 256:]
            prob = probs[b]
            all_rows = dot(grad_mixed, v, NT)
            g_row = jnp.sum(jnp.where(sub_item == b, all_rows, 0.0), axis=0, keepdims=True)
            centred = g_row - jnp.sum(prob * g_row, axis=-1, keepdims=True)
            dscores = (prob * centred * score_scale).astype(bf16)
            grad_q = dot(dscores, k)
            grad_k = dot(dscores, q, TN)
            gp[b] = jnp.concatenate([grad_q, grad_k], axis=1).astype(bf16)

        def send_la(j, _):
            q = rem(p + j, 16)
            push(labuf.at[p], labuf.at[p], ssem.at[LA], rsem.at[LA], plane_dev(q))
            return 0

        lax.fori_loop(1, 16, send_la, 0)
        return 0

    lax.fori_loop(0, 1, backward, 0)

    def scatter(k, _):
        z2 = rem(z + k, 4)
        for yl2 in range(2):
            rows = pl.ds(pl.multiple_of((yl2 * 4 + z2) * 256, 256), 256)
            value = dot(xt[rows, :], gp[...].reshape(16 * CROP, 256)).astype(bf16)
            for half in range(2):
                y2 = half * 2 + yl2
                block = value[half * 128 : (half + 1) * 128]
                zsend[z2, y2, :128] = block[:, :128]
                zsend[z2, y2, 128:] = block[:16, 128:]
                ysend[y2, z2] = block[16:, 128:]

                @pl.when(y2 != y)
                def _():
                    push(ysend.at[y2, z2], yrecv.at[y, z2], ssem.at[RY], rsem.at[RY], at(y2, z))

        @pl.when(z2 != z)
        def _():
            push(zsend.at[z2], zrecv.at[z], ssem.at[RZ], rsem.at[RZ], at(y, z2))

        return 0

    lax.fori_loop(1, 5, scatter, 0)
    zrecv[z] = zsend[z]
    yrecv[y] = ysend[y]

    def add_up(ref, *index):
        total = ref[(0, *index)].astype(f32)
        for q in range(1, 4):
            total = total + ref[(q, *index)].astype(f32)
        return total.astype(bf16)

    await_bytes(yrecv.at[pl.ds(0, 3)], rsem.at[RY])
    for i in range(4):
        ymid[i] = add_up(yrecv, i)
    for j in range(1, 4):
        z2 = rem(z + j, 4)
        push(ymid.at[z2], krecv.at[z], ssem.at[BK], rsem.at[BK], at(y, z2))
    krecv[z] = ymid[z]

    await_bytes(eabuf.at[pl.ds(0, 15)], rsem.at[EA])
    await_bytes(labuf.at[pl.ds(0, 15)], rsem.at[LA])
    early = eabuf[...].reshape(256, 256)
    late = labuf[...].reshape(256, SLICE + 128)
    o_tmp[...] = dot(early[:, 128:], late[:, :SLICE], TN)
    s_fin[2] = dot(early[:, :128], late[:, SLICE:], TN).astype(bf16)
    o_fin[...] = o_tmp[pl.ds(pl.multiple_of(yh * 64, 64), 64), :].astype(bf16)

    s_cols = pl.ds(pl.multiple_of(t * 128, 128), 128)
    o_cols = pl.ds(pl.multiple_of(t * SLICE, SLICE), SLICE)

    def each_target(fn):
        for k in range(1, 8):
            fn(rem(dp + k, 8))

        @pl.when(c != yh)
        def _():
            fn(dp)

    def send_early(j):
        dev = (j, base + yh)
        push(s_fin.at[2], s_out.at[2, :, s_cols], f_send.at[2], f_recv.at[2], dev)
        push(o_fin, o_out.at[:, o_cols], f_send.at[3], f_recv.at[3], dev)

    each_target(send_early)

    await_bytes(zrecv.at[pl.ds(0, 3)], rsem.at[RZ])
    for i in range(4):
        zmid[i] = add_up(zrecv, i)
    for j in range(1, 4):
        y2 = rem(y + j, 4)
        push(zmid.at[y2], qrecv.at[y], ssem.at[BQ], rsem.at[BQ], at(y2, z))
    qrecv[y] = zmid[y]

    def send_part(i, rows, sem):
        def send(j):
            push(
                s_fin.at[i, rows], s_out.at[i, rows, s_cols], f_send.at[sem], f_recv.at[sem],
                (j, base + yh),
            )

        each_target(send)

    all_rows, first_half, last_half = pl.ds(0, 128), pl.ds(0, 16), pl.ds(16, 112)
    await_bytes(krecv.at[pl.ds(0, 3)], rsem.at[BK])
    s_fin[1, 16:] = add_up(krecv)
    send_part(1, last_half, 4)
    await_bytes(qrecv.at[pl.ds(0, 3)], rsem.at[BQ])
    added = add_up(qrecv)
    s_fin[0] = added[:128]
    s_fin[1, :16] = added[128:]
    send_part(0, all_rows, 0)
    send_part(1, first_half, 1)

    @pl.when(c == yh)
    def _():
        s_out[:, :, s_cols] = s_fin[...]
        o_out[:, o_cols] = o_fin[...]

    def await_all(sems):
        def await_parts(members):
            cols = pl.ds(0, members * 128)
            await_bytes(s_out.at[0, :, cols], sems.at[0])
            await_bytes(s_out.at[1, first_half, cols], sems.at[1])
            await_bytes(s_out.at[2, :, cols], sems.at[2])
            await_bytes(o_out.at[:, pl.ds(0, members * SLICE)], sems.at[3])
            await_bytes(s_out.at[1, last_half, cols], sems.at[4])

        @pl.when(c == yh)
        def _():
            await_parts(7)

        @pl.when(c != yh)
        def _():
            await_parts(8)

    await_all(f_recv)
    await_all(f_send)
    await_bytes(xbuf.at[pl.ds(0, 14)], xssem)
    for sem, ref in (
        (W, wbuf), (WO, wobuf), (EA, eabuf), (PO, pobuf), (TO, tobuf), (LA, labuf),
    ):
        await_bytes(ref.at[pl.ds(0, 15)], ssem.at[sem])
    for sem, ref in ((RZ, zrecv), (RY, yrecv), (BQ, qrecv), (BK, krecv)):
        await_bytes(ref.at[pl.ds(0, 3)], ssem.at[sem])
    for sem, ref in ((MC, mcbuf), (MM, mmbuf), (GR, grbuf), (SS, ssbuf), (GM, gmbuf)):
        await_bytes(ref.at[pl.ds(0, 7)], ssem.at[sem])


def norm_kernel(starts, frames, xn, mc, raw, sems):
    begin = [starts[i] for i in range(2)]
    base = [(b // 16) * 16 for b in begin]
    base = [jnp.minimum(b, CROP - 16) for b in base]
    loads = [
        pltpu.make_async_copy(
            frames.at[i, pl.ds(pl.multiple_of(base[i], 16), CROP + 16)], raw.at[i], sems.at[i]
        )
        for i in range(2)
    ]
    for load in loads:
        load.start()
    for i in range(2):
        loads[i].wait()
        odd = begin[i] - base[i]

        def chunk(r, total):
            near = raw[i, pl.ds(pl.multiple_of(r * 16, 16), 32), :].astype(f32)
            rows = pltpu.roll(near, (32 - odd) % 32, 0)[:16]
            centred = rows - jnp.mean(rows, axis=-1, keepdims=True)
            scale = lax.rsqrt(jnp.mean(centred * centred, axis=-1, keepdims=True) + norm_eps)
            xn[i, pl.ds(pl.multiple_of(r * 16, 16), 16), :] = (centred * scale).astype(bf16)
            return total + rows[:8] + rows[8:]

        total = lax.fori_loop(0, CROP // 16, chunk, jnp.zeros((8, D), f32), unroll=8)
        mean = jnp.sum(total, axis=0, keepdims=True) * (1.0 / CROP)
        for m in range(8):
            mc[i, m : m + 1, :] = mean[:, m * SLICE : (m + 1) * SLICE]


def run_norm(frames, starts):
    vmem = pl.BlockSpec(memory_space=pltpu.VMEM)
    return pl.pallas_call(
        norm_kernel,
        out_shape=(
            jax.ShapeDtypeStruct((2, CROP, D), bf16),
            jax.ShapeDtypeStruct((2, 8, SLICE), f32),
        ),
        in_specs=[
            pl.BlockSpec(memory_space=pltpu.SMEM), pl.BlockSpec(memory_space=pltpu.HBM),
        ],
        out_specs=(vmem, vmem),
        scratch_shapes=[
            pltpu.VMEM((2, CROP + 16, D), bf16),
            pltpu.SemaphoreType.DMA((2,)),
        ],
        compiler_params=pltpu.CompilerParams(vmem_limit_bytes=24 * 1024 * 1024),
        name="norm",
    )(starts, frames)


def run_kernel(*args):
    vmem = pl.BlockSpec(memory_space=pltpu.VMEM)
    hbm = pl.BlockSpec(memory_space=pltpu.HBM)
    return pl.pallas_call(
        kernel,
        out_shape=(
            jax.ShapeDtypeStruct((16, 128), f32),
            jax.ShapeDtypeStruct((3, 128, INNER), bf16),
            jax.ShapeDtypeStruct((64, D), bf16),
        ),
        in_specs=[vmem, vmem, vmem, vmem, hbm, hbm, vmem],
        out_specs=(vmem, vmem, vmem),
        scratch_shapes=[
            pltpu.VMEM((3, 128, 256), f32),
            pltpu.VMEM((64, 512), f32),
            pltpu.VMEM((2, 128, QKV), bf16),
            pltpu.VMEM((2, 64, SLICE), bf16),
            pltpu.VMEM((8, 2, SLICE), f32),
            pltpu.VMEM((16, 256), f32),
            pltpu.VMEM((16, CROP, D), bf16),
            pltpu.VMEM((D, 16 * CROP), bf16),
            pltpu.VMEM((16, 128, QKV), bf16),
            pltpu.VMEM((16, 64, SLICE), bf16),
            pltpu.VMEM((8, 2, SLICE), f32),
            pltpu.VMEM((16, CROP, QKV), bf16),
            pltpu.VMEM((16, CROP, CROP), f32),
            pltpu.VMEM((16, D), f32),
            pltpu.VMEM((8, 16, 128), f32),
            pltpu.VMEM((16, 16, 256), bf16),
            pltpu.VMEM((16, 16, 256), bf16),
            pltpu.VMEM((16, 16, SLICE), f32),
            pltpu.VMEM((8, 16, 256), f32),
            pltpu.VMEM((8, 1, 256), f32),
            pltpu.VMEM((16, 1, 256), f32),
            pltpu.VMEM((16, 16, SLICE + 128), bf16),
            pltpu.VMEM((8, 16, 128), f32),
            pltpu.VMEM((8, 16, 128), f32),
            pltpu.VMEM((16, CROP, 256), bf16),
            pltpu.VMEM((4, 4, 144, 128), bf16),
            pltpu.VMEM((4, 4, 112, 128), bf16),
            pltpu.VMEM((4, 4, 144, 128), bf16),
            pltpu.VMEM((4, 4, 112, 128), bf16),
            pltpu.VMEM((4, 144, 128), bf16),
            pltpu.VMEM((4, 112, 128), bf16),
            pltpu.VMEM((4, 144, 128), bf16),
            pltpu.VMEM((4, 112, 128), bf16),
            pltpu.VMEM((3, 128, 128), bf16),
            pltpu.VMEM((128, SLICE), f32),
            pltpu.VMEM((64, SLICE), bf16),
            pltpu.VMEM((CROP, CROP), f32),
            pltpu.VMEM((HEADS, 2 * CROP), f32),
            pltpu.SemaphoreType.DMA((4,)),
            pltpu.SemaphoreType.DMA((15,)),
            pltpu.SemaphoreType.DMA((15,)),
            pltpu.SemaphoreType.DMA,
            pltpu.SemaphoreType.DMA((16,)),
        ]
        + [pltpu.SemaphoreType.DMA((5,))] * 2,
        compiler_params=pltpu.CompilerParams(
            collective_id=0, has_side_effects=True, vmem_limit_bytes=40 * 1024 * 1024
        ),
        cost_estimate=pl.CostEstimate(
            flops=15_000_000_000, bytes_accessed=300_000_000, transcendentals=300_000
        ),
        name="encoder",
    )(*args)


STEPS = 8


def adam_kernel(
    share, o_grad, losses, gain, gain_m, gain_s, in_w, in_m, in_s, out_w, out_m, out_s,
    pair_losses, new_in_w, new_in_m, new_in_s, new_out_w, new_out_m, new_out_s, new_gw, new_gm, new_gs,
    column, in_new, out_new, isems, osems,
):
    t = 2 * (lax.axis_index("dp") // 2) + lax.axis_index("shard") % 2
    item = lax.broadcasted_iota(jnp.int32, (16, 128), 0)
    lane = lax.broadcasted_iota(jnp.int32, (16, 128), 1)
    for i in range(2):
        mine = jnp.logical_and(item == 2 * t + i, lane == 0)
        pair_losses[i] = jnp.sum(jnp.where(mine, losses[...], 0.0))
    square = lax.broadcasted_iota(jnp.int32, (128, 128), 0) == lax.broadcasted_iota(
        jnp.int32, (128, 128), 1
    )
    gain_row = gain[...].astype(bf16).astype(f32)
    column[...] = jnp.broadcast_to(
        jnp.sum(jnp.where(square, gain_row, 0.0), axis=1, keepdims=True), (128, 128)
    )
    rows = 128 // STEPS
    stores = []
    for step in range(STEPS):
        at_rows = pl.ds(step * rows, rows)
        gain_col = column[at_rows, :][:, :1]

        def part(j, total):
            i, cols = j, pl.ds(pl.multiple_of(j * 1024, 1024), 1024)
            inner = pl.ds(0, 1024)
            master = in_w[at_rows, cols]
            piece = share[i, at_rows, inner].astype(f32)
            new = adam_update(
                master, in_m[at_rows, cols], in_s[at_rows, cols], piece * gain_col, weight_decay
            )
            for n in range(3):
                in_new[n, at_rows, cols] = new[n]
            terms = piece * master.astype(bf16).astype(f32)
            return total + sum(terms[:, n * 128 : (n + 1) * 128] for n in range(8))

        total = lax.fori_loop(0, 3, part, jnp.zeros((rows, 128), f32), unroll=3)
        column[at_rows, :] = jnp.broadcast_to(jnp.sum(total, axis=1, keepdims=True), (rows, 128))
        for n, ref in enumerate((new_in_w, new_in_m, new_in_s)):
            stores.append(
                pltpu.make_async_copy(in_new.at[n, at_rows], ref.at[at_rows], isems.at[n, step])
            )
            stores[-1].start()
    for step in range(2):
        at_rows = pl.ds(step * 32, 32)

        def out_part(j, _):
            cols = pl.ds(pl.multiple_of(j * 512, 512), 512)
            new = adam_update(
                out_w[at_rows, cols], out_m[at_rows, cols], out_s[at_rows, cols],
                o_grad[at_rows, cols].astype(f32), weight_decay,
            )
            for n in range(3):
                out_new[n, at_rows, cols] = new[n]
            return 0

        lax.fori_loop(0, 4, out_part, 0, unroll=4)
        for n, ref in enumerate((new_out_w, new_out_m, new_out_s)):
            stores.append(
                pltpu.make_async_copy(out_new.at[n, at_rows], ref.at[at_rows], osems.at[n, step])
            )
            stores[-1].start()
    grad = jnp.sum(jnp.where(square, column[...], 0.0), axis=0, keepdims=True)
    new_gw[...], new_gm[...], new_gs[...] = adam_update(
        gain[...], gain_m[...], gain_s[...], grad, 0.0
    )
    for store in stores:
        store.wait()


def run_adam(share, o_grad, losses, gains, inputs, outputs):
    vmem = pl.BlockSpec(memory_space=pltpu.VMEM)
    hbm = pl.BlockSpec(memory_space=pltpu.HBM)
    return pl.pallas_call(
        adam_kernel,
        out_shape=[jax.ShapeDtypeStruct((2,), f32)]
        + [jax.ShapeDtypeStruct((128, 3 * INNER), f32)] * 3
        + [jax.ShapeDtypeStruct((64, D), f32)] * 3
        + [jax.ShapeDtypeStruct((1, 128), f32)] * 3,
        in_specs=[vmem] * 12,
        out_specs=[pl.BlockSpec(memory_space=pltpu.SMEM)] + [hbm] * 6 + [vmem] * 3,
        scratch_shapes=[
            pltpu.VMEM((128, 128), f32),
            pltpu.VMEM((3, 128, 3 * INNER), f32),
            pltpu.VMEM((3, 64, D), f32),
            pltpu.SemaphoreType.DMA((3, STEPS)),
            pltpu.SemaphoreType.DMA((3, 2)),
        ],
        compiler_params=pltpu.CompilerParams(vmem_limit_bytes=24 * 1024 * 1024),
        name="adam",
    )(share, o_grad, losses, *gains, *inputs, *outputs)


def per_device(
    frames, crop_starts, pairing, bias_table,
    input_master, input_moment, input_square,
    output_master, output_moment, output_square,
    gain_master, gain_moment, gain_square,
):
    gains = [g.reshape(1, 128) for g in (gain_master, gain_moment, gain_square)]
    losses, s_grad, o_grad = run_kernel(
        *run_norm(frames, crop_starts), pairing.reshape(1, 256), bias_table,
        input_master, output_master, gains[0],
    )
    new = run_adam(
        s_grad, o_grad, losses, gains,
        (input_master, input_moment, input_square),
        (output_master, output_moment, output_square),
    )
    return (*new[:7], *(g.reshape(128) for g in new[7:]))


def solution(mesh):
    one = P("shard")
    two = P("shard", None)
    items = P(("dp", "shard"))
    in_specs = (P(("dp", "shard"), None, None), items, P(), P()) + (two,) * 6 + (one,) * 3
    out_specs = (items,) + (two,) * 6 + (one,) * 3
    return jax.shard_map(
        per_device, mesh=mesh, in_specs=in_specs, out_specs=out_specs, check_vma=False
    )
```

```python
import functools

import jax
import jax.numpy as jnp
from jax import lax
from jax.experimental import pallas as pl
from jax.experimental.pallas import tpu as pltpu
from jax.sharding import PartitionSpec as P

D = 2048
HEADS = 8
HEAD_DIM = 128
INNER = 1024
CROP = 128
QKV = 3 * HEAD_DIM
SLICE = D // 8

inv_tau = 20.0
norm_eps = 1e-05
embed_eps = 1e-06
beta_one = 0.9
beta_two = 0.999
adam_eps = 1e-08
learn_rate = 0.002
weight_decay = 0.1
adam_step = 1000
score_scale = HEAD_DIM ** (-0.5)

f32 = jnp.float32
bf16 = jnp.bfloat16
NT = (((1,), (1,)), ((), ()))
TN = (((0,), (0,)), ((), ()))


def dot(a, b, dims=(((1,), (0,)), ((), ()))):
    return lax.dot_general(a, b, dims, preferred_element_type=f32)


def split(a):
    high = a.astype(bf16)
    return high, (a - high.astype(f32)).astype(bf16)


def dot3(a, b, dims=(((1,), (0,)), ((), ()))):
    rows = a.shape[0]
    high, low = split(a)
    both = dot(jnp.concatenate([high, low], axis=0), b[0], dims)
    return both[:rows] + both[rows:] + dot(high, b[1], dims)


def adam_update(master, moment, square, gradient, decay):
    moment_new = beta_one * moment + (1.0 - beta_one) * gradient
    square_new = beta_two * square + (1.0 - beta_two) * gradient * gradient
    mean_scale = learn_rate / (1.0 - beta_one**adam_step)
    square_scale = 1.0 / (1.0 - beta_two**adam_step)
    step = moment_new * mean_scale / (jnp.sqrt(square_new * square_scale) + adam_eps)
    return (master * (1.0 - learn_rate * decay) - step, moment_new, square_new)


W, WO, MC, MM, EA, PO, GR, TO, LA, GM, RZ, RY, BQ, BK, SS = range(15)


def div(a, b):
    return lax.div(a, jnp.int32(b))


def rem(a, b):
    return lax.rem(a, jnp.int32(b))


def item_of(row):
    t, p = (row // 2) % 8, row // 16
    return 2 * (
        ((t // 2) * 2 + p // 8) * 16 + ((p // 4) % 2) * 8 + (p % 4) * 2 + t % 2
    ) + row % 2


def kernel(
    xn, mc, pairing, bias, input_master, output_master, gain,
    loss_out, s_out, o_out,
    wraw, woraw, wp, wo2, mcsend, target,
    xbuf, xt, wbuf, wobuf, mcbuf, qkvbuf, probs, arows, mmbuf, eabuf, easend, pobuf, grbuf, ssbuf,
    tobuf, labuf, gmsend, gmbuf, gp, zsend, ysend, zrecv, yrecv, zmid, ymid, qrecv, krecv, s_fin, o_tmp, o_fin, band, table,
    lsem, ssem, rsem, xssem, xrsem, f_send, f_recv,
):
    dp = lax.axis_index("dp")
    sh = lax.axis_index("shard")
    x, yh = div(dp, 2), rem(dp, 2)
    yl, z, c = div(sh, 8), rem(div(sh, 2), 4), rem(sh, 2)
    base = yl * 8 + z * 2
    t = 2 * x + c
    p = yh * 8 + yl * 4 + z
    y = yh * 2 + yl

    def tp_dev(m):
        return (div(m, 2) * 2 + yh, base + rem(m, 2))

    def plane_dev(q):
        return (x * 2 + div(q, 8), rem(div(q, 4), 2) * 8 + rem(q, 4) * 2 + c)

    def at(y2, z2):
        y2 = jnp.int32(y2)
        return (x * 2 + div(y2, 2), rem(y2, 2) * 8 + z2 * 2 + c)

    def push(src, dst, send, recv, dev):
        pltpu.make_async_remote_copy(
            src_ref=src, dst_ref=dst, send_sem=send, recv_sem=recv,
            device_id=dev, device_id_type=pl.DeviceIdType.MESH,
        ).start()

    def await_bytes(ref, sem):
        pltpu.make_async_copy(ref, ref, sem).wait()

    loads = []
    for i in range(3):
        cols = pl.ds(pl.multiple_of(i * INNER + x * 256, 256), 256)
        loads.append(
            pltpu.make_async_copy(input_master.at[:, cols], wraw.at[i], lsem.at[i])
        )
    loads.append(
        pltpu.make_async_copy(
            output_master.at[:, pl.ds(pl.multiple_of(x * 512, 512), 512)], woraw, lsem.at[3]
        )
    )
    for load in loads:
        load.start()

    barrier = pltpu.get_barrier_semaphore()

    def greet(dev):
        pl.semaphore_signal(barrier, inc=1, device_id=dev, device_id_type=pl.DeviceIdType.MESH)

    for k in range(1, 16):
        greet((dp, rem(sh + k, 16)))
    for k in range(8):
        greet((x * 2 + 1 - yh, div(jnp.int32(k), 4) * 8 + (k % 4) * 2 + c))
    for k in range(1, 8):
        j = rem(dp + k, 8)
        greet((j, base + 1 - c))
        if k % 2 == 0:
            greet((j, base + c))
        else:
            @pl.when(div(j, 2) != x)
            def _():
                greet((j, base + c))

    right = rem(x + 1, 4) * 2 + c
    left = rem(x + 3, 4) * 2 + c
    far = rem(x + 2, 4) * 2 + c
    sib = x * 2 + 1 - c
    other = 1 - 2 * c

    def send_item(src, slot, member):
        push(src, xbuf.at[slot], xssem, xrsem.at[slot], tp_dev(member))

    pl.semaphore_wait(barrier, 36)
    send_item(xn.at[0], 2 * t, right)
    send_item(xn.at[1], 2 * t + 1, left)
    send_item(xn.at[0], 2 * t, sib)
    send_item(xn.at[1], 2 * t + 1, sib)
    send_item(xn.at[1], 2 * t + 1, right)
    send_item(xn.at[0], 2 * t, left)

    for load in loads:
        load.wait()
    square = lax.broadcasted_iota(jnp.int32, (128, 128), 0) == lax.broadcasted_iota(
        jnp.int32, (128, 128), 1
    )
    gain_row = gain[...].astype(bf16).astype(f32)
    gain_col = jnp.sum(jnp.where(square, gain_row, 0.0), axis=1, keepdims=True)
    for core in range(2):
        for i in range(3):
            piece = wraw[i, :, core * 128 : (core + 1) * 128].astype(bf16).astype(f32)
            wp[core, :, i * 128 : (i + 1) * 128] = (piece * gain_col).astype(bf16)
        wo2[core] = woraw[:, core * SLICE : (core + 1) * SLICE].astype(bf16)

    def send_w(k, _):
        s = rem(sh + k, 16)
        push(wp.at[rem(s, 2)], wbuf.at[sh], ssem.at[W], rsem.at[W], (dp, s))
        return 0

    lax.fori_loop(1, 16, send_w, 0, unroll=True)

    def send_wo(k, _):
        s = rem(sh + k, 16)
        push(wo2.at[rem(s, 2)], wobuf.at[sh], ssem.at[WO], rsem.at[WO], (dp, s))
        return 0

    lax.fori_loop(1, 16, send_wo, 0, unroll=True)

    for m in range(8):
        for i in range(2):
            mcsend[m, i : i + 1, :] = mc[i, m : m + 1, :]

    def send_mc(k, _):
        m = rem(t + k, 8)
        push(mcsend.at[m], mcbuf.at[t], ssem.at[MC], rsem.at[MC], tp_dev(m))
        return 0

    lax.fori_loop(1, 8, send_mc, 0, unroll=True)

    wbuf[sh] = wp[c]
    wobuf[sh] = wo2[c]
    mcbuf[t] = mcsend[t]
    xbuf[2 * t] = xn[0]
    xbuf[2 * t + 1] = xn[1]

    table[...] = jnp.zeros_like(table)
    table[:, : 2 * CROP - 1] = bias[...]
    row = jnp.broadcast_to(table[pl.ds(t, 1), :], (CROP, 2 * CROP))
    shifted = pltpu.roll(row, CROP + 1, 1, stride=1, stride_axis=0)
    band[...] = shifted[:, :CROP].T

    lane16 = lax.broadcasted_iota(jnp.int32, (16, 256), 1)
    sub16 = lax.broadcasted_iota(jnp.int32, (16, 256), 0)
    pair = jnp.broadcast_to(pairing[...], (16, 256))
    swapped = jnp.where(lane16 % 2 == 0, pltpu.roll(pair, 255, 1), pltpu.roll(pair, 1, 1))
    hot_a = (pair == item_of(sub16 + p * 16)).astype(f32).astype(bf16)
    rows256 = lax.broadcasted_iota(jnp.int32, (256, 256), 0)
    hot_b = (jnp.broadcast_to(swapped[:1], (256, 256)) == item_of(rows256)).astype(f32).astype(bf16)
    target[...] = dot(hot_a, hot_b, NT)

    def wait_item(slot):
        await_bytes(xbuf.at[slot], xrsem.at[slot])

    wait_item(2 * left)
    send_item(xbuf.at[2 * left], 2 * left, right)
    send_item(xbuf.at[2 * left], 2 * left, sib)
    wait_item(2 * right + 1)
    send_item(xbuf.at[2 * right + 1], 2 * right + 1, left)
    send_item(xbuf.at[2 * right + 1], 2 * right + 1, sib)
    wait_item(2 * sib)
    wait_item(2 * sib + 1)
    await_bytes(wbuf.at[pl.ds(0, 15)], rsem.at[W])

    half_mask = (
        lax.broadcasted_iota(jnp.int32, (16, 256), 0)
        == lax.broadcasted_iota(jnp.int32, (16, 256), 1) // 128
    )

    def forward(m):
        rows = xbuf[pl.ds(2 * m, 2)].reshape(2 * CROP, D)
        packed = dot(rows, wbuf[...].reshape(D, QKV)).astype(bf16)
        xt[:, pl.ds(pl.multiple_of(m * 256, 256), 256)] = rows.T
        qkvbuf[pl.ds(2 * m, 2)] = packed.reshape(2, CROP, QKV)
        mass = []
        for i in range(2):
            part = packed[i * CROP : (i + 1) * CROP]
            q, k, v = part[:, :128], part[:, 128:256], part[:, 256:]
            scores = dot(q, k, NT) * score_scale + band[...]
            raised = jnp.exp(scores - jnp.max(scores, axis=-1, keepdims=True))
            prob = raised / jnp.sum(raised, axis=-1, keepdims=True)
            probs[2 * m + i] = prob
            mixed = dot(prob.astype(bf16), v).astype(bf16).astype(f32)
            mmbuf[t, pl.ds(2 * m + i, 1), :] = jnp.sum(mixed, axis=0, keepdims=True)
            mass.append(jnp.sum(prob, axis=0, keepdims=True))
        both = jnp.where(half_mask, jnp.concatenate(mass, axis=1), 0.0).astype(bf16)
        weighed = dot(both, rows)
        for i in range(2):
            arows[pl.ds(2 * m + i, 1), :] = weighed[i : i + 1]

    def fwd_own(k, _):
        forward(t + k * other)
        return 0

    lax.fori_loop(0, 2, fwd_own, 0)

    wait_item(2 * left + 1)
    send_item(xbuf.at[2 * left + 1], 2 * left + 1, sib)
    wait_item(2 * right)
    send_item(xbuf.at[2 * right], 2 * right, sib)

    def fwd_near(k, _):
        member = rem(x + 3 + 2 * rem(k, 2), 4) * 2 + c + div(k, 2) * other

        @pl.when(k >= 2)
        def _():
            wait_item(2 * member)
            wait_item(2 * member + 1)

        forward(member)
        return 0

    lax.fori_loop(0, 4, fwd_near, 0)

    wait_item(2 * far)
    send_item(xbuf.at[2 * far], 2 * far, sib)
    wait_item(2 * far + 1)
    send_item(xbuf.at[2 * far + 1], 2 * far + 1, sib)

    def fwd_far(k, _):
        member = far + k * other

        @pl.when(k >= 1)
        def _():
            wait_item(2 * member)
            wait_item(2 * member + 1)

        forward(member)
        return 0

    lax.fori_loop(0, 2, fwd_far, 0)

    def send_mm(k, _):
        push(mmbuf.at[t], mmbuf.at[t], ssem.at[MM], rsem.at[MM], tp_dev(rem(t + k, 8)))
        return 0

    lax.fori_loop(1, 8, send_mm, 0, unroll=True)
    await_bytes(wobuf.at[pl.ds(0, 15)], rsem.at[WO])
    await_bytes(mcbuf.at[pl.ds(0, 7)], rsem.at[MC])
    await_bytes(mmbuf.at[pl.ds(0, 7)], rsem.at[MM])

    wo_slice = wobuf[...].reshape(INNER, SLICE)
    summed = jnp.concatenate([mmbuf[h] for h in range(8)], axis=1)
    product = dot(jnp.concatenate(split(summed), axis=0), wo_slice)
    means = jnp.concatenate([mcbuf[m] for m in range(8)], axis=0)
    pooled = means + (product[:16] + product[16:]) * (1.0 / CROP)
    pobuf[p] = pooled

    def send_po(k, _):
        q = rem(p + k, 16)
        push(pobuf.at[p], pobuf.at[p], ssem.at[PO], rsem.at[PO], plane_dev(q))
        return 0

    lax.fori_loop(1, 16, send_po, 0, unroll=True)

    own = (lane16 == sub16 + p * 16).astype(f32)
    for s in range(16):
        q = (s % 2) * 8 + s // 2
        easend[q, :, :128] = arows[:, s * 128 : (s + 1) * 128].astype(bf16)
        easend[q, :, 128:] = mmbuf[s // 2].astype(bf16)
    eabuf[p] = easend[p]

    await_bytes(pobuf.at[pl.ds(0, 15)], rsem.at[PO])
    everyone = pobuf[...].reshape(256, SLICE)
    parts = split(everyone)
    grbuf[t] = dot3(pooled, parts, NT)
    squares = jnp.concatenate(split(everyone * everyone), axis=1)
    ssbuf[t] = dot(jnp.ones((8, 2 * SLICE), bf16), squares, NT)[:1]

    def send_gr(k, _):
        dev = tp_dev(rem(t + k, 8))
        push(grbuf.at[t], grbuf.at[t], ssem.at[GR], rsem.at[GR], dev)
        push(ssbuf.at[t], ssbuf.at[t], ssem.at[SS], rsem.at[SS], dev)
        return 0

    lax.fori_loop(1, 8, send_gr, 0, unroll=True)
    def send_ea(k, _):
        q = rem(p + k, 16)
        push(easend.at[q], eabuf.at[p], ssem.at[EA], rsem.at[EA], plane_dev(q))
        return 0

    lax.fori_loop(1, 16, send_ea, 0, unroll=True)
    await_bytes(grbuf.at[pl.ds(0, 7)], rsem.at[GR])
    await_bytes(ssbuf.at[pl.ds(0, 7)], rsem.at[SS])
    gram = grbuf[0]
    for m in range(1, 8):
        gram = gram + grbuf[m]
    inv_row = lax.rsqrt(jnp.sum(ssbuf[...], axis=0) + embed_eps)
    inv_col = jnp.sum(own * inv_row, axis=1, keepdims=True)
    sims = gram * inv_col * inv_row * inv_tau
    exponents = jnp.where(own > 0.5, 0.0, jnp.exp(sims - inv_tau))
    totals = jnp.sum(exponents, axis=1, keepdims=True)
    tobuf[p] = jnp.sum(own * totals, axis=0, keepdims=True)

    def send_to(k, _):
        q = rem(p + k, 16)
        push(tobuf.at[p], tobuf.at[p], ssem.at[TO], rsem.at[TO], plane_dev(q))
        return 0

    lax.fori_loop(1, 16, send_to, 0, unroll=True)
    losses = jnp.log(totals) + inv_tau - jnp.sum(sims * target[...], axis=1, keepdims=True)
    loss_out[...] = jnp.broadcast_to(losses, (16, 128))
    await_bytes(tobuf.at[pl.ds(0, 15)], rsem.at[TO])
    column_totals = jnp.sum(tobuf[...], axis=0)
    weights = exponents / totals + exponents / column_totals - 2.0 * target[...]
    grad_embedding = dot3(weights * inv_row, parts) * inv_tau
    along = jnp.sum(weights * sims, axis=1, keepdims=True)
    grad_pooled = (grad_embedding - pooled * inv_col * along) * inv_col
    grad_frame = (grad_pooled * (1.0 / CROP)).astype(bf16)
    partial = dot(grad_frame, wo_slice, NT)
    for h in range(8):
        gmsend[h] = partial[:, h * 128 : (h + 1) * 128]
    labuf[p, :, :SLICE] = grad_frame

    def send_gm(k, _):
        m = rem(t + k, 8)
        push(gmsend.at[m], gmbuf.at[t], ssem.at[GM], rsem.at[GM], tp_dev(m))
        return 0

    lax.fori_loop(1, 8, send_gm, 0, unroll=True)
    gmbuf[t] = gmsend[t]

    await_bytes(gmbuf.at[pl.ds(0, 7)], rsem.at[GM])
    gm = gmbuf[0]
    for m in range(1, 8):
        gm = gm + gmbuf[m]
    grad_mixed = gm.astype(bf16)
    labuf[p, :, SLICE:] = grad_mixed
    sub_item = lax.broadcasted_iota(jnp.int32, (16, 128), 0)

    def backward(step, _):
        for i in range(16):
            b = step * 16 + i
            part = qkvbuf[b]
            q, k, v = part[:, :128], part[:, 128:256], part[:, 256:]
            prob = probs[b]
            all_rows = dot(grad_mixed, v, NT)
            g_row = jnp.sum(jnp.where(sub_item == b, all_rows, 0.0), axis=0, keepdims=True)
            centred = g_row - jnp.sum(prob * g_row, axis=-1, keepdims=True)
            dscores = (prob * centred * score_scale).astype(bf16)
            grad_q = dot(dscores, k)
            grad_k = dot(dscores, q, TN)
            gp[b] = jnp.concatenate([grad_q, grad_k], axis=1).astype(bf16)

        def send_la(j, _):
            q = rem(p + j, 16)
            push(labuf.at[p], labuf.at[p], ssem.at[LA], rsem.at[LA], plane_dev(q))
            return 0

        lax.fori_loop(1, 16, send_la, 0)
        return 0

    lax.fori_loop(0, 1, backward, 0)

    def scatter(k, _):
        z2 = rem(z + k, 4)
        for yl2 in range(2):
            rows = pl.ds(pl.multiple_of((yl2 * 4 + z2) * 256, 256), 256)
            value = dot(xt[rows, :], gp[...].reshape(16 * CROP, 256)).astype(bf16)
            for half in range(2):
                y2 = half * 2 + yl2
                block = value[half * 128 : (half + 1) * 128]
                zsend[z2, y2, :128] = block[:, :128]
                zsend[z2, y2, 128:] = block[:16, 128:]
                ysend[y2, z2] = block[16:, 128:]

                @pl.when(y2 != y)
                def _():
                    push(ysend.at[y2, z2], yrecv.at[y, z2], ssem.at[RY], rsem.at[RY], at(y2, z))

        @pl.when(z2 != z)
        def _():
            push(zsend.at[z2], zrecv.at[z], ssem.at[RZ], rsem.at[RZ], at(y, z2))

        return 0

    lax.fori_loop(1, 5, scatter, 0)
    zrecv[z] = zsend[z]
    yrecv[y] = ysend[y]

    def add_up(ref, *index):
        total = ref[(0, *index)].astype(f32)
        for q in range(1, 4):
            total = total + ref[(q, *index)].astype(f32)
        return total.astype(bf16)

    await_bytes(yrecv.at[pl.ds(0, 3)], rsem.at[RY])
    for i in range(4):
        ymid[i] = add_up(yrecv, i)
    for j in range(1, 4):
        z2 = rem(z + j, 4)
        push(ymid.at[z2], krecv.at[z], ssem.at[BK], rsem.at[BK], at(y, z2))
    krecv[z] = ymid[z]

    await_bytes(eabuf.at[pl.ds(0, 15)], rsem.at[EA])
    await_bytes(labuf.at[pl.ds(0, 15)], rsem.at[LA])
    early = eabuf[...].reshape(256, 256)
    late = labuf[...].reshape(256, SLICE + 128)
    o_tmp[...] = dot(early[:, 128:], late[:, :SLICE], TN)
    s_fin[2] = dot(early[:, :128], late[:, SLICE:], TN).astype(bf16)
    o_fin[...] = o_tmp[pl.ds(pl.multiple_of(yh * 64, 64), 64), :].astype(bf16)

    s_cols = pl.ds(pl.multiple_of(t * 128, 128), 128)
    o_cols = pl.ds(pl.multiple_of(t * SLICE, SLICE), SLICE)

    def each_target(fn):
        for k in range(1, 8):
            fn(rem(dp + k, 8))

        @pl.when(c != yh)
        def _():
            fn(dp)

    def send_early(j):
        dev = (j, base + yh)
        push(s_fin.at[2], s_out.at[2, :, s_cols], f_send.at[2], f_recv.at[2], dev)
        push(o_fin, o_out.at[:, o_cols], f_send.at[3], f_recv.at[3], dev)

    each_target(send_early)

    await_bytes(zrecv.at[pl.ds(0, 3)], rsem.at[RZ])
    for i in range(4):
        zmid[i] = add_up(zrecv, i)
    for j in range(1, 4):
        y2 = rem(y + j, 4)
        push(zmid.at[y2], qrecv.at[y], ssem.at[BQ], rsem.at[BQ], at(y2, z))
    qrecv[y] = zmid[y]

    def send_part(i, rows, sem):
        def send(j):
            push(
                s_fin.at[i, rows], s_out.at[i, rows, s_cols], f_send.at[sem], f_recv.at[sem],
                (j, base + yh),
            )

        each_target(send)

    all_rows, first_half, last_half = pl.ds(0, 128), pl.ds(0, 16), pl.ds(16, 112)
    await_bytes(krecv.at[pl.ds(0, 3)], rsem.at[BK])
    s_fin[1, 16:] = add_up(krecv)
    send_part(1, last_half, 4)
    await_bytes(qrecv.at[pl.ds(0, 3)], rsem.at[BQ])
    added = add_up(qrecv)
    s_fin[0] = added[:128]
    s_fin[1, :16] = added[128:]
    send_part(0, all_rows, 0)
    send_part(1, first_half, 1)

    @pl.when(c == yh)
    def _():
        s_out[:, :, s_cols] = s_fin[...]
        o_out[:, o_cols] = o_fin[...]

    def await_all(sems):
        def await_parts(members):
            cols = pl.ds(0, members * 128)
            await_bytes(s_out.at[0, :, cols], sems.at[0])
            await_bytes(s_out.at[1, first_half, cols], sems.at[1])
            await_bytes(s_out.at[2, :, cols], sems.at[2])
            await_bytes(o_out.at[:, pl.ds(0, members * SLICE)], sems.at[3])
            await_bytes(s_out.at[1, last_half, cols], sems.at[4])

        @pl.when(c == yh)
        def _():
            await_parts(7)

        @pl.when(c != yh)
        def _():
            await_parts(8)

    await_all(f_recv)
    await_all(f_send)
    await_bytes(xbuf.at[pl.ds(0, 14)], xssem)
    for sem, ref in (
        (W, wbuf), (WO, wobuf), (EA, eabuf), (PO, pobuf), (TO, tobuf), (LA, labuf),
    ):
        await_bytes(ref.at[pl.ds(0, 15)], ssem.at[sem])
    for sem, ref in ((RZ, zrecv), (RY, yrecv), (BQ, qrecv), (BK, krecv)):
        await_bytes(ref.at[pl.ds(0, 3)], ssem.at[sem])
    for sem, ref in ((MC, mcbuf), (MM, mmbuf), (GR, grbuf), (SS, ssbuf), (GM, gmbuf)):
        await_bytes(ref.at[pl.ds(0, 7)], ssem.at[sem])


def norm_kernel(starts, frames, xn, mc, raw, sems):
    begin = [starts[i] for i in range(2)]
    base = [(b // 16) * 16 for b in begin]
    base = [jnp.minimum(b, CROP - 16) for b in base]
    loads = [
        pltpu.make_async_copy(
            frames.at[i, pl.ds(pl.multiple_of(base[i], 16), CROP + 16)], raw.at[i], sems.at[i]
        )
        for i in range(2)
    ]
    for load in loads:
        load.start()
    for i in range(2):
        loads[i].wait()
        odd = begin[i] - base[i]

        def chunk(r, total):
            near = raw[i, pl.ds(pl.multiple_of(r * 16, 16), 32), :].astype(f32)
            rows = pltpu.roll(near, (32 - odd) % 32, 0)[:16]
            centred = rows - jnp.mean(rows, axis=-1, keepdims=True)
            scale = lax.rsqrt(jnp.mean(centred * centred, axis=-1, keepdims=True) + norm_eps)
            xn[i, pl.ds(pl.multiple_of(r * 16, 16), 16), :] = (centred * scale).astype(bf16)
            return total + rows[:8] + rows[8:]

        total = lax.fori_loop(0, CROP // 16, chunk, jnp.zeros((8, D), f32), unroll=8)
        mean = jnp.sum(total, axis=0, keepdims=True) * (1.0 / CROP)
        for m in range(8):
            mc[i, m : m + 1, :] = mean[:, m * SLICE : (m + 1) * SLICE]


def run_norm(frames, starts):
    vmem = pl.BlockSpec(memory_space=pltpu.VMEM)
    return pl.pallas_call(
        norm_kernel,
        out_shape=(
            jax.ShapeDtypeStruct((2, CROP, D), bf16),
            jax.ShapeDtypeStruct((2, 8, SLICE), f32),
        ),
        in_specs=[
            pl.BlockSpec(memory_space=pltpu.SMEM), pl.BlockSpec(memory_space=pltpu.HBM),
        ],
        out_specs=(vmem, vmem),
        scratch_shapes=[
            pltpu.VMEM((2, CROP + 16, D), bf16),
            pltpu.SemaphoreType.DMA((2,)),
        ],
        compiler_params=pltpu.CompilerParams(vmem_limit_bytes=24 * 1024 * 1024),
        name="norm",
    )(starts, frames)


def run_kernel(*args):
    vmem = pl.BlockSpec(memory_space=pltpu.VMEM)
    hbm = pl.BlockSpec(memory_space=pltpu.HBM)
    return pl.pallas_call(
        kernel,
        out_shape=(
            jax.ShapeDtypeStruct((16, 128), f32),
            jax.ShapeDtypeStruct((3, 128, INNER), bf16),
            jax.ShapeDtypeStruct((64, D), bf16),
        ),
        in_specs=[vmem, vmem, vmem, vmem, hbm, hbm, vmem],
        out_specs=(vmem, vmem, vmem),
        scratch_shapes=[
            pltpu.VMEM((3, 128, 256), f32),
            pltpu.VMEM((64, 512), f32),
            pltpu.VMEM((2, 128, QKV), bf16),
            pltpu.VMEM((2, 64, SLICE), bf16),
            pltpu.VMEM((8, 2, SLICE), f32),
            pltpu.VMEM((16, 256), f32),
            pltpu.VMEM((16, CROP, D), bf16),
            pltpu.VMEM((D, 16 * CROP), bf16),
            pltpu.VMEM((16, 128, QKV), bf16),
            pltpu.VMEM((16, 64, SLICE), bf16),
            pltpu.VMEM((8, 2, SLICE), f32),
            pltpu.VMEM((16, CROP, QKV), bf16),
            pltpu.VMEM((16, CROP, CROP), f32),
            pltpu.VMEM((16, D), f32),
            pltpu.VMEM((8, 16, 128), f32),
            pltpu.VMEM((16, 16, 256), bf16),
            pltpu.VMEM((16, 16, 256), bf16),
            pltpu.VMEM((16, 16, SLICE), f32),
            pltpu.VMEM((8, 16, 256), f32),
            pltpu.VMEM((8, 1, 256), f32),
            pltpu.VMEM((16, 1, 256), f32),
            pltpu.VMEM((16, 16, SLICE + 128), bf16),
            pltpu.VMEM((8, 16, 128), f32),
            pltpu.VMEM((8, 16, 128), f32),
            pltpu.VMEM((16, CROP, 256), bf16),
            pltpu.VMEM((4, 4, 144, 128), bf16),
            pltpu.VMEM((4, 4, 112, 128), bf16),
            pltpu.VMEM((4, 4, 144, 128), bf16),
            pltpu.VMEM((4, 4, 112, 128), bf16),
            pltpu.VMEM((4, 144, 128), bf16),
            pltpu.VMEM((4, 112, 128), bf16),
            pltpu.VMEM((4, 144, 128), bf16),
            pltpu.VMEM((4, 112, 128), bf16),
            pltpu.VMEM((3, 128, 128), bf16),
            pltpu.VMEM((128, SLICE), f32),
            pltpu.VMEM((64, SLICE), bf16),
            pltpu.VMEM((CROP, CROP), f32),
            pltpu.VMEM((HEADS, 2 * CROP), f32),
            pltpu.SemaphoreType.DMA((4,)),
            pltpu.SemaphoreType.DMA((15,)),
            pltpu.SemaphoreType.DMA((15,)),
            pltpu.SemaphoreType.DMA,
            pltpu.SemaphoreType.DMA((16,)),
        ]
        + [pltpu.SemaphoreType.DMA((5,))] * 2,
        compiler_params=pltpu.CompilerParams(
            collective_id=0, has_side_effects=True, vmem_limit_bytes=40 * 1024 * 1024
        ),
        cost_estimate=pl.CostEstimate(
            flops=15_000_000_000, bytes_accessed=300_000_000, transcendentals=300_000
        ),
        name="encoder",
    )(*args)


STEPS = 8


def adam_kernel(
    share, o_grad, losses, gain, gain_m, gain_s, in_w, in_m, in_s, out_w, out_m, out_s,
    pair_losses, new_in_w, new_in_m, new_in_s, new_out_w, new_out_m, new_out_s, new_gw, new_gm, new_gs,
    column, in_new, out_new, isems, osems,
):
    t = 2 * (lax.axis_index("dp") // 2) + lax.axis_index("shard") % 2
    item = lax.broadcasted_iota(jnp.int32, (16, 128), 0)
    lane = lax.broadcasted_iota(jnp.int32, (16, 128), 1)
    for i in range(2):
        mine = jnp.logical_and(item == 2 * t + i, lane == 0)
        pair_losses[i] = jnp.sum(jnp.where(mine, losses[...], 0.0))
    square = lax.broadcasted_iota(jnp.int32, (128, 128), 0) == lax.broadcasted_iota(
        jnp.int32, (128, 128), 1
    )
    gain_row = gain[...].astype(bf16).astype(f32)
    column[...] = jnp.broadcast_to(
        jnp.sum(jnp.where(square, gain_row, 0.0), axis=1, keepdims=True), (128, 128)
    )
    rows = 128 // STEPS
    stores = []
    for step in range(STEPS):
        at_rows = pl.ds(step * rows, rows)
        gain_col = column[at_rows, :][:, :1]

        def part(j, total):
            i, cols = j, pl.ds(pl.multiple_of(j * 1024, 1024), 1024)
            inner = pl.ds(0, 1024)
            master = in_w[at_rows, cols]
            piece = share[i, at_rows, inner].astype(f32)
            new = adam_update(
                master, in_m[at_rows, cols], in_s[at_rows, cols], piece * gain_col, weight_decay
            )
            for n in range(3):
                in_new[n, at_rows, cols] = new[n]
            terms = piece * master.astype(bf16).astype(f32)
            return total + sum(terms[:, n * 128 : (n + 1) * 128] for n in range(8))

        total = lax.fori_loop(0, 3, part, jnp.zeros((rows, 128), f32), unroll=3)
        column[at_rows, :] = jnp.broadcast_to(jnp.sum(total, axis=1, keepdims=True), (rows, 128))
        for n, ref in enumerate((new_in_w, new_in_m, new_in_s)):
            stores.append(
                pltpu.make_async_copy(in_new.at[n, at_rows], ref.at[at_rows], isems.at[n, step])
            )
            stores[-1].start()
    for step in range(2):
        at_rows = pl.ds(step * 32, 32)

        def out_part(j, _):
            cols = pl.ds(pl.multiple_of(j * 512, 512), 512)
            new = adam_update(
                out_w[at_rows, cols], out_m[at_rows, cols], out_s[at_rows, cols],
                o_grad[at_rows, cols].astype(f32), weight_decay,
            )
            for n in range(3):
                out_new[n, at_rows, cols] = new[n]
            return 0

        lax.fori_loop(0, 4, out_part, 0, unroll=4)
        for n, ref in enumerate((new_out_w, new_out_m, new_out_s)):
            stores.append(
                pltpu.make_async_copy(out_new.at[n, at_rows], ref.at[at_rows], osems.at[n, step])
            )
            stores[-1].start()
    grad = jnp.sum(jnp.where(square, column[...], 0.0), axis=0, keepdims=True)
    new_gw[...], new_gm[...], new_gs[...] = adam_update(
        gain[...], gain_m[...], gain_s[...], grad, 0.0
    )
    for store in stores:
        store.wait()


def run_adam(share, o_grad, losses, gains, inputs, outputs):
    vmem = pl.BlockSpec(memory_space=pltpu.VMEM)
    hbm = pl.BlockSpec(memory_space=pltpu.HBM)
    return pl.pallas_call(
        adam_kernel,
        out_shape=[jax.ShapeDtypeStruct((2,), f32)]
        + [jax.ShapeDtypeStruct((128, 3 * INNER), f32)] * 3
        + [jax.ShapeDtypeStruct((64, D), f32)] * 3
        + [jax.ShapeDtypeStruct((1, 128), f32)] * 3,
        in_specs=[vmem] * 12,
        out_specs=[pl.BlockSpec(memory_space=pltpu.SMEM)] + [hbm] * 6 + [vmem] * 3,
        scratch_shapes=[
            pltpu.VMEM((128, 128), f32),
            pltpu.VMEM((3, 128, 3 * INNER), f32),
            pltpu.VMEM((3, 64, D), f32),
            pltpu.SemaphoreType.DMA((3, STEPS)),
            pltpu.SemaphoreType.DMA((3, 2)),
        ],
        compiler_params=pltpu.CompilerParams(vmem_limit_bytes=24 * 1024 * 1024),
        name="adam",
    )(share, o_grad, losses, *gains, *inputs, *outputs)


def per_device(
    frames, crop_starts, pairing, bias_table,
    input_master, input_moment, input_square,
    output_master, output_moment, output_square,
    gain_master, gain_moment, gain_square,
):
    gains = [g.reshape(1, 128) for g in (gain_master, gain_moment, gain_square)]
    losses, s_grad, o_grad = run_kernel(
        *run_norm(frames, crop_starts), pairing.reshape(1, 256), bias_table,
        input_master, output_master, gains[0],
    )
    new = run_adam(
        s_grad, o_grad, losses, gains,
        (input_master, input_moment, input_square),
        (output_master, output_moment, output_square),
    )
    return (*new[:7], *(g.reshape(128) for g in new[7:]))


def solution(mesh):
    one = P("shard")
    two = P("shard", None)
    items = P(("dp", "shard"))
    in_specs = (P(("dp", "shard"), None, None), items, P(), P()) + (two,) * 6 + (one,) * 3
    out_specs = (items,) + (two,) * 6 + (one,) * 3
    return jax.shard_map(
        per_device, mesh=mesh, in_specs=in_specs, out_specs=out_specs, check_vma=False
    )
```

```python
import functools

import jax
import jax.numpy as jnp
from jax import lax
from jax.experimental import pallas as pl
from jax.experimental.pallas import tpu as pltpu
from jax.sharding import PartitionSpec as P

D = 2048
HEADS = 8
HEAD_DIM = 128
INNER = 1024
CROP = 128
QKV = 3 * HEAD_DIM
SLICE = D // 8

inv_tau = 20.0
norm_eps = 1e-05
embed_eps = 1e-06
beta_one = 0.9
beta_two = 0.999
adam_eps = 1e-08
learn_rate = 0.002
weight_decay = 0.1
adam_step = 1000
score_scale = HEAD_DIM ** (-0.5)

f32 = jnp.float32
bf16 = jnp.bfloat16
NT = (((1,), (1,)), ((), ()))
TN = (((0,), (0,)), ((), ()))


def dot(a, b, dims=(((1,), (0,)), ((), ()))):
    return lax.dot_general(a, b, dims, preferred_element_type=f32)


def split(a):
    high = a.astype(bf16)
    return high, (a - high.astype(f32)).astype(bf16)


def dot3(a, b, dims=(((1,), (0,)), ((), ()))):
    rows = a.shape[0]
    high, low = split(a)
    both = dot(jnp.concatenate([high, low], axis=0), b[0], dims)
    return both[:rows] + both[rows:] + dot(high, b[1], dims)


def adam_update(master, moment, square, gradient, decay):
    moment_new = beta_one * moment + (1.0 - beta_one) * gradient
    square_new = beta_two * square + (1.0 - beta_two) * gradient * gradient
    mean_scale = learn_rate / (1.0 - beta_one**adam_step)
    square_scale = 1.0 / (1.0 - beta_two**adam_step)
    step = moment_new * mean_scale / (jnp.sqrt(square_new * square_scale) + adam_eps)
    return (master * (1.0 - learn_rate * decay) - step, moment_new, square_new)


W, WO, MC, MM, EA, PO, GR, TO, LA, GM, RZ, RY, BQ, BK, SS = range(15)


def div(a, b):
    return lax.div(a, jnp.int32(b))


def rem(a, b):
    return lax.rem(a, jnp.int32(b))


def item_of(row):
    t, p = (row // 2) % 8, row // 16
    return 2 * (
        ((t // 2) * 2 + p // 8) * 16 + ((p // 4) % 2) * 8 + (p % 4) * 2 + t % 2
    ) + row % 2


def kernel(
    xn, mc, pairing, bias, input_master, output_master, gain,
    loss_out, s_out, o_out,
    wraw, woraw, wp, wo2, mcsend, target,
    xbuf, xt, wbuf, wobuf, mcbuf, qkvbuf, probs, arows, mmbuf, eabuf, easend, pobuf, grbuf, ssbuf,
    tobuf, labuf, gmsend, gmbuf, gp, zsend, ysend, zrecv, yrecv, zmid, ymid, qrecv, krecv, s_fin, o_tmp, o_fin, band, table,
    lsem, ssem, rsem, xssem, xrsem, f_send, f_recv,
):
    dp = lax.axis_index("dp")
    sh = lax.axis_index("shard")
    x, yh = div(dp, 2), rem(dp, 2)
    yl, z, c = div(sh, 8), rem(div(sh, 2), 4), rem(sh, 2)
    base = yl * 8 + z * 2
    t = 2 * x + c
    p = yh * 8 + yl * 4 + z
    y = yh * 2 + yl

    def tp_dev(m):
        return (div(m, 2) * 2 + yh, base + rem(m, 2))

    def plane_dev(q):
        return (x * 2 + div(q, 8), rem(div(q, 4), 2) * 8 + rem(q, 4) * 2 + c)

    def at(y2, z2):
        y2 = jnp.int32(y2)
        return (x * 2 + div(y2, 2), rem(y2, 2) * 8 + z2 * 2 + c)

    def push(src, dst, send, recv, dev):
        pltpu.make_async_remote_copy(
            src_ref=src, dst_ref=dst, send_sem=send, recv_sem=recv,
            device_id=dev, device_id_type=pl.DeviceIdType.MESH,
        ).start()

    def await_bytes(ref, sem):
        pltpu.make_async_copy(ref, ref, sem).wait()

    loads = []
    for i in range(3):
        cols = pl.ds(pl.multiple_of(i * INNER + x * 256, 256), 256)
        loads.append(
            pltpu.make_async_copy(input_master.at[:, cols], wraw.at[i], lsem.at[i])
        )
    loads.append(
        pltpu.make_async_copy(
            output_master.at[:, pl.ds(pl.multiple_of(x * 512, 512), 512)], woraw, lsem.at[3]
        )
    )
    for load in loads:
        load.start()

    barrier = pltpu.get_barrier_semaphore()

    def greet(dev):
        pl.semaphore_signal(barrier, inc=1, device_id=dev, device_id_type=pl.DeviceIdType.MESH)

    for k in range(1, 16):
        greet((dp, rem(sh + k, 16)))
    for k in range(8):
        greet((x * 2 + 1 - yh, div(jnp.int32(k), 4) * 8 + (k % 4) * 2 + c))
    for k in range(1, 8):
        j = rem(dp + k, 8)
        greet((j, base + 1 - c))
        if k % 2 == 0:
            greet((j, base + c))
        else:
            @pl.when(div(j, 2) != x)
            def _():
                greet((j, base + c))

    right = rem(x + 1, 4) * 2 + c
    left = rem(x + 3, 4) * 2 + c
    far = rem(x + 2, 4) * 2 + c
    sib = x * 2 + 1 - c
    other = 1 - 2 * c

    def send_item(src, slot, member):
        push(src, xbuf.at[slot], xssem, xrsem.at[slot], tp_dev(member))

    pl.semaphore_wait(barrier, 36)
    send_item(xn.at[0], 2 * t, right)
    send_item(xn.at[1], 2 * t + 1, left)
    send_item(xn.at[0], 2 * t, sib)
    send_item(xn.at[1], 2 * t + 1, sib)
    send_item(xn.at[1], 2 * t + 1, right)
    send_item(xn.at[0], 2 * t, left)

    for load in loads:
        load.wait()
    square = lax.broadcasted_iota(jnp.int32, (128, 128), 0) == lax.broadcasted_iota(
        jnp.int32, (128, 128), 1
    )
    gain_row = gain[...].astype(bf16).astype(f32)
    gain_col = jnp.sum(jnp.where(square, gain_row, 0.0), axis=1, keepdims=True)
    for core in range(2):
        for i in range(3):
            piece = wraw[i, :, core * 128 : (core + 1) * 128].astype(bf16).astype(f32)
            wp[core, :, i * 128 : (i + 1) * 128] = (piece * gain_col).astype(bf16)
        wo2[core] = woraw[:, core * SLICE : (core + 1) * SLICE].astype(bf16)

    def send_w(k, _):
        s = rem(sh + k, 16)
        push(wp.at[rem(s, 2)], wbuf.at[sh], ssem.at[W], rsem.at[W], (dp, s))
        return 0

    lax.fori_loop(1, 16, send_w, 0, unroll=True)

    def send_wo(k, _):
        s = rem(sh + k, 16)
        push(wo2.at[rem(s, 2)], wobuf.at[sh], ssem.at[WO], rsem.at[WO], (dp, s))
        return 0

    lax.fori_loop(1, 16, send_wo, 0, unroll=True)

    for m in range(8):
        for i in range(2):
            mcsend[m, i : i + 1, :] = mc[i, m : m + 1, :]

    def send_mc(k, _):
        m = rem(t + k, 8)
        push(mcsend.at[m], mcbuf.at[t], ssem.at[MC], rsem.at[MC], tp_dev(m))
        return 0

    lax.fori_loop(1, 8, send_mc, 0, unroll=True)

    wbuf[sh] = wp[c]
    wobuf[sh] = wo2[c]
    mcbuf[t] = mcsend[t]
    xbuf[2 * t] = xn[0]
    xbuf[2 * t + 1] = xn[1]

    table[...] = jnp.zeros_like(table)
    table[:, : 2 * CROP - 1] = bias[...]
    row = jnp.broadcast_to(table[pl.ds(t, 1), :], (CROP, 2 * CROP))
    shifted = pltpu.roll(row, CROP + 1, 1, stride=1, stride_axis=0)
    band[...] = shifted[:, :CROP].T

    lane16 = lax.broadcasted_iota(jnp.int32, (16, 256), 1)
    sub16 = lax.broadcasted_iota(jnp.int32, (16, 256), 0)
    pair = jnp.broadcast_to(pairing[...], (16, 256))
    swapped = jnp.where(lane16 % 2 == 0, pltpu.roll(pair, 255, 1), pltpu.roll(pair, 1, 1))
    hot_a = (pair == item_of(sub16 + p * 16)).astype(f32).astype(bf16)
    rows256 = lax.broadcasted_iota(jnp.int32, (256, 256), 0)
    hot_b = (jnp.broadcast_to(swapped[:1], (256, 256)) == item_of(rows256)).astype(f32).astype(bf16)
    target[...] = dot(hot_a, hot_b, NT)

    def wait_item(slot):
        await_bytes(xbuf.at[slot], xrsem.at[slot])

    wait_item(2 * left)
    send_item(xbuf.at[2 * left], 2 * left, right)
    send_item(xbuf.at[2 * left], 2 * left, sib)
    wait_item(2 * right + 1)
    send_item(xbuf.at[2 * right + 1], 2 * right + 1, left)
    send_item(xbuf.at[2 * right + 1], 2 * right + 1, sib)
    wait_item(2 * sib)
    wait_item(2 * sib + 1)
    await_bytes(wbuf.at[pl.ds(0, 15)], rsem.at[W])

    half_mask = (
        lax.broadcasted_iota(jnp.int32, (16, 256), 0)
        == lax.broadcasted_iota(jnp.int32, (16, 256), 1) // 128
    )

    def forward(m):
        rows = xbuf[pl.ds(2 * m, 2)].reshape(2 * CROP, D)
        packed = dot(rows, wbuf[...].reshape(D, QKV)).astype(bf16)
        xt[:, pl.ds(pl.multiple_of(m * 256, 256), 256)] = rows.T
        qkvbuf[pl.ds(2 * m, 2)] = packed.reshape(2, CROP, QKV)
        mass = []
        for i in range(2):
            part = packed[i * CROP : (i + 1) * CROP]
            q, k, v = part[:, :128], part[:, 128:256], part[:, 256:]
            scores = dot(q, k, NT) * score_scale + band[...]
            raised = jnp.exp(scores - jnp.max(scores, axis=-1, keepdims=True))
            prob = raised / jnp.sum(raised, axis=-1, keepdims=True)
            probs[2 * m + i] = prob
            mixed = dot(prob.astype(bf16), v).astype(bf16).astype(f32)
            mmbuf[t, pl.ds(2 * m + i, 1), :] = jnp.sum(mixed, axis=0, keepdims=True)
            mass.append(jnp.sum(prob, axis=0, keepdims=True))
        both = jnp.where(half_mask, jnp.concatenate(mass, axis=1), 0.0).astype(bf16)
        weighed = dot(both, rows)
        for i in range(2):
            arows[pl.ds(2 * m + i, 1), :] = weighed[i : i + 1]

    def fwd_own(k, _):
        forward(t + k * other)
        return 0

    lax.fori_loop(0, 2, fwd_own, 0)

    wait_item(2 * left + 1)
    send_item(xbuf.at[2 * left + 1], 2 * left + 1, sib)
    wait_item(2 * right)
    send_item(xbuf.at[2 * right], 2 * right, sib)

    def fwd_near(k, _):
        member = rem(x + 3 + 2 * rem(k, 2), 4) * 2 + c + div(k, 2) * other

        @pl.when(k >= 2)
        def _():
            wait_item(2 * member)
            wait_item(2 * member + 1)

        forward(member)
        return 0

    lax.fori_loop(0, 4, fwd_near, 0)

    wait_item(2 * far)
    send_item(xbuf.at[2 * far], 2 * far, sib)
    wait_item(2 * far + 1)
    send_item(xbuf.at[2 * far + 1], 2 * far + 1, sib)

    def fwd_far(k, _):
        member = far + k * other

        @pl.when(k >= 1)
        def _():
            wait_item(2 * member)
            wait_item(2 * member + 1)

        forward(member)
        return 0

    lax.fori_loop(0, 2, fwd_far, 0)

    def send_mm(k, _):
        push(mmbuf.at[t], mmbuf.at[t], ssem.at[MM], rsem.at[MM], tp_dev(rem(t + k, 8)))
        return 0

    lax.fori_loop(1, 8, send_mm, 0, unroll=True)
    await_bytes(wobuf.at[pl.ds(0, 15)], rsem.at[WO])
    await_bytes(mcbuf.at[pl.ds(0, 7)], rsem.at[MC])
    await_bytes(mmbuf.at[pl.ds(0, 7)], rsem.at[MM])

    wo_slice = wobuf[...].reshape(INNER, SLICE)
    summed = jnp.concatenate([mmbuf[h] for h in range(8)], axis=1)
    product = dot(jnp.concatenate(split(summed), axis=0), wo_slice)
    means = jnp.concatenate([mcbuf[m] for m in range(8)], axis=0)
    pooled = means + (product[:16] + product[16:]) * (1.0 / CROP)
    pobuf[p] = pooled

    def send_po(k, _):
        q = rem(p + k, 16)
        push(pobuf.at[p], pobuf.at[p], ssem.at[PO], rsem.at[PO], plane_dev(q))
        return 0

    lax.fori_loop(1, 16, send_po, 0, unroll=True)

    own = (lane16 == sub16 + p * 16).astype(f32)
    for s in range(16):
        q = (s % 2) * 8 + s // 2
        easend[q, :, :128] = arows[:, s * 128 : (s + 1) * 128].astype(bf16)
        easend[q, :, 128:] = mmbuf[s // 2].astype(bf16)
    eabuf[p] = easend[p]

    await_bytes(pobuf.at[pl.ds(0, 15)], rsem.at[PO])
    everyone = pobuf[...].reshape(256, SLICE)
    parts = split(everyone)
    grbuf[t] = dot3(pooled, parts, NT)
    squares = jnp.concatenate(split(everyone * everyone), axis=1)
    ssbuf[t] = dot(jnp.ones((8, 2 * SLICE), bf16), squares, NT)[:1]

    def send_gr(k, _):
        dev = tp_dev(rem(t + k, 8))
        push(grbuf.at[t], grbuf.at[t], ssem.at[GR], rsem.at[GR], dev)
        push(ssbuf.at[t], ssbuf.at[t], ssem.at[SS], rsem.at[SS], dev)
        return 0

    lax.fori_loop(1, 8, send_gr, 0, unroll=True)
    def send_ea(k, _):
        q = rem(p + k, 16)
        push(easend.at[q], eabuf.at[p], ssem.at[EA], rsem.at[EA], plane_dev(q))
        return 0

    lax.fori_loop(1, 16, send_ea, 0, unroll=True)
    await_bytes(grbuf.at[pl.ds(0, 7)], rsem.at[GR])
    await_bytes(ssbuf.at[pl.ds(0, 7)], rsem.at[SS])
    gram = grbuf[0]
    for m in range(1, 8):
        gram = gram + grbuf[m]
    inv_row = lax.rsqrt(jnp.sum(ssbuf[...], axis=0) + embed_eps)
    inv_col = jnp.sum(own * inv_row, axis=1, keepdims=True)
    sims = gram * inv_col * inv_row * inv_tau
    exponents = jnp.where(own > 0.5, 0.0, jnp.exp(sims - inv_tau))
    totals = jnp.sum(exponents, axis=1, keepdims=True)
    tobuf[p] = jnp.sum(own * totals, axis=0, keepdims=True)

    def send_to(k, _):
        q = rem(p + k, 16)
        push(tobuf.at[p], tobuf.at[p], ssem.at[TO], rsem.at[TO], plane_dev(q))
        return 0

    lax.fori_loop(1, 16, send_to, 0, unroll=True)
    losses = jnp.log(totals) + inv_tau - jnp.sum(sims * target[...], axis=1, keepdims=True)
    loss_out[...] = jnp.broadcast_to(losses, (16, 128))
    await_bytes(tobuf.at[pl.ds(0, 15)], rsem.at[TO])
    column_totals = jnp.sum(tobuf[...], axis=0)
    weights = exponents / totals + exponents / column_totals - 2.0 * target[...]
    grad_embedding = dot3(weights * inv_row, parts) * inv_tau
    along = jnp.sum(weights * sims, axis=1, keepdims=True)
    grad_pooled = (grad_embedding - pooled * inv_col * along) * inv_col
    grad_frame = (grad_pooled * (1.0 / CROP)).astype(bf16)
    partial = dot(grad_frame, wo_slice, NT)
    for h in range(8):
        gmsend[h] = partial[:, h * 128 : (h + 1) * 128]
    labuf[p, :, :SLICE] = grad_frame

    def send_gm(k, _):
        m = rem(t + k, 8)
        push(gmsend.at[m], gmbuf.at[t], ssem.at[GM], rsem.at[GM], tp_dev(m))
        return 0

    lax.fori_loop(1, 8, send_gm, 0, unroll=True)
    gmbuf[t] = gmsend[t]

    await_bytes(gmbuf.at[pl.ds(0, 7)], rsem.at[GM])
    gm = gmbuf[0]
    for m in range(1, 8):
        gm = gm + gmbuf[m]
    grad_mixed = gm.astype(bf16)
    labuf[p, :, SLICE:] = grad_mixed

    def send_la(k, _):
        push(
            labuf.at[p], labuf.at[p], ssem.at[LA], rsem.at[LA], plane_dev(rem(p + k, 16))
        )
        return 0

    lax.fori_loop(1, 16, send_la, 0, unroll=True)
    sub_item = lax.broadcasted_iota(jnp.int32, (16, 128), 0)

    def backward(step, _):
        for i in range(16):
            b = step * 16 + i
            part = qkvbuf[b]
            q, k, v = part[:, :128], part[:, 128:256], part[:, 256:]
            prob = probs[b]
            all_rows = dot(grad_mixed, v, NT)
            g_row = jnp.sum(jnp.where(sub_item == b, all_rows, 0.0), axis=0, keepdims=True)
            centred = g_row - jnp.sum(prob * g_row, axis=-1, keepdims=True)
            dscores = (prob * centred * score_scale).astype(bf16)
            grad_q = dot(dscores, k)
            grad_k = dot(dscores, q, TN)
            gp[b] = jnp.concatenate([grad_q, grad_k], axis=1).astype(bf16)
        return 0

    lax.fori_loop(0, 1, backward, 0)

    def scatter(k, _):
        z2 = rem(z + k, 4)
        for yl2 in range(2):
            rows = pl.ds(pl.multiple_of((yl2 * 4 + z2) * 256, 256), 256)
            value = dot(xt[rows, :], gp[...].reshape(16 * CROP, 256)).astype(bf16)
            for half in range(2):
                y2 = half * 2 + yl2
                block = value[half * 128 : (half + 1) * 128]
                zsend[z2, y2, :128] = block[:, :128]
                zsend[z2, y2, 128:] = block[:16, 128:]
                ysend[y2, z2] = block[16:, 128:]

                @pl.when(y2 != y)
                def _():
                    push(ysend.at[y2, z2], yrecv.at[y, z2], ssem.at[RY], rsem.at[RY], at(y2, z))

        @pl.when(z2 != z)
        def _():
            push(zsend.at[z2], zrecv.at[z], ssem.at[RZ], rsem.at[RZ], at(y, z2))

        return 0

    lax.fori_loop(1, 5, scatter, 0)
    zrecv[z] = zsend[z]
    yrecv[y] = ysend[y]

    def add_up(ref, *index):
        total = ref[(0, *index)].astype(f32)
        for q in range(1, 4):
            total = total + ref[(q, *index)].astype(f32)
        return total.astype(bf16)

    await_bytes(yrecv.at[pl.ds(0, 3)], rsem.at[RY])
    for i in range(4):
        ymid[i] = add_up(yrecv, i)
    for j in range(1, 4):
        z2 = rem(z + j, 4)
        push(ymid.at[z2], krecv.at[z], ssem.at[BK], rsem.at[BK], at(y, z2))
    krecv[z] = ymid[z]

    await_bytes(eabuf.at[pl.ds(0, 15)], rsem.at[EA])
    await_bytes(labuf.at[pl.ds(0, 15)], rsem.at[LA])
    early = eabuf[...].reshape(256, 256)
    late = labuf[...].reshape(256, SLICE + 128)
    o_tmp[...] = dot(early[:, 128:], late[:, :SLICE], TN)
    s_fin[2] = dot(early[:, :128], late[:, SLICE:], TN).astype(bf16)
    o_fin[...] = o_tmp[pl.ds(pl.multiple_of(yh * 64, 64), 64), :].astype(bf16)

    s_cols = pl.ds(pl.multiple_of(t * 128, 128), 128)
    o_cols = pl.ds(pl.multiple_of(t * SLICE, SLICE), SLICE)

    def each_target(fn):
        for k in range(1, 8):
            fn(rem(dp + k, 8))

        @pl.when(c != yh)
        def _():
            fn(dp)

    def send_early(j):
        dev = (j, base + yh)
        push(s_fin.at[2], s_out.at[2, :, s_cols], f_send.at[2], f_recv.at[2], dev)
        push(o_fin, o_out.at[:, o_cols], f_send.at[3], f_recv.at[3], dev)

    each_target(send_early)

    await_bytes(zrecv.at[pl.ds(0, 3)], rsem.at[RZ])
    for i in range(4):
        zmid[i] = add_up(zrecv, i)
    for j in range(1, 4):
        y2 = rem(y + j, 4)
        push(zmid.at[y2], qrecv.at[y], ssem.at[BQ], rsem.at[BQ], at(y2, z))
    qrecv[y] = zmid[y]

    def send_part(i, rows, sem):
        def send(j):
            push(
                s_fin.at[i, rows], s_out.at[i, rows, s_cols], f_send.at[sem], f_recv.at[sem],
                (j, base + yh),
            )

        each_target(send)

    all_rows, first_half, last_half = pl.ds(0, 128), pl.ds(0, 16), pl.ds(16, 112)
    await_bytes(krecv.at[pl.ds(0, 3)], rsem.at[BK])
    s_fin[1, 16:] = add_up(krecv)
    send_part(1, last_half, 4)
    await_bytes(qrecv.at[pl.ds(0, 3)], rsem.at[BQ])
    added = add_up(qrecv)
    s_fin[0] = added[:128]
    s_fin[1, :16] = added[128:]
    send_part(0, all_rows, 0)
    send_part(1, first_half, 1)

    @pl.when(c == yh)
    def _():
        s_out[:, :, s_cols] = s_fin[...]
        o_out[:, o_cols] = o_fin[...]

    def await_all(sems):
        def await_parts(members):
            cols = pl.ds(0, members * 128)
            await_bytes(s_out.at[0, :, cols], sems.at[0])
            await_bytes(s_out.at[1, first_half, cols], sems.at[1])
            await_bytes(s_out.at[2, :, cols], sems.at[2])
            await_bytes(o_out.at[:, pl.ds(0, members * SLICE)], sems.at[3])
            await_bytes(s_out.at[1, last_half, cols], sems.at[4])

        @pl.when(c == yh)
        def _():
            await_parts(7)

        @pl.when(c != yh)
        def _():
            await_parts(8)

    await_all(f_recv)
    await_all(f_send)
    await_bytes(xbuf.at[pl.ds(0, 14)], xssem)
    for sem, ref in (
        (W, wbuf), (WO, wobuf), (EA, eabuf), (PO, pobuf), (TO, tobuf), (LA, labuf),
    ):
        await_bytes(ref.at[pl.ds(0, 15)], ssem.at[sem])
    for sem, ref in ((RZ, zrecv), (RY, yrecv), (BQ, qrecv), (BK, krecv)):
        await_bytes(ref.at[pl.ds(0, 3)], ssem.at[sem])
    for sem, ref in ((MC, mcbuf), (MM, mmbuf), (GR, grbuf), (SS, ssbuf), (GM, gmbuf)):
        await_bytes(ref.at[pl.ds(0, 7)], ssem.at[sem])


def norm_kernel(starts, frames, xn, mc, raw, sems):
    begin = [starts[i] for i in range(2)]
    base = [(b // 16) * 16 for b in begin]
    base = [jnp.minimum(b, CROP - 16) for b in base]
    loads = [
        pltpu.make_async_copy(
            frames.at[i, pl.ds(pl.multiple_of(base[i], 16), CROP + 16)], raw.at[i], sems.at[i]
        )
        for i in range(2)
    ]
    for load in loads:
        load.start()
    for i in range(2):
        loads[i].wait()
        odd = begin[i] - base[i]

        def chunk(r, total):
            near = raw[i, pl.ds(pl.multiple_of(r * 16, 16), 32), :].astype(f32)
            rows = pltpu.roll(near, (32 - odd) % 32, 0)[:16]
            centred = rows - jnp.mean(rows, axis=-1, keepdims=True)
            scale = lax.rsqrt(jnp.mean(centred * centred, axis=-1, keepdims=True) + norm_eps)
            xn[i, pl.ds(pl.multiple_of(r * 16, 16), 16), :] = (centred * scale).astype(bf16)
            return total + rows[:8] + rows[8:]

        total = lax.fori_loop(0, CROP // 16, chunk, jnp.zeros((8, D), f32), unroll=8)
        mean = jnp.sum(total, axis=0, keepdims=True) * (1.0 / CROP)
        for m in range(8):
            mc[i, m : m + 1, :] = mean[:, m * SLICE : (m + 1) * SLICE]


def run_norm(frames, starts):
    vmem = pl.BlockSpec(memory_space=pltpu.VMEM)
    return pl.pallas_call(
        norm_kernel,
        out_shape=(
            jax.ShapeDtypeStruct((2, CROP, D), bf16),
            jax.ShapeDtypeStruct((2, 8, SLICE), f32),
        ),
        in_specs=[
            pl.BlockSpec(memory_space=pltpu.SMEM), pl.BlockSpec(memory_space=pltpu.HBM),
        ],
        out_specs=(vmem, vmem),
        scratch_shapes=[
            pltpu.VMEM((2, CROP + 16, D), bf16),
            pltpu.SemaphoreType.DMA((2,)),
        ],
        compiler_params=pltpu.CompilerParams(vmem_limit_bytes=24 * 1024 * 1024),
        name="norm",
    )(starts, frames)


def run_kernel(*args):
    vmem = pl.BlockSpec(memory_space=pltpu.VMEM)
    hbm = pl.BlockSpec(memory_space=pltpu.HBM)
    return pl.pallas_call(
        kernel,
        out_shape=(
            jax.ShapeDtypeStruct((16, 128), f32),
            jax.ShapeDtypeStruct((3, 128, INNER), bf16),
            jax.ShapeDtypeStruct((64, D), bf16),
        ),
        in_specs=[vmem, vmem, vmem, vmem, hbm, hbm, vmem],
        out_specs=(vmem, vmem, vmem),
        scratch_shapes=[
            pltpu.VMEM((3, 128, 256), f32),
            pltpu.VMEM((64, 512), f32),
            pltpu.VMEM((2, 128, QKV), bf16),
            pltpu.VMEM((2, 64, SLICE), bf16),
            pltpu.VMEM((8, 2, SLICE), f32),
            pltpu.VMEM((16, 256), f32),
            pltpu.VMEM((16, CROP, D), bf16),
            pltpu.VMEM((D, 16 * CROP), bf16),
            pltpu.VMEM((16, 128, QKV), bf16),
            pltpu.VMEM((16, 64, SLICE), bf16),
            pltpu.VMEM((8, 2, SLICE), f32),
            pltpu.VMEM((16, CROP, QKV), bf16),
            pltpu.VMEM((16, CROP, CROP), f32),
            pltpu.VMEM((16, D), f32),
            pltpu.VMEM((8, 16, 128), f32),
            pltpu.VMEM((16, 16, 256), bf16),
            pltpu.VMEM((16, 16, 256), bf16),
            pltpu.VMEM((16, 16, SLICE), f32),
            pltpu.VMEM((8, 16, 256), f32),
            pltpu.VMEM((8, 1, 256), f32),
            pltpu.VMEM((16, 1, 256), f32),
            pltpu.VMEM((16, 16, SLICE + 128), bf16),
            pltpu.VMEM((8, 16, 128), f32),
            pltpu.VMEM((8, 16, 128), f32),
            pltpu.VMEM((16, CROP, 256), bf16),
            pltpu.VMEM((4, 4, 144, 128), bf16),
            pltpu.VMEM((4, 4, 112, 128), bf16),
            pltpu.VMEM((4, 4, 144, 128), bf16),
            pltpu.VMEM((4, 4, 112, 128), bf16),
            pltpu.VMEM((4, 144, 128), bf16),
            pltpu.VMEM((4, 112, 128), bf16),
            pltpu.VMEM((4, 144, 128), bf16),
            pltpu.VMEM((4, 112, 128), bf16),
            pltpu.VMEM((3, 128, 128), bf16),
            pltpu.VMEM((128, SLICE), f32),
            pltpu.VMEM((64, SLICE), bf16),
            pltpu.VMEM((CROP, CROP), f32),
            pltpu.VMEM((HEADS, 2 * CROP), f32),
            pltpu.SemaphoreType.DMA((4,)),
            pltpu.SemaphoreType.DMA((15,)),
            pltpu.SemaphoreType.DMA((15,)),
            pltpu.SemaphoreType.DMA,
            pltpu.SemaphoreType.DMA((16,)),
        ]
        + [pltpu.SemaphoreType.DMA((5,))] * 2,
        compiler_params=pltpu.CompilerParams(
            collective_id=0, has_side_effects=True, vmem_limit_bytes=40 * 1024 * 1024
        ),
        cost_estimate=pl.CostEstimate(
            flops=15_000_000_000, bytes_accessed=300_000_000, transcendentals=300_000
        ),
        name="encoder",
    )(*args)


STEPS = 8


def adam_kernel(
    share, o_grad, losses, gain, gain_m, gain_s, in_w, in_m, in_s, out_w, out_m, out_s,
    pair_losses, new_in_w, new_in_m, new_in_s, new_out_w, new_out_m, new_out_s, new_gw, new_gm, new_gs,
    column, in_new, out_new, isems, osems,
):
    t = 2 * (lax.axis_index("dp") // 2) + lax.axis_index("shard") % 2
    item = lax.broadcasted_iota(jnp.int32, (16, 128), 0)
    lane = lax.broadcasted_iota(jnp.int32, (16, 128), 1)
    for i in range(2):
        mine = jnp.logical_and(item == 2 * t + i, lane == 0)
        pair_losses[i] = jnp.sum(jnp.where(mine, losses[...], 0.0))
    square = lax.broadcasted_iota(jnp.int32, (128, 128), 0) == lax.broadcasted_iota(
        jnp.int32, (128, 128), 1
    )
    gain_row = gain[...].astype(bf16).astype(f32)
    column[...] = jnp.broadcast_to(
        jnp.sum(jnp.where(square, gain_row, 0.0), axis=1, keepdims=True), (128, 128)
    )
    rows = 128 // STEPS
    stores = []
    for step in range(STEPS):
        at_rows = pl.ds(step * rows, rows)
        gain_col = column[at_rows, :][:, :1]

        def part(j, total):
            i, cols = j, pl.ds(pl.multiple_of(j * 1024, 1024), 1024)
            inner = pl.ds(0, 1024)
            master = in_w[at_rows, cols]
            piece = share[i, at_rows, inner].astype(f32)
            new = adam_update(
                master, in_m[at_rows, cols], in_s[at_rows, cols], piece * gain_col, weight_decay
            )
            for n in range(3):
                in_new[n, at_rows, cols] = new[n]
            terms = piece * master.astype(bf16).astype(f32)
            return total + sum(terms[:, n * 128 : (n + 1) * 128] for n in range(8))

        total = lax.fori_loop(0, 3, part, jnp.zeros((rows, 128), f32), unroll=3)
        column[at_rows, :] = jnp.broadcast_to(jnp.sum(total, axis=1, keepdims=True), (rows, 128))
        for n, ref in enumerate((new_in_w, new_in_m, new_in_s)):
            stores.append(
                pltpu.make_async_copy(in_new.at[n, at_rows], ref.at[at_rows], isems.at[n, step])
            )
            stores[-1].start()
    for step in range(2):
        at_rows = pl.ds(step * 32, 32)

        def out_part(j, _):
            cols = pl.ds(pl.multiple_of(j * 512, 512), 512)
            new = adam_update(
                out_w[at_rows, cols], out_m[at_rows, cols], out_s[at_rows, cols],
                o_grad[at_rows, cols].astype(f32), weight_decay,
            )
            for n in range(3):
                out_new[n, at_rows, cols] = new[n]
            return 0

        lax.fori_loop(0, 4, out_part, 0, unroll=4)
        for n, ref in enumerate((new_out_w, new_out_m, new_out_s)):
            stores.append(
                pltpu.make_async_copy(out_new.at[n, at_rows], ref.at[at_rows], osems.at[n, step])
            )
            stores[-1].start()
    grad = jnp.sum(jnp.where(square, column[...], 0.0), axis=0, keepdims=True)
    new_gw[...], new_gm[...], new_gs[...] = adam_update(
        gain[...], gain_m[...], gain_s[...], grad, 0.0
    )
    for store in stores:
        store.wait()


def run_adam(share, o_grad, losses, gains, inputs, outputs):
    vmem = pl.BlockSpec(memory_space=pltpu.VMEM)
    hbm = pl.BlockSpec(memory_space=pltpu.HBM)
    return pl.pallas_call(
        adam_kernel,
        out_shape=[jax.ShapeDtypeStruct((2,), f32)]
        + [jax.ShapeDtypeStruct((128, 3 * INNER), f32)] * 3
        + [jax.ShapeDtypeStruct((64, D), f32)] * 3
        + [jax.ShapeDtypeStruct((1, 128), f32)] * 3,
        in_specs=[vmem] * 12,
        out_specs=[pl.BlockSpec(memory_space=pltpu.SMEM)] + [hbm] * 6 + [vmem] * 3,
        scratch_shapes=[
            pltpu.VMEM((128, 128), f32),
            pltpu.VMEM((3, 128, 3 * INNER), f32),
            pltpu.VMEM((3, 64, D), f32),
            pltpu.SemaphoreType.DMA((3, STEPS)),
            pltpu.SemaphoreType.DMA((3, 2)),
        ],
        compiler_params=pltpu.CompilerParams(vmem_limit_bytes=24 * 1024 * 1024),
        name="adam",
    )(share, o_grad, losses, *gains, *inputs, *outputs)


def per_device(
    frames, crop_starts, pairing, bias_table,
    input_master, input_moment, input_square,
    output_master, output_moment, output_square,
    gain_master, gain_moment, gain_square,
):
    gains = [g.reshape(1, 128) for g in (gain_master, gain_moment, gain_square)]
    losses, s_grad, o_grad = run_kernel(
        *run_norm(frames, crop_starts), pairing.reshape(1, 256), bias_table,
        input_master, output_master, gains[0],
    )
    new = run_adam(
        s_grad, o_grad, losses, gains,
        (input_master, input_moment, input_square),
        (output_master, output_moment, output_square),
    )
    return (*new[:7], *(g.reshape(128) for g in new[7:]))


def solution(mesh):
    one = P("shard")
    two = P("shard", None)
    items = P(("dp", "shard"))
    in_specs = (P(("dp", "shard"), None, None), items, P(), P()) + (two,) * 6 + (one,) * 3
    out_specs = (items,) + (two,) * 6 + (one,) * 3
    return jax.shard_map(
        per_device, mesh=mesh, in_specs=in_specs, out_specs=out_specs, check_vma=False
    )
```
